32 devices in a mesh: group: 1, req: 4 (over z), head: 4 (over y, x), pool: 2 (over core).
Axes of the slice: x: 2, y: 2, z: 4, core: 2. Of those that a mesh axis runs over, the one named last changes fastest.
Arguments:
- queries: bfloat16 [192, 4096], P(('group', 'req'), 'head'), may hold values from -128 to 128
- new_entries: bfloat16 [192, 2, 4, 256], P(('group', 'req'), None, 'head'), may hold values from -6 to 6
- cache_pages: bfloat16 [4, 416, 16, 256], P('head', ('group', 'req', 'pool')), may hold values from -6 to 6
- page_table: int32 [192, 2, 1], P(('group', 'req'), 'pool'), may hold values from 0 to 51, as said below
- cached_length: int32 [192, 2], P(('group', 'req'), 'pool'), may hold values from 1 to 16, as said below
- leave_slots: int32 [32], P(('group', 'req', 'pool')), may hold values from 0 to 50, as said below
- arrive_slots: int32 [32], P(('group', 'req', 'pool')), may hold values from 0 to 51, as said below
- residual: bfloat16 [192, 2048], P(('group', 'req', 'head')), may hold values from -5 to 5
- norm_gain: float32 [2048], replicated, may hold values from 0.5 to 1.5
- output_weight: bfloat16 [4096, 2048], P(('head', 'pool')), may hold values from -0.25 to 0.25
- expert_choice: int32 [192, 8], P(('group', 'req', 'head')), may hold values from 0 to 15, all different within a row; in each aligned block of 12 rows (0 to 11, 12 to 23, ...) at most 12 rows name the same one
- route_weight: float32 [192, 8], P(('group', 'req', 'head')), may hold values from 0.2 to 1
- gate_up: bfloat16 [16, 2, 384, 2048], P(('req', 'head'), None, 'pool'), may hold values from -0.125 to 0.125
- down_weight: bfloat16 [16, 384, 2048], P(('req', 'head'), 'pool'), may hold values from -0.3125 to 0.3125
Outputs:
- decoded: bfloat16 [192, 2048], P(('group', 'req', 'head'), 'pool')
The draws below stay inside these ranges and needn't reach their ends.
Inputs may be any that keep to these rules, and one draw needn't show every extreme that they name: `page_table`: within each block of one index of req and one pool, the 48 entries name distinct slots, none of them among that block's leave_slots. `leave_slots`: each block's 4 entries are distinct. `arrive_slots`: each block's 4 entries are distinct slots that its page table names. `cached_length`: in every block of 48 requests and each pool some request has 16. `expert_choice`: each row names 8 distinct experts; in each aligned block of 12 rows no expert is named more than 12 times, a bound that some block reaches.
All inputs are finite; a program needn't handle non-finite values.
Results may differ from the reference program's by a relative error of at most 0.023.
Values may be sent and summed in bfloat16 or wider, within the bound.
No kernel may reach another device: no remote copies, remote signals or barrier semaphores. Data moves between devices by JAX's collectives and lax.ppermute only.
A program may use at most 64 MiB of HBM per device.

```python
import math
import jax
import jax.numpy as jnp
import numpy as np
from jax import lax

D = 2048
HEADS = 32
KVH = 4
HEAD_SIZE = 128
TOPK = 8
FF_E = 384
B_DEV = 48
PAGE = 16
PPR = 1
MOVE = 4
SLOT_DEV = 52
SLOTS = 416
REQS = 192
RD = 12
EXPERTS = 16
CAP = 12
N_REQ = 4
N_POOL = 2


def paging(key):
    used_count = B_DEV * PPR
    base_key = jax.random.fold_in(key, 7001)

    def single(device_key):
        first_key, second_key, third_key = jax.random.split(device_key, 3)
        base_order = jax.random.permutation(first_key, SLOT_DEV - 2).astype(jnp.int32)
        leaving = jnp.concatenate([jnp.full((1,), SLOT_DEV - 2, jnp.int32), base_order[:MOVE - 1]])
        others = base_order[MOVE - 1:]
        table_rows = jnp.concatenate([jnp.full((1,), SLOT_DEV - 1, jnp.int32), others])
        table_rows = table_rows[jax.random.permutation(second_key, used_count)]
        picked = others[jax.random.permutation(third_key, used_count - 1)[:MOVE - 1]]
        arriving = jnp.concatenate([jnp.full((1,), SLOT_DEV - 1, jnp.int32), picked])
        return (table_rows.reshape(B_DEV, PPR), leaving, arriving)
    tables, leaving, arriving = jax.vmap(single)(jax.random.split(base_key, N_REQ * N_POOL))
    tables = tables.reshape(N_REQ, N_POOL, B_DEV, PPR).transpose(0, 2, 1, 3).reshape(N_REQ * B_DEV, N_POOL, PPR)
    return (tables.astype(jnp.int32), leaving.reshape(-1).astype(jnp.int32), arriving.reshape(-1).astype(jnp.int32))


def draw_page_table(key, part):
    return paging(key)[0]


def draw_leave_slots(key, part):
    return paging(key)[1]


def draw_arrive_slots(key, part):
    return paging(key)[2]


def draw_cached_length(key, part):
    first_key, second_key = jax.random.split(jax.random.fold_in(key, 7002))
    longest = PPR * PAGE
    lengths = jax.random.randint(first_key, (N_REQ, B_DEV, N_POOL), 1, longest + 1)
    chosen = jax.random.randint(second_key, (N_REQ, 1, N_POOL), 0, B_DEV)
    at_most = jnp.arange(B_DEV)[None, :, None] == chosen
    return jnp.where(at_most, longest, lengths).reshape(N_REQ * B_DEV, N_POOL).astype(jnp.int32)


def attention_draw(key):
    split_keys = jax.random.split(jax.random.fold_in(key, 7003), 2)
    total_rows = N_REQ * B_DEV
    group_size = HEADS // KVH
    queries = jnp.clip(jax.random.normal(split_keys[0], (total_rows, KVH, group_size, HEAD_SIZE), jnp.float32), -6.0, 6.0)
    entries = jnp.clip(jax.random.normal(split_keys[1], (total_rows, 2, KVH, 2 * HEAD_SIZE), jnp.float32), -6.0, 6.0)
    return (queries.reshape(total_rows, HEADS * HEAD_SIZE), entries)


def draw_queries(key, part):
    return attention_draw(key)[0].astype(jnp.bfloat16)


def draw_new_entries(key, part):
    return attention_draw(key)[1].astype(jnp.bfloat16)


def draw_residual(key, part):
    first_key = jax.random.fold_in(jax.random.fold_in(key, 7004), 0)
    total_rows = N_REQ * B_DEV
    values = jnp.clip(jax.random.normal(first_key, (total_rows, D), jnp.float32), -6.0, 6.0) * 0.5
    return values.astype(jnp.bfloat16)


def block_scale(key, shape, cuts, smallest, largest):
    level, own = 1.0, jax.random.fold_in(key, 6)
    for axis_at, blocks in cuts:
        steps = jnp.exp(jax.random.uniform(jax.random.fold_in(own, axis_at), (blocks,), jnp.float32, smallest / len(cuts), largest / len(cuts)))
        level = level * jnp.repeat(steps, shape[axis_at] // blocks).reshape([-1 if axis == axis_at else 1 for axis in range(len(shape))])
    return level


def routed_block(stream_key, own, number, rows, count, top, limit, lean):
    sequence = jax.random.permutation(stream_key, count)
    crowded, usual = load_shares(count, rows * top, limit, lean, True), load_shares(count, rows * top, limit, lean, False)
    places = jnp.arange(count)

    def named(sizes, rotation):
        used = int((sizes > 0).sum())
        fixed = max(1, used // 4)
        moved = fixed + (places - fixed + rotation * (used - fixed)) % max(1, count - fixed)
        return jnp.zeros((count,), jnp.int32).at[sequence[jnp.where(places < fixed, places, moved)]].set(jnp.asarray(sizes, jnp.int32))

    sizes = jnp.where(number % 4 == 0, named(crowded, number // 4), named(usual, number - number // 4 - 1))
    mixed = jax.random.permutation(jax.random.fold_in(own, 3), count)
    source_of, sink = mixed[0:count // 2 * 2:2], mixed[1:count // 2 * 2:2]
    room = jnp.minimum(sizes[source_of] - 1, limit - sizes[sink]) // 2
    room = jnp.where((source_of == sequence[0]) | (sink == sequence[0]) | (sizes[sink] == 0), 0, jnp.maximum(room, 0))
    moved = jax.random.randint(jax.random.fold_in(own, 4), (count // 2,), 0, 1 << 20) % (room + 1)
    sizes = sizes.at[source_of].add(-moved).at[sink].add(moved)
    members = jnp.searchsorted(jnp.cumsum(sizes), jnp.arange(rows * top), side="right").astype(jnp.int32)
    grid = members.reshape(top, rows).T
    grid = grid[jax.random.permutation(jax.random.fold_in(own, 1), rows)]
    rotation = jax.random.randint(jax.random.fold_in(own, 2), (rows, 1), 0, top)
    return jnp.take_along_axis(grid, (jnp.arange(top)[None, :] + rotation) % top, axis=1)


def load_shares(number_of, total, reach, slope, full):
    loads = [(1 << 20) // math.isqrt(rank ** slope) + 1 for rank in range(1, number_of + 1)]
    largest = reach if full else min(reach, max(-(-total // number_of), total * loads[0] // sum(loads)))
    least = 1 if total - largest >= number_of - 1 else 0
    given, rest = [largest] + [least] * (number_of - 1), total - largest - least * (number_of - 1)
    while rest > 0:
        movable = [i for i in range(1, number_of) if given[i] < largest] or [i for i in range(1, number_of) if given[i] < reach]
        mass, left = sum([loads[i] for i in movable]), rest
        for i in movable:
            extra = min(reach - given[i], max(1, left * loads[i] // mass), rest)
            given[i] = given[i] + extra
            rest = rest - extra
    return np.array(given)


def normal_values(own_key, shape, scale, bound, cuts=(), held_as=jnp.bfloat16):
    loudness = block_scale(own_key, shape, cuts, -0.22, 0.18) if cuts else 1.0
    values = jax.random.normal(own_key, shape, jnp.float32) * scale * loudness
    return jnp.minimum(jnp.maximum(values, -bound), bound).astype(held_as)


def setup_inputs(seed: int = 0, part: int = 0) -> dict:
    arg_keys = jax.random.split(jax.random.key(seed), 15)
    part_splits = jax.random.split(jax.random.fold_in(arg_keys[14], part), 15)
    queries = draw_queries(jax.random.fold_in(jax.random.fold_in(arg_keys[14], part), 71), part)
    new_entries = draw_new_entries(jax.random.fold_in(jax.random.fold_in(arg_keys[14], part), 71), part)
    cache_pages = normal_values(part_splits[2], (KVH, SLOTS, PAGE, 2 * HEAD_SIZE), 1.0, 6.0, ((0, 4), (1, 8)))
    page_table = draw_page_table(jax.random.fold_in(jax.random.fold_in(arg_keys[14], part), 71), part)
    cached_length = draw_cached_length(jax.random.fold_in(jax.random.fold_in(arg_keys[14], part), 71), part)
    leave_slots = draw_leave_slots(jax.random.fold_in(jax.random.fold_in(arg_keys[14], part), 71), part)
    arrive_slots = draw_arrive_slots(jax.random.fold_in(jax.random.fold_in(arg_keys[14], part), 71), part)
    residual = draw_residual(jax.random.fold_in(jax.random.fold_in(arg_keys[14], part), 71), part)
    norm_gain = jnp.clip(1.0 + 0.1 * jax.random.normal(arg_keys[8], (D,), jnp.float32), 0.5, 1.5)
    output_weight = normal_values(arg_keys[9], (HEADS * HEAD_SIZE, D), (HEADS * HEAD_SIZE // 8) ** -0.5, 0.25, ((0, 8),))
    expert_choice_keys = jax.random.split(jax.random.fold_in(part_splits[10], 1), REQS // RD)
    expert_choice_turns = jax.random.permutation(jax.random.fold_in(part_splits[10], 3), REQS // RD)
    expert_choice = jax.vmap(lambda own, number: routed_block(jax.random.fold_in(part_splits[10], 2), own, number, RD, EXPERTS, TOPK, CAP, 2))(expert_choice_keys, expert_choice_turns).reshape((REQS, TOPK))
    route_weight = jnp.clip(0.2 + 0.8 * jax.random.uniform(part_splits[11], (REQS, TOPK), jnp.float32) ** block_scale(part_splits[11], (REQS, TOPK), ((0, 16),), -0.2, 0.2), 0.2, 1.0)
    gate_up = normal_values(arg_keys[12], (EXPERTS, 2, FF_E, D), D ** -0.5, 0.125, ((0, 16), (2, 2)))
    down_weight = normal_values(arg_keys[13], (EXPERTS, FF_E, D), FF_E ** -0.5, 0.3125, ((0, 16), (1, 2)))
    return dict(queries=queries, new_entries=new_entries, cache_pages=cache_pages, page_table=page_table, cached_length=cached_length, leave_slots=leave_slots, arrive_slots=arrive_slots, residual=residual, norm_gain=norm_gain, output_weight=output_weight, expert_choice=expert_choice, route_weight=route_weight, gate_up=gate_up, down_weight=down_weight)


def reference(queries, new_entries, cache_pages, page_table, cached_length, leave_slots, arrive_slots, residual, norm_gain, output_weight, expert_choice, route_weight, gate_up, down_weight):
    slot_count = B_DEV * PPR + MOVE
    total_rows = N_REQ * B_DEV
    group_size = HEADS // KVH
    page_store = cache_pages.reshape(KVH, N_REQ, N_POOL, slot_count, PAGE, 2 * HEAD_SIZE)
    leaving = leave_slots.reshape(N_REQ, N_POOL, MOVE)
    arriving = arrive_slots.reshape(N_REQ, N_POOL, MOVE)
    req_index = jnp.arange(N_REQ, dtype=jnp.int32)[:, None, None]
    pool_index = jnp.arange(N_POOL, dtype=jnp.int32)[None, :, None]
    moved_pages = page_store[:, req_index, 1 - pool_index, leaving[:, ::-1, :]]
    page_store = page_store.at[:, req_index, pool_index, arriving].set(moved_pages)
    owner_index = (jnp.arange(total_rows, dtype=jnp.int32) // B_DEV)[:, None, None]
    positions = jnp.arange(PPR * PAGE, dtype=jnp.int32)
    valid_mask = (positions[None, None, :] < cached_length[:, :, None]).reshape(total_rows, N_POOL * PPR * PAGE)
    valid_mask = jnp.concatenate([valid_mask, jnp.ones((total_rows, 2), dtype=bool)], axis=1)
    grouped_queries = queries.astype(jnp.float32).reshape(total_rows, KVH, group_size, HEAD_SIZE)
    newest = new_entries.astype(jnp.float32)

    def one_group(query_group_index):
        context = page_store[query_group_index][owner_index, pool_index, page_table]
        context = context.reshape(total_rows, N_POOL * PPR * PAGE, 2 * HEAD_SIZE).astype(jnp.float32)
        entries = jnp.concatenate([context, newest[:, :, query_group_index, :]], axis=1)
        paged_key_rows = entries[:, :, :HEAD_SIZE]
        paged_value_rows = entries[:, :, HEAD_SIZE:]
        attention_scores = jnp.einsum('xsw,xlw->xsl', grouped_queries[:, query_group_index], paged_key_rows) * HEAD_SIZE ** (-0.5)
        attention_scores = jnp.where(valid_mask[:, None, :], attention_scores, -jnp.inf)
        attention_weights = jax.nn.softmax(attention_scores, axis=-1)
        return jnp.einsum('usj,ujw->usw', attention_weights, paged_value_rows)
    attended = lax.map(one_group, jnp.arange(KVH, dtype=jnp.int32))
    attended = attended.transpose(1, 0, 2, 3).reshape(total_rows, HEADS * HEAD_SIZE).astype(jnp.bfloat16)
    attention = jnp.dot(attended, output_weight, preferred_element_type=jnp.float32)
    hidden = residual.astype(jnp.float32) + attention
    normed = (hidden * lax.rsqrt(lax.optimization_barrier(jnp.mean(hidden * hidden, axis=-1, keepdims=True)) + 1e-06) * norm_gain.astype(jnp.float32)).astype(jnp.bfloat16)
    capacity = EXPERTS * CAP
    row_ids = jnp.arange(total_rows, dtype=jnp.int32)

    def one_expert(accumulated, expert):
        expert_hits = expert_choice == expert
        weight = lax.optimization_barrier(jnp.sum(jnp.where(expert_hits, route_weight.astype(jnp.float32), 0.0), axis=1))
        chosen = jnp.any(expert_hits, axis=1)
        ranking = jnp.where(chosen, total_rows - row_ids, 0).astype(jnp.int32)
        top_values, picked = lax.top_k(ranking, capacity)
        picked = picked.astype(jnp.int32)
        inputs = normed[picked]
        projected = jnp.dot(inputs, gate_up[expert].reshape(2 * FF_E, D).T, preferred_element_type=jnp.float32)
        activated = (jax.nn.silu(projected[:, :FF_E]) * projected[:, FF_E:]).astype(jnp.bfloat16)
        output = jnp.dot(activated, down_weight[expert], preferred_element_type=jnp.float32).astype(jnp.bfloat16)
        contribution = weight[picked][:, None] * output.astype(jnp.float32)
        return (accumulated.at[picked].add(contribution), None)
    mixture, unused = lax.scan(one_expert, jnp.zeros((total_rows, D), jnp.float32), jnp.arange(EXPERTS, dtype=jnp.int32))
    return (hidden + mixture).astype(jnp.bfloat16)
```

```python
import functools

import jax
import jax.numpy as jnp
import numpy as np
from jax import lax
from jax.experimental import pallas as pl
from jax.experimental.pallas import tpu as pltpu
from jax.sharding import PartitionSpec as P

F32 = jnp.float32
BF16 = jnp.bfloat16
VMEM_LIMIT = 56 * 2**20
LANES = 128


def send(value, axes, step):
    size = lax.axis_size(axes)
    return lax.ppermute(value, axes, [(i, i ^ step) for i in range(size)])


def dot(a, b, contract=((1,), (0,))):
    return lax.dot_general(a, b, (contract, ((), ())), preferred_element_type=F32)


def kernel_call(body, out_shape, args, scratch=()):
    return pl.pallas_call(
        body,
        out_shape=out_shape,
        in_specs=[pl.BlockSpec(memory_space=pltpu.VMEM)] * len(args),
        out_specs=jax.tree.map(lambda _: pl.BlockSpec(memory_space=pltpu.VMEM), out_shape),
        scratch_shapes=list(scratch),
        compiler_params=pltpu.CompilerParams(vmem_limit_bytes=VMEM_LIMIT),
    )(*args)


def column(row, start, count):
    lane = lax.broadcasted_iota(jnp.int32, (count, row.shape[1]), 1)
    line = lax.broadcasted_iota(jnp.int32, (count, row.shape[1]), 0)
    return jnp.sum(jnp.where(lane == line + start, row, 0.0), axis=1, keepdims=True)


def attend_kernel(sizes, q_ref, new_ref, own_ref, other_ref, own_ints_ref, other_ints_ref, residual_ref, weight_ref, *rest):
    requests, pages, moved, page, heads, pools, head_dim = sizes
    outs, partial_ref = rest[:-1], rest[-1]
    slots = own_ref.shape[0] // page
    here = lax.axis_index("pool")
    me = lax.axis_index("head") * pools + here
    group = q_ref.shape[1] // head_dim // pools
    rows = requests // pools
    columns = weight_ref.shape[1] // heads

    ints = [own_ints_ref[...].astype(F32), other_ints_ref[...].astype(F32)]
    live_from, live_count = [], []
    for q in range(2):
        row, across = ints[q], ints[1 - q]
        base = pages * requests
        length = column(row, base, requests)
        for j in range(pages):
            slot = column(row, j * requests, requests)
            source = slot + float(q * slots)
            for k in range(moved):
                leave = column(across, base + requests + k, 1)
                arrive = column(row, base + requests + moved + k, 1)
                source = jnp.where(slot == arrive, leave + float((1 - q) * slots), source)
            live_from.append((source * float(page)).astype(jnp.int32))
            live_count.append(jnp.clip(length - float(j * page), 0.0, float(page)).astype(jnp.int32))

    def cache_mask(offset, count):
        entry = lax.broadcasted_iota(jnp.int32, (requests, count), 1) + offset
        mask = None
        for start, amount in zip(live_from, live_count):
            apart = entry - start
            one = (apart >= 0) & (apart < amount)
            mask = one if mask is None else mask | one
        return mask

    count = own_ref.shape[0]
    fresh = new_ref.shape[0] // requests
    entry = lax.broadcasted_iota(jnp.int32, (requests, new_ref.shape[0]), 1)
    first = lax.broadcasted_iota(jnp.int32, (requests, new_ref.shape[0]), 0) * fresh
    masks = [cache_mask(0, count), cache_mask(count, count), (entry >= first) & (entry < first + fresh)]
    queries = jnp.concatenate(
        [
            q_ref[:, pl.ds(pl.multiple_of((here * group + g) * head_dim, LANES), head_dim)]
            for g in range(group)
        ],
        axis=0,
    )
    scale = head_dim ** (-0.5)
    scores = []
    for ref, mask in zip((own_ref, other_ref, new_ref), masks):
        score = dot(queries, ref[:, :head_dim], ((1,), (1,))) * scale
        bias = jnp.where(mask, 0.0, -jnp.inf)
        scores.append(score + jnp.concatenate([bias] * group, axis=0))
    largest = functools.reduce(
        jnp.maximum, [jnp.max(score, axis=1, keepdims=True) for score in scores]
    )
    total, value = 0.0, 0.0
    for ref, score in zip((own_ref, other_ref, new_ref), scores):
        weights = jnp.exp(score - largest)
        total = total + jnp.sum(weights, axis=1, keepdims=True)
        value = value + dot(weights.astype(BF16), ref[:, head_dim:])
    value = (value / total).astype(BF16)
    attended = jnp.concatenate(
        [value[g * requests : (g + 1) * requests] for g in range(group)], axis=1
    )
    partial_ref[...] = dot(attended, weight_ref[...]) + residual_ref[...].astype(F32)
    for step, out in enumerate(outs):
        to = me ^ step
        to_head, to_pool = to // pools, to % pools
        out[...] = partial_ref[
            pl.ds(pl.multiple_of(to_pool * rows, 8), rows),
            pl.ds(pl.multiple_of(to_head * columns, LANES), columns),
        ].astype(BF16)


def expert_kernel(sizes, *refs):
    heads, pools, rows_here = sizes
    blocks, refs = refs[:heads], refs[heads:]
    gates, ups, downs, refs = refs[:pools], refs[pools : 2 * pools], refs[2 * pools : 3 * pools], refs[3 * pools :]
    gain_ref, order_ref, route_ref = refs[:3]
    outs, sum_ref = refs[3:-1], refs[-1]
    head, pool = lax.axis_index("head"), lax.axis_index("pool")
    planes, plane_rows, columns = blocks[0].shape
    width = heads * columns
    squares = 0.0
    gate = [0.0] * pools
    up = [0.0] * pools
    for step in range(heads):
        start = pl.multiple_of((head ^ step) * columns, LANES)
        block = blocks[step][...].astype(F32).reshape(planes * plane_rows, columns)
        squares = squares + jnp.sum(block * block, axis=1, keepdims=True)
        block = (block * gain_ref[:, pl.ds(start, columns)]).astype(BF16)
        for half in range(pools):
            gate[half] = gate[half] + dot(block, gates[half][:, pl.ds(start, columns)], ((1,), (1,)))
            up[half] = up[half] + dot(block, ups[half][:, pl.ds(start, columns)], ((1,), (1,)))
    scale = lax.rsqrt(squares / width + 1e-06)
    result = 0.0
    for half in range(pools):
        g, u = gate[half] * scale, up[half] * scale
        activated = (g / (1.0 + jnp.exp(-g)) * u).astype(BF16)
        activated = (dot(order_ref[...], activated) * route_ref[...]).astype(BF16)
        result = result + dot(activated, downs[half][...])
    sum_ref[...] = result
    hidden = blocks[0][0].astype(F32)
    own = pl.ds(pl.multiple_of(head * columns, LANES), columns)
    parts = plane_rows // rows_here
    for a in range(parts):
        at = slice(a * planes * rows_here, a * planes * rows_here + rows_here)
        sum_ref[at, own] = sum_ref[at, own] + hidden[a * rows_here : (a + 1) * rows_here]
    rows, half = planes * rows_here, width // pools
    for step, out in enumerate(outs):
        to = head ^ step
        a, b = to // pools, to % pools
        out[...] = sum_ref[
            pl.ds(pl.multiple_of(a * rows, 8), rows), pl.ds(pl.multiple_of(b * half, LANES), half)
        ].astype(BF16)


def local(
    queries,
    new_entries,
    cache_pages,
    page_table,
    cached_length,
    leave_slots,
    arrive_slots,
    residual,
    norm_gain,
    output_weight,
    expert_choice,
    route_weight,
    gate_up,
    down_weight,
):
    pools, heads, planes = lax.axis_size("pool"), lax.axis_size("head"), lax.axis_size("req")
    experts = heads * planes
    requests = queries.shape[0]
    slots, page, entry = cache_pages.shape[1:]
    head_dim = entry // 2
    moved = leave_slots.shape[0]
    pages = page_table.shape[2]
    rows_here, width = residual.shape
    head, pool, plane = lax.axis_index("head"), lax.axis_index("pool"), lax.axis_index("req")
    both = ("head", "pool")

    own_cache = cache_pages.reshape(slots * page, entry)
    other_cache = send(own_cache, "pool", 1)
    ints = jnp.concatenate(
        [page_table[:, 0, j] for j in range(pages)]
        + [cached_length.reshape(-1), leave_slots, arrive_slots]
    )
    ints = jnp.pad(ints, (0, -ints.shape[0] % LANES)).reshape(1, -1)
    other_ints = send(ints, "pool", 1)

    choice = expert_choice[:, :, None] == jnp.arange(experts, dtype=jnp.int32)[None, None, :]
    mix = jnp.sum(jnp.where(choice, route_weight[:, :, None], 0.0), axis=1)
    mix = jnp.stack([mix] + [send(mix, "req", step) for step in range(1, planes)])
    mix = jnp.stack([mix] + [send(mix, "head", step) for step in range(1, heads)])
    mix = lax.dynamic_index_in_dim(mix, plane * heads + head, 3, False)
    parts = heads // pools
    route = jnp.stack(
        [
            lax.dynamic_index_in_dim(mix, (pool * parts + a) ^ head, 0, False)
            for a in range(parts)
        ]
    ).reshape(-1, 1)

    added = lax.dynamic_update_slice_in_dim(
        jnp.zeros((requests, width), BF16),
        jnp.where(pool == 0, residual, jnp.zeros_like(residual)),
        head * rows_here,
        0,
    )
    sizes = (requests, pages, moved, page, heads, pools, head_dim)
    args = (
        queries,
        new_entries.reshape(-1, entry),
        own_cache,
        other_cache,
        ints,
        other_ints,
        added,
        output_weight,
    )
    piece = jax.ShapeDtypeStruct((requests // pools, width // heads), BF16)
    pieces = kernel_call(
        functools.partial(attend_kernel, sizes),
        [piece] * (heads * pools),
        args,
        [pltpu.VMEM((requests, width), F32)],
    )
    arrived = [pieces[0]] + [send(pieces[step], both, step) for step in range(1, heads * pools)]
    hidden = sum(value.astype(F32) for value in arrived).astype(BF16)

    held = lax.optimization_barrier((gate_up, down_weight, other_cache))
    other_gate_up, other_down = send(held[0], "pool", 1), send(held[1], "pool", 1)

    block = jnp.stack([hidden] + [send(hidden, "req", step) for step in range(1, planes)])
    blocks = [block] + [send(block, "head", step) for step in range(1, heads)]

    order = np.zeros((planes * parts * rows_here,) * 2, np.float32)
    for a in range(parts):
        for r in range(planes):
            for i in range(rows_here):
                order[(a * planes + r) * rows_here + i, (r * parts + a) * rows_here + i] = 1.0
    piece = jax.ShapeDtypeStruct((planes * rows_here, width // pools), BF16)
    args = (
        *blocks,
        gate_up[0, 0],
        other_gate_up[0, 0],
        gate_up[0, 1],
        other_gate_up[0, 1],
        down_weight[0],
        other_down[0],
        norm_gain.reshape(1, -1),
        jnp.asarray(order, BF16),
        route,
    )
    pieces = kernel_call(
        functools.partial(expert_kernel, (heads, pools, rows_here)),
        [piece] * heads,
        args,
        [pltpu.VMEM((planes * parts * rows_here, width), F32)],
    )
    returned = []
    for step in range(heads):
        pairs = []
        for h in range(heads):
            for p in range(pools):
                to = h ^ step
                pairs.append((h * pools + p, (p * parts + to // pools) * pools + to % pools))
        returned.append(lax.ppermute(pieces[step], both, pairs))
    mixed = sum(value.astype(F32) for value in returned).astype(BF16)
    mixed = mixed.reshape(planes, rows_here, -1)
    total = mixed[0].astype(F32)
    for step in range(1, planes):
        total = total + send(mixed[step], "req", step).astype(F32)
    return total.astype(BF16)


def solution(mesh):
    return jax.shard_map(
        local,
        mesh=mesh,
        in_specs=(
            P(("group", "req"), "head"),
            P(("group", "req"), None, "head", None),
            P("head", ("group", "req", "pool"), None, None),
            P(("group", "req"), "pool", None),
            P(("group", "req"), "pool"),
            P(("group", "req", "pool")),
            P(("group", "req", "pool")),
            P(("group", "req", "head"), None),
            P(),
            P(("head", "pool"), None),
            P(("group", "req", "head"), None),
            P(("group", "req", "head"), None),
            P(("req", "head"), None, "pool", None),
            P(("req", "head"), "pool", None),
        ),
        out_specs=P(("group", "req", "head"), "pool"),
        check_vma=False,
    )
```

```python
import functools

import jax
import jax.numpy as jnp
import numpy as np
from jax import lax
from jax.experimental import pallas as pl
from jax.experimental.pallas import tpu as pltpu
from jax.sharding import PartitionSpec as P

F32 = jnp.float32
BF16 = jnp.bfloat16
VMEM_LIMIT = 56 * 2**20
LANES = 128


def send(value, axes, step):
    size = lax.axis_size(axes)
    return lax.ppermute(value, axes, [(i, i ^ step) for i in range(size)])


def dot(a, b, contract=((1,), (0,))):
    return lax.dot_general(a, b, (contract, ((), ())), preferred_element_type=F32)


def kernel_call(body, out_shape, args, scratch=()):
    return pl.pallas_call(
        body,
        out_shape=out_shape,
        in_specs=[pl.BlockSpec(memory_space=pltpu.VMEM)] * len(args),
        out_specs=jax.tree.map(lambda _: pl.BlockSpec(memory_space=pltpu.VMEM), out_shape),
        scratch_shapes=list(scratch),
        compiler_params=pltpu.CompilerParams(vmem_limit_bytes=VMEM_LIMIT),
    )(*args)


def column(row, start, count):
    lane = lax.broadcasted_iota(jnp.int32, (count, row.shape[1]), 1)
    line = lax.broadcasted_iota(jnp.int32, (count, row.shape[1]), 0)
    return jnp.sum(jnp.where(lane == line + start, row, 0.0), axis=1, keepdims=True)


def place_kernel(sizes, residual_ref, choice_ref, route_ref, placed_ref):
    heads, pools, planes = sizes
    head = lax.axis_index("head")
    first = jnp.where(lax.axis_index("pool") == 0, 1.0, 0.0)
    rows_here, width = residual_ref.shape
    part = rows_here // pools
    total = heads * rows_here
    line = lax.broadcasted_iota(jnp.int32, (total, rows_here), 0)
    lane = lax.broadcasted_iota(jnp.int32, (total, rows_here), 1)
    own = None
    for p in range(pools):
        inside = line - (p * heads * part + head * part)
        one = (inside >= 0) & (inside < part) & (lane == inside + p * part)
        own = one if own is None else own | one
    spread = jnp.where(own, first, 0.0)
    placed_ref[:, :width] = dot(spread.astype(BF16), residual_ref[...]).astype(BF16)
    mixes = placed_ref.shape[1] - width
    target = lax.broadcasted_iota(jnp.int32, (total, mixes), 1)
    mix = jnp.zeros((total, mixes), F32)
    for k in range(choice_ref.shape[0]):
        expert = jnp.sum(spread * choice_ref[k : k + 1, :].astype(F32), axis=1, keepdims=True).astype(jnp.int32)
        weight = jnp.sum(spread * route_ref[k : k + 1, :], axis=1, keepdims=True)
        high = weight.astype(BF16).astype(F32)
        lanes = (expert % heads) * (mixes // heads) + expert // heads
        mix = mix + jnp.where(target == lanes, high, 0.0)
        mix = mix + jnp.where(target == lanes + planes, weight - high, 0.0)
    placed_ref[:, width:] = mix.astype(BF16)


def attend_kernel(sizes, q_ref, new_ref, own_ref, other_ref, own_ints_ref, other_ints_ref, placed_ref, order_ref, weight_ref, out_ref):
    requests, pages, moved, page, heads, pools, head_dim = sizes
    slots = own_ref.shape[0] // page
    here = lax.axis_index("pool")
    group = q_ref.shape[1] // head_dim // pools
    rows = requests // pools
    width = weight_ref.shape[1]
    columns = width // heads
    mixes = (placed_ref.shape[1] - width) // heads

    ints = [own_ints_ref[...].astype(F32), other_ints_ref[...].astype(F32)]
    live_from, live_count = [], []
    for q in range(2):
        row, across = ints[q], ints[1 - q]
        base = pages * requests
        length = column(row, base, requests)
        for j in range(pages):
            slot = column(row, j * requests, requests)
            source = slot + float(q * slots)
            for k in range(moved):
                leave = column(across, base + requests + k, 1)
                arrive = column(row, base + requests + moved + k, 1)
                source = jnp.where(slot == arrive, leave + float((1 - q) * slots), source)
            live_from.append((source * float(page)).astype(jnp.int32))
            live_count.append(jnp.clip(length - float(j * page), 0.0, float(page)).astype(jnp.int32))

    def cache_mask(offset, count):
        entry = lax.broadcasted_iota(jnp.int32, (requests, count), 1) + offset
        mask = None
        for start, amount in zip(live_from, live_count):
            apart = entry - start
            one = (apart >= 0) & (apart < amount)
            mask = one if mask is None else mask | one
        return mask

    count = own_ref.shape[0]
    fresh = new_ref.shape[0] // requests
    entry = lax.broadcasted_iota(jnp.int32, (requests, new_ref.shape[0]), 1)
    first = lax.broadcasted_iota(jnp.int32, (requests, new_ref.shape[0]), 0) * fresh
    masks = [cache_mask(0, count), cache_mask(count, count), (entry >= first) & (entry < first + fresh)]
    queries = jnp.concatenate(
        [
            q_ref[:, pl.ds(pl.multiple_of((here * group + g) * head_dim, LANES), head_dim)]
            for g in range(group)
        ],
        axis=0,
    )
    scale = head_dim ** (-0.5)
    scores = []
    for ref, mask in zip((own_ref, other_ref, new_ref), masks):
        score = dot(queries, ref[:, :head_dim], ((1,), (1,))) * scale
        bias = jnp.where(mask, 0.0, -jnp.inf)
        scores.append(score + jnp.concatenate([bias] * group, axis=0))
    largest = functools.reduce(
        jnp.maximum, [jnp.max(score, axis=1, keepdims=True) for score in scores]
    )
    total, value = 0.0, 0.0
    for ref, score in zip((own_ref, other_ref, new_ref), scores):
        weights = jnp.exp(score - largest)
        total = total + jnp.sum(weights, axis=1, keepdims=True)
        value = value + dot(weights.astype(BF16), ref[:, head_dim:])
    value = (value / total).astype(BF16)
    attended = jnp.concatenate(
        [value[g * requests : (g + 1) * requests] for g in range(group)], axis=1
    )
    attended = dot(order_ref[...], attended).astype(BF16)
    partial = dot(attended, weight_ref[...])
    placed = placed_ref[...].astype(F32)
    partial = partial + placed[:, :width]
    for h in range(heads):
        for p in range(pools):
            at = slice(p * rows, (p + 1) * rows)
            out_ref[h * pools + p, :, :columns] = partial[
                at, h * columns : (h + 1) * columns
            ].astype(BF16)
            out_ref[h * pools + p, :, columns:] = placed[
                at, width + h * mixes : width + (h + 1) * mixes
            ].astype(BF16)


def expert_kernel(sizes, blocks_ref, mix_ref, own_up_ref, other_up_ref, own_down_ref, other_down_ref, gain_ref, order_ref, out_ref):
    heads, planes = sizes
    head, plane = lax.axis_index("head"), lax.axis_index("req")
    columns = blocks_ref.shape[3]
    plane_rows = blocks_ref.shape[2]
    rows = planes * plane_rows
    width = heads * columns
    units = own_down_ref.shape[0]
    squares, projected = 0.0, 0.0
    for h in range(heads):
        at = slice(h * columns, (h + 1) * columns)
        block = blocks_ref[h].astype(F32).reshape(rows, columns)
        squares = squares + jnp.sum(block * block, axis=1, keepdims=True)
        block = (block * gain_ref[:, at]).astype(BF16)
        weights = jnp.concatenate(
            [own_up_ref[:units, at], other_up_ref[:units, at], own_up_ref[units:, at], other_up_ref[units:, at]],
            axis=0,
        )
        projected = projected + dot(block, weights, ((1,), (1,)))
    projected = projected * lax.rsqrt(squares / width + 1e-06)
    gate, up = projected[:, : 2 * units], projected[:, 2 * units :]
    mix = mix_ref[...].astype(F32).reshape(rows, mix_ref.shape[2])
    lane = lax.broadcasted_iota(jnp.int32, mix.shape, 1)
    route = jnp.sum(
        jnp.where((lane == plane) | (lane == plane + planes), mix, 0.0), axis=1, keepdims=True
    )
    activated = (gate / (1.0 + jnp.exp(-gate)) * up * route).astype(BF16)
    activated = dot(order_ref[...], activated).astype(BF16)
    down = jnp.concatenate([own_down_ref[...], other_down_ref[...]], axis=0)
    line = lax.broadcasted_iota(jnp.int32, (rows, columns), 0) - plane * plane_rows
    here = jnp.where(
        (line >= 0) & (line < plane_rows), blocks_ref[head].astype(F32).reshape(rows, columns), 0.0
    )
    here = dot(order_ref[...], here.astype(BF16))
    for h in range(heads):
        at = slice(h * columns, (h + 1) * columns)
        part = dot(activated, down[:, at]) + jnp.where(head == h, here, 0.0)
        for to in range(heads):
            lines = slice(to * rows // heads, (to + 1) * rows // heads)
            out_ref[to, :, at] = part[lines].astype(BF16)


def one_hot(rows):
    return jnp.asarray(np.eye(len(rows), dtype=np.float32)[np.asarray(rows)], BF16)


def exchange(value, axes):
    return lax.all_to_all(value, axes, split_axis=0, concat_axis=0, tiled=True)


def to_all(value, axes):
    return exchange(jnp.broadcast_to(value[None], (lax.axis_size(axes), *value.shape)), axes)


def local(
    queries,
    new_entries,
    cache_pages,
    page_table,
    cached_length,
    leave_slots,
    arrive_slots,
    residual,
    norm_gain,
    output_weight,
    expert_choice,
    route_weight,
    gate_up,
    down_weight,
):
    pools, heads, planes = lax.axis_size("pool"), lax.axis_size("head"), lax.axis_size("req")
    requests = queries.shape[0]
    slots, page, entry = cache_pages.shape[1:]
    moved = leave_slots.shape[0]
    pages = page_table.shape[2]
    rows_here, width = residual.shape
    part = rows_here // pools
    columns = width // heads
    mixes = 2 * planes + -2 * planes % LANES

    own_cache = cache_pages.reshape(slots * page, entry)
    other_cache = send(own_cache, "pool", 1)
    ints = jnp.concatenate(
        [page_table[:, 0, j] for j in range(pages)]
        + [cached_length.reshape(-1), leave_slots, arrive_slots]
    )
    ints = jnp.pad(ints, (0, -ints.shape[0] % LANES)).reshape(1, -1)
    other_ints = send(ints, "pool", 1)

    placed = kernel_call(
        functools.partial(place_kernel, (heads, pools, planes)),
        jax.ShapeDtypeStruct((requests, width + heads * mixes), BF16),
        (residual, expert_choice.T, route_weight.T),
    )
    order = [
        h * rows_here + p * part + i for p in range(pools) for h in range(heads) for i in range(part)
    ]
    args = (
        queries,
        new_entries.reshape(-1, entry),
        own_cache,
        other_cache,
        ints,
        other_ints,
        placed,
        one_hot(order),
        output_weight,
    )
    sizes = (requests, pages, moved, page, heads, pools, entry // 2)
    pieces = kernel_call(
        functools.partial(attend_kernel, sizes),
        jax.ShapeDtypeStruct((heads * pools, requests // pools, columns + mixes), BF16),
        args,
    )
    hidden = jnp.sum(exchange(pieces, ("head", "pool")).astype(F32), axis=0).astype(BF16)

    held = lax.optimization_barrier((gate_up, down_weight, other_cache))
    other_up = send(held[0].reshape(-1, width), "pool", 1)
    other_down = send(held[1].reshape(-1, width), "pool", 1)

    plane_blocks = to_all(hidden, "req")
    blocks = to_all(plane_blocks[:, :, :columns], "head")
    order = [
        (r * heads + h) * part + i for h in range(heads) for r in range(planes) for i in range(part)
    ]
    args = (
        blocks,
        plane_blocks[:, :, columns:],
        gate_up.reshape(-1, width),
        other_up,
        down_weight.reshape(-1, width),
        other_down,
        norm_gain.reshape(1, -1),
        one_hot(order),
    )
    pieces = kernel_call(
        functools.partial(expert_kernel, (heads, planes)),
        jax.ShapeDtypeStruct((heads, planes * part, width), BF16),
        args,
    )
    mixed = jnp.sum(exchange(pieces, "head").astype(F32), axis=0).astype(BF16)
    mixed = mixed.reshape(planes, part, pools, width // pools).transpose(0, 2, 1, 3)
    mixed = exchange(mixed.reshape(planes * pools, part, -1), ("req", "pool"))
    total = jnp.sum(mixed.reshape(planes, pools, part, -1).astype(F32), axis=0)
    return total.reshape(rows_here, -1).astype(BF16)


def solution(mesh):
    return jax.shard_map(
        local,
        mesh=mesh,
        in_specs=(
            P(("group", "req"), "head"),
            P(("group", "req"), None, "head", None),
            P("head", ("group", "req", "pool"), None, None),
            P(("group", "req"), "pool", None),
            P(("group", "req"), "pool"),
            P(("group", "req", "pool")),
            P(("group", "req", "pool")),
            P(("group", "req", "head"), None),
            P(),
            P(("head", "pool"), None),
            P(("group", "req", "head"), None),
            P(("group", "req", "head"), None),
            P(("req", "head"), None, "pool", None),
            P(("req", "head"), "pool", None),
        ),
        out_specs=P(("group", "req", "head"), "pool"),
        check_vma=False,
    )
```

```python
import functools

import jax
import jax.numpy as jnp
import numpy as np
from jax import lax
from jax.experimental import pallas as pl
from jax.experimental.pallas import tpu as pltpu
from jax.sharding import PartitionSpec as P

F32 = jnp.float32
BF16 = jnp.bfloat16
VMEM_LIMIT = 32 * 2**20
LANES = 128


def send(value, axes, step):
    size = lax.axis_size(axes)
    return lax.ppermute(value, axes, [(i, i ^ step) for i in range(size)])


def dot(a, b, contract=((1,), (0,))):
    return lax.dot_general(a, b, (contract, ((), ())), preferred_element_type=F32)


def kernel_call(body, out_shape, args, scratch=()):
    return pl.pallas_call(
        body,
        out_shape=jax.tree.map(lambda out: pltpu.VMEM(out.shape, out.dtype), out_shape),
        in_specs=[pl.BlockSpec(memory_space=pltpu.VMEM)] * len(args),
        out_specs=jax.tree.map(lambda _: pl.BlockSpec(memory_space=pltpu.VMEM), out_shape),
        scratch_shapes=list(scratch),
        compiler_params=pltpu.CompilerParams(vmem_limit_bytes=VMEM_LIMIT),
    )(*[pltpu.with_memory_space_constraint(arg, pltpu.VMEM) for arg in args])


def column(row, start, count):
    lane = lax.broadcasted_iota(jnp.int32, (count, row.shape[1]), 1)
    line = lax.broadcasted_iota(jnp.int32, (count, row.shape[1]), 0)
    return jnp.sum(jnp.where(lane == line + start, row, 0.0), axis=1, keepdims=True)


def place_kernel(sizes, residual_ref, choice_ref, route_ref, placed_ref):
    heads, pools, planes = sizes
    head, pool = lax.axis_index("head"), lax.axis_index("pool")
    first = jnp.where(pool == 0, 1.0, 0.0)
    rows_here, width = residual_ref.shape
    part = rows_here // pools
    total = heads * rows_here
    line = lax.broadcasted_iota(jnp.int32, (total, rows_here), 0)
    lane = lax.broadcasted_iota(jnp.int32, (total, rows_here), 1)
    own = None
    for p in range(pools):
        inside = line - (p * heads * part + head * part)
        one = (inside >= 0) & (inside < part) & (lane == inside + (pool ^ p) * part)
        own = one if own is None else own | one
    spread = jnp.where(own, first, 0.0)
    mixes = placed_ref.shape[1] - width
    placed = dot(spread.astype(BF16), residual_ref[...])
    target = lax.broadcasted_iota(jnp.int32, (total, mixes), 1)
    mix = jnp.zeros((total, mixes), F32)
    for k in range(choice_ref.shape[0]):
        expert = jnp.sum(spread * choice_ref[k : k + 1, :].astype(F32), axis=1, keepdims=True).astype(jnp.int32)
        weight = jnp.sum(spread * route_ref[k : k + 1, :], axis=1, keepdims=True)
        high = weight.astype(BF16).astype(F32)
        lanes = (expert % heads) * (mixes // heads) + expert // heads
        mix = mix + jnp.where(target == lanes, high, 0.0)
        mix = mix + jnp.where(target == lanes + planes, weight - high, 0.0)
    columns, share = width // heads, mixes // heads
    for h in range(heads):
        start = h * (columns + share)
        placed_ref[:, start : start + columns] = placed[:, h * columns : (h + 1) * columns].astype(BF16)
        placed_ref[:, start + columns : start + columns + share] = mix[
            :, h * share : (h + 1) * share
        ].astype(BF16)


def attend_kernel(sizes, q_ref, new_ref, own_ref, other_ref, own_ints_ref, other_ints_ref, placed_ref, order_ref, weight_ref, own_out_ref, other_out_ref):
    requests, pages, moved, page, heads, pools, head_dim = sizes
    slots = own_ref.shape[0] // page
    here = lax.axis_index("pool")
    group = q_ref.shape[1] // head_dim // pools
    rows = requests // pools
    width = weight_ref.shape[1]
    columns = width // heads
    mixes = (placed_ref.shape[1] - width) // heads

    ints = [own_ints_ref[...].astype(F32), other_ints_ref[...].astype(F32)]
    live_from, live_count = [], []
    for q in range(2):
        row, across = ints[q], ints[1 - q]
        base = pages * requests
        length = column(row, base, requests)
        for j in range(pages):
            slot = column(row, j * requests, requests)
            source = slot + float(q * slots)
            for k in range(moved):
                leave = column(across, base + requests + k, 1)
                arrive = column(row, base + requests + moved + k, 1)
                source = jnp.where(slot == arrive, leave + float((1 - q) * slots), source)
            live_from.append((source * float(page)).astype(jnp.int32))
            live_count.append(jnp.clip(length - float(j * page), 0.0, float(page)).astype(jnp.int32))

    def cache_mask(offset, count):
        entry = lax.broadcasted_iota(jnp.int32, (requests, count), 1) + offset
        mask = None
        for start, amount in zip(live_from, live_count):
            apart = entry - start
            one = (apart >= 0) & (apart < amount)
            mask = one if mask is None else mask | one
        return mask

    count = own_ref.shape[0]
    fresh = new_ref.shape[0] // requests
    entry = lax.broadcasted_iota(jnp.int32, (requests, new_ref.shape[0]), 1)
    first = lax.broadcasted_iota(jnp.int32, (requests, new_ref.shape[0]), 0) * fresh
    masks = [cache_mask(0, count), cache_mask(count, count), (entry >= first) & (entry < first + fresh)]
    queries = jnp.concatenate(
        [
            q_ref[:, pl.ds(pl.multiple_of((here * group + g) * head_dim, LANES), head_dim)]
            for g in range(group)
        ],
        axis=0,
    )
    scale = head_dim ** (-0.5)
    scores = []
    for ref, mask in zip((own_ref, other_ref, new_ref), masks):
        score = dot(queries, ref[:, :head_dim], ((1,), (1,))) * scale
        bias = jnp.where(mask, 0.0, -jnp.inf)
        scores.append(score + jnp.concatenate([bias] * group, axis=0))
    largest = functools.reduce(
        jnp.maximum, [jnp.max(score, axis=1, keepdims=True) for score in scores]
    )
    total, value = 0.0, 0.0
    for ref, score in zip((own_ref, other_ref, new_ref), scores):
        weights = jnp.exp(score - largest)
        total = total + jnp.sum(weights, axis=1, keepdims=True)
        value = value + dot(weights.astype(BF16), ref[:, head_dim:])
    value = (value / total).astype(BF16)
    attended = jnp.concatenate(
        [value[g * requests : (g + 1) * requests] for g in range(group)], axis=1
    )
    attended = dot(order_ref[...], attended).astype(BF16)
    partial = dot(attended, weight_ref[...])
    for h in range(heads):
        start = h * (columns + mixes)
        at = slice(start, start + columns)
        part = partial[:, h * columns : (h + 1) * columns] + placed_ref[:, at].astype(F32)
        own_out_ref[:, at] = part[:rows]
        other_out_ref[:, at] = part[rows:].astype(BF16)
        at = slice(start + columns, start + columns + mixes)
        part = placed_ref[:, at].astype(F32)
        own_out_ref[:, at] = part[:rows]
        other_out_ref[:, at] = part[rows:].astype(BF16)


def split_kernel(own_ref, other_ref, *outs):
    head = lax.axis_index("head")
    columns = own_ref.shape[1] // len(outs)
    for step, out in enumerate(outs):
        at = pl.ds(pl.multiple_of((head ^ step) * columns, LANES), columns)
        out[...] = (own_ref[:, at] + other_ref[:, at].astype(F32)).astype(out.dtype)


def expert_kernel(sizes, *refs):
    heads, planes = sizes
    blocks, refs = refs[:heads], refs[heads:]
    own_up_ref, other_up_ref, own_down_ref, other_down_ref, gain_ref, order_ref = refs[:6]
    outs = refs[6:]
    head, plane = lax.axis_index("head"), lax.axis_index("req")
    plane_rows, columns = blocks[1].shape[1:]
    rows = planes * plane_rows
    width = heads * columns
    units = own_down_ref.shape[0]
    squares, projected = 0.0, 0.0
    for step in range(heads):
        at = pl.ds(pl.multiple_of((head ^ step) * columns, LANES), columns)
        block = blocks[step][:, :, :columns].astype(F32).reshape(rows, columns)
        squares = squares + jnp.sum(block * block, axis=1, keepdims=True)
        block = (block * gain_ref[:, at]).astype(BF16)
        weights = jnp.concatenate(
            [own_up_ref[:units, at], other_up_ref[:units, at], own_up_ref[units:, at], other_up_ref[units:, at]],
            axis=0,
        )
        projected = projected + dot(block, weights, ((1,), (1,)))
    projected = projected * lax.rsqrt(squares / width + 1e-06)
    gate, up = projected[:, : 2 * units], projected[:, 2 * units :]
    mix = blocks[0][:, :, columns:].astype(F32)
    mix = mix.reshape(rows, mix.shape[2])
    lane = lax.broadcasted_iota(jnp.int32, mix.shape, 1)
    route = jnp.sum(
        jnp.where((lane == plane) | (lane == plane + planes), mix, 0.0), axis=1, keepdims=True
    )
    activated = (gate / (1.0 + jnp.exp(-gate)) * up * route).astype(BF16)
    activated = dot(order_ref[...], activated).astype(BF16)
    down = jnp.concatenate([own_down_ref[...], other_down_ref[...]], axis=0)
    line = lax.broadcasted_iota(jnp.int32, (rows, columns), 0)
    own = blocks[0][:, :, :columns].astype(F32).reshape(rows, columns)
    own = dot(order_ref[...], jnp.where(line < plane_rows, own, 0.0).astype(BF16))
    count = rows // heads
    for h in range(heads):
        at = slice(h * columns, (h + 1) * columns)
        part = dot(activated, down[:, at]) + jnp.where(head == h, own, 0.0)
        for step, out in enumerate(outs):
            out[:, at] = part[step * count : (step + 1) * count].astype(out.dtype)


def halve_kernel(*refs):
    parts, (own_ref, other_ref) = refs[:-2], refs[-2:]
    pool = lax.axis_index("pool")
    columns = own_ref.shape[1]
    for out, to in ((own_ref, pool), (other_ref, 1 - pool)):
        at = pl.ds(pl.multiple_of(to * columns, LANES), columns)
        out[...] = functools.reduce(
            jnp.add, [part[:, at].astype(F32) for part in parts]
        ).astype(BF16)


def spread_kernel(own_ref, other_ref, order_ref, *outs):
    pool = lax.axis_index("pool")
    own, other = own_ref[...].astype(F32), other_ref[...].astype(F32)
    both = jnp.concatenate([jnp.where(pool == 0, own, other), jnp.where(pool == 0, other, own)], axis=0)
    both = both.astype(BF16)
    columns = both.shape[1] // 2
    value = dot(order_ref[0], both[:, :columns]) + dot(order_ref[1], both[:, columns:])
    count = value.shape[0] // len(outs)
    for step, out in enumerate(outs):
        out[...] = value[step * count : (step + 1) * count].astype(BF16)


def total_kernel(*refs):
    parts, out_ref = refs[:-1], refs[-1]
    total = functools.reduce(jnp.add, [part[...].astype(F32) for part in parts])
    rows, columns = total.shape[0] // 2, total.shape[1]
    out_ref[:, :columns] = total[:rows].astype(BF16)
    out_ref[:, columns:] = total[rows:].astype(BF16)


def one_hot(rows, count):
    picked = np.asarray(rows)[..., None] == np.arange(count)
    return jnp.asarray(picked.astype(np.float32), BF16)


def shape(*dims, dtype=BF16):
    return jax.ShapeDtypeStruct(dims, dtype)


def local(
    queries,
    new_entries,
    cache_pages,
    page_table,
    cached_length,
    leave_slots,
    arrive_slots,
    residual,
    norm_gain,
    output_weight,
    expert_choice,
    route_weight,
    gate_up,
    down_weight,
):
    pools, heads, planes = lax.axis_size("pool"), lax.axis_size("head"), lax.axis_size("req")
    requests = queries.shape[0]
    slots, page, entry = cache_pages.shape[1:]
    moved = leave_slots.shape[0]
    pages = page_table.shape[2]
    rows_here, width = residual.shape
    part = rows_here // pools
    columns = width // heads
    mixes = 2 * planes + -2 * planes % LANES

    ints = jnp.concatenate(
        [page_table[:, 0, j] for j in range(pages)]
        + [cached_length.reshape(-1), leave_slots, arrive_slots]
    )
    ints = jnp.pad(ints, (0, -ints.shape[0] % LANES)).reshape(1, -1)
    own_cache = cache_pages.reshape(slots * page, entry)
    other_cache = send(own_cache, "pool", 1)
    other_ints = send(ints, "pool", 1)

    head, pool = lax.axis_index("head"), lax.axis_index("pool")
    placed = kernel_call(
        functools.partial(place_kernel, (heads, pools, planes)),
        shape(requests, heads * (columns + mixes)),
        (residual, expert_choice.T, route_weight.T),
    )
    order = [
        [h * rows_here + (here ^ p) * part + i for p in range(pools) for h in range(heads) for i in range(part)]
        for here in range(pools)
    ]
    args = (
        queries,
        new_entries.reshape(-1, entry),
        own_cache,
        other_cache,
        ints,
        other_ints,
        placed,
        lax.dynamic_index_in_dim(one_hot(order, requests), pool, 0, False),
        output_weight,
    )
    rows = requests // pools
    sizes = (requests, pages, moved, page, heads, pools, entry // 2)
    own, other = kernel_call(
        functools.partial(attend_kernel, sizes),
        [shape(rows, heads * (columns + mixes), dtype=F32), shape(rows, heads * (columns + mixes))],
        args,
    )
    other = send(other, "pool", 1)

    gate_up, down_weight = gate_up.reshape(-1, width), down_weight.reshape(-1, width)
    held = lax.optimization_barrier((gate_up, down_weight, other))
    other_up, other_down = send(held[0], "pool", 1), send(held[1], "pool", 1)

    piece = shape(rows, columns + mixes)
    pieces = kernel_call(split_kernel, [shape(rows, columns + mixes, dtype=F32)] + [piece] * (heads - 1), (own, other))
    hidden = pieces[0]
    for step in range(1, heads):
        hidden = hidden + send(pieces[step], "head", step).astype(F32)
    hidden = hidden.astype(BF16)

    plane_blocks = jnp.stack([hidden] + [send(hidden, "req", step) for step in range(1, planes)])
    sent = plane_blocks[:, :, :columns]
    blocks = [plane_blocks] + [send(sent, "head", step) for step in range(1, heads)]
    order = [
        [(r * heads + (here ^ h)) * part + i for h in range(heads) for r in range(planes) for i in range(part)]
        for here in range(heads)
    ]
    args = (
        *blocks,
        gate_up,
        other_up,
        down_weight,
        other_down,
        norm_gain.reshape(1, -1),
        lax.dynamic_index_in_dim(one_hot(order, planes * rows), head, 0, False),
    )
    piece = shape(planes * part, width)
    pieces = kernel_call(
        functools.partial(expert_kernel, (heads, planes)),
        [shape(planes * part, width, dtype=F32)] + [piece] * (heads - 1),
        args,
    )
    arrived = [pieces[0]] + [send(pieces[step], "head", step) for step in range(1, heads)]
    own, other = kernel_call(halve_kernel, [shape(planes * part, width // pools)] * 2, arrived)
    other = send(other, "pool", 1)
    order = [
        [
            p * planes * part + r * part + i if half == at else -1
            for r in range(planes)
            for at in range(2)
            for p in range(pools)
            for i in range(part)
        ]
        for half in range(2)
    ]
    piece = shape(2 * rows_here, width // pools // 2)
    pieces = kernel_call(
        spread_kernel, [piece] * planes, (own, other, one_hot(order, pools * planes * part))
    )
    arrived = [pieces[0]] + [send(pieces[step], "req", step) for step in range(1, planes)]
    return kernel_call(total_kernel, shape(rows_here, width // pools), arrived)


def solution(mesh):
    return jax.shard_map(
        local,
        mesh=mesh,
        in_specs=(
            P(("group", "req"), "head"),
            P(("group", "req"), None, "head", None),
            P("head", ("group", "req", "pool"), None, None),
            P(("group", "req"), "pool", None),
            P(("group", "req"), "pool"),
            P(("group", "req", "pool")),
            P(("group", "req", "pool")),
            P(("group", "req", "head"), None),
            P(),
            P(("head", "pool"), None),
            P(("group", "req", "head"), None),
            P(("group", "req", "head"), None),
            P(("req", "head"), None, "pool", None),
            P(("req", "head"), "pool", None),
        ),
        out_specs=P(("group", "req", "head"), "pool"),
        check_vma=False,
    )
```

```python
import functools

import jax
import jax.numpy as jnp
import numpy as np
from jax import lax
from jax.experimental import pallas as pl
from jax.experimental.pallas import tpu as pltpu
from jax.sharding import PartitionSpec as P

F32 = jnp.float32
BF16 = jnp.bfloat16
VMEM_LIMIT = 32 * 2**20
LANES = 128


def send(value, axes, step):
    size = lax.axis_size(axes)
    return lax.ppermute(value, axes, [(i, i ^ step) for i in range(size)])


def dot(a, b, contract=((1,), (0,))):
    return lax.dot_general(a, b, (contract, ((), ())), preferred_element_type=F32)


def kernel_call(body, out_shape, args, scratch=(), outside=()):
    return pl.pallas_call(
        body,
        out_shape=jax.tree.map(lambda out: pltpu.VMEM(out.shape, out.dtype), out_shape),
        in_specs=[pl.BlockSpec(memory_space=pl.ANY)] * len(outside)
        + [pl.BlockSpec(memory_space=pltpu.VMEM)] * len(args),
        out_specs=jax.tree.map(lambda _: pl.BlockSpec(memory_space=pltpu.VMEM), out_shape),
        scratch_shapes=list(scratch),
        compiler_params=pltpu.CompilerParams(vmem_limit_bytes=VMEM_LIMIT),
    )(*outside, *args)


def held(*args):
    return [pltpu.with_memory_space_constraint(arg, pltpu.VMEM) for arg in args]


def column(row, start, count):
    lane = lax.broadcasted_iota(jnp.int32, (count, row.shape[1]), 1)
    line = lax.broadcasted_iota(jnp.int32, (count, row.shape[1]), 0)
    return jnp.sum(jnp.where(lane == line + start, row, 0.0), axis=1, keepdims=True)


def place_kernel(sizes, *refs):
    heads, pools, planes, count = sizes
    sources, refs = refs[:count], refs[count:]
    residual_ref, choice_ref, route_ref, placed_ref = refs[:4]
    targets, semaphores = refs[4 : 4 + count], refs[-1]
    head, pool = lax.axis_index("head"), lax.axis_index("pool")
    picked = {count - 2: pool, count - 1: head}
    copies = []
    for i in range(count):
        source = sources[i].at[picked[i]] if i in picked else sources[i]
        copies.append(pltpu.make_async_copy(source, targets[i], semaphores.at[i]))
    for copy in copies:
        copy.start()
    first = jnp.where(pool == 0, 1.0, 0.0)
    rows_here, width = residual_ref.shape
    part = rows_here // pools
    total = heads * rows_here
    line = lax.broadcasted_iota(jnp.int32, (total, rows_here), 0)
    lane = lax.broadcasted_iota(jnp.int32, (total, rows_here), 1)
    own = None
    for p in range(pools):
        inside = line - (p * heads * part + head * part)
        one = (inside >= 0) & (inside < part) & (lane == inside + (pool ^ p) * part)
        own = one if own is None else own | one
    spread = jnp.where(own, first, 0.0)
    mixes = placed_ref.shape[1] - width
    placed = dot(spread.astype(BF16), residual_ref[...])
    target = lax.broadcasted_iota(jnp.int32, (total, mixes), 1)
    mix = jnp.zeros((total, mixes), F32)
    for k in range(choice_ref.shape[0]):
        expert = jnp.sum(spread * choice_ref[k : k + 1, :].astype(F32), axis=1, keepdims=True).astype(jnp.int32)
        weight = jnp.sum(spread * route_ref[k : k + 1, :], axis=1, keepdims=True)
        high = weight.astype(BF16).astype(F32)
        lanes = (expert % heads) * (mixes // heads) + expert // heads
        mix = mix + jnp.where(target == lanes, high, 0.0)
        mix = mix + jnp.where(target == lanes + planes, weight - high, 0.0)
    columns, share = width // heads, mixes // heads
    for h in range(heads):
        start = h * (columns + share)
        placed_ref[:, start : start + columns] = placed[:, h * columns : (h + 1) * columns].astype(BF16)
        placed_ref[:, start + columns : start + columns + share] = mix[
            :, h * share : (h + 1) * share
        ].astype(BF16)
    for copy in copies:
        copy.wait()


def attend_kernel(sizes, q_ref, new_ref, own_ref, other_ref, own_ints_ref, other_ints_ref, placed_ref, order_ref, weight_ref, own_out_ref, other_out_ref):
    requests, pages, moved, page, heads, pools, head_dim = sizes
    slots = own_ref.shape[0] // page
    here = lax.axis_index("pool")
    group = q_ref.shape[1] // head_dim // pools
    rows = requests // pools
    width = weight_ref.shape[1]
    columns = width // heads
    mixes = (placed_ref.shape[1] - width) // heads

    ints = [own_ints_ref[...].astype(F32), other_ints_ref[...].astype(F32)]
    live_from, live_count = [], []
    for q in range(2):
        row, across = ints[q], ints[1 - q]
        base = pages * requests
        length = column(row, base, requests)
        for j in range(pages):
            slot = column(row, j * requests, requests)
            source = slot + float(q * slots)
            for k in range(moved):
                leave = column(across, base + requests + k, 1)
                arrive = column(row, base + requests + moved + k, 1)
                source = jnp.where(slot == arrive, leave + float((1 - q) * slots), source)
            live_from.append((source * float(page)).astype(jnp.int32))
            live_count.append(jnp.clip(length - float(j * page), 0.0, float(page)).astype(jnp.int32))

    def cache_mask(offset, count):
        entry = lax.broadcasted_iota(jnp.int32, (requests, count), 1) + offset
        mask = None
        for start, amount in zip(live_from, live_count):
            apart = entry - start
            one = (apart >= 0) & (apart < amount)
            mask = one if mask is None else mask | one
        return mask

    count = own_ref.shape[0]
    fresh = new_ref.shape[0] // requests
    entry = lax.broadcasted_iota(jnp.int32, (requests, new_ref.shape[0]), 1)
    first = lax.broadcasted_iota(jnp.int32, (requests, new_ref.shape[0]), 0) * fresh
    masks = [cache_mask(0, count), cache_mask(count, count), (entry >= first) & (entry < first + fresh)]
    queries = jnp.concatenate(
        [
            q_ref[:, pl.ds(pl.multiple_of((here * group + g) * head_dim, LANES), head_dim)]
            for g in range(group)
        ],
        axis=0,
    )
    scale = head_dim ** (-0.5)
    scores = []
    for ref, mask in zip((own_ref, other_ref, new_ref), masks):
        score = dot(queries, ref[:, :head_dim], ((1,), (1,))) * scale
        bias = jnp.where(mask, 0.0, -jnp.inf)
        scores.append(score + jnp.concatenate([bias] * group, axis=0))
    largest = functools.reduce(
        jnp.maximum, [jnp.max(score, axis=1, keepdims=True) for score in scores]
    )
    total, value = 0.0, 0.0
    for ref, score in zip((own_ref, other_ref, new_ref), scores):
        weights = jnp.exp(score - largest)
        total = total + jnp.sum(weights, axis=1, keepdims=True)
        value = value + dot(weights.astype(BF16), ref[:, head_dim:])
    value = (value / total).astype(BF16)
    attended = jnp.concatenate(
        [value[g * requests : (g + 1) * requests] for g in range(group)], axis=1
    )
    attended = dot(order_ref[...], attended).astype(BF16)
    partial = dot(attended, weight_ref[...])
    for h in range(heads):
        start = h * (columns + mixes)
        at = slice(start, start + columns)
        part = partial[:, h * columns : (h + 1) * columns] + placed_ref[:, at].astype(F32)
        own_out_ref[:, at] = part[:rows]
        other_out_ref[:, at] = part[rows:].astype(BF16)
        at = slice(start + columns, start + columns + mixes)
        part = placed_ref[:, at].astype(F32)
        own_out_ref[:, at] = part[:rows]
        other_out_ref[:, at] = part[rows:].astype(BF16)


def split_kernel(own_ref, other_ref, *outs):
    head = lax.axis_index("head")
    columns = own_ref.shape[1] // len(outs)
    for step, out in enumerate(outs):
        at = pl.ds(pl.multiple_of((head ^ step) * columns, LANES), columns)
        out[...] = (own_ref[:, at] + other_ref[:, at].astype(F32)).astype(out.dtype)


def project_kernel(step, planes, block_ref, own_up_ref, other_up_ref, gain_ref, *refs):
    head = lax.axis_index("head")
    plane_rows = block_ref.shape[1]
    rows = planes * plane_rows
    columns = gain_ref.shape[1] // lax.axis_size("head")
    units = own_up_ref.shape[0] // 2
    at = pl.ds(pl.multiple_of((head ^ step) * columns, LANES), columns)
    block = block_ref[:, :, :columns].astype(F32).reshape(rows, columns)
    scaled = (block * gain_ref[:, at]).astype(BF16)
    weights = jnp.concatenate(
        [own_up_ref[:units, at], other_up_ref[:units, at], own_up_ref[units:, at], other_up_ref[units:, at]],
        axis=0,
    )
    projected = dot(scaled, weights, ((1,), (1,)))
    squares = jnp.sum(block * block, axis=1, keepdims=True)
    if step:
        before_ref, before_squares_ref, projected_ref, squares_ref = refs
        projected_ref[...] = before_ref[...] + projected
        squares_ref[...] = before_squares_ref[...] + squares
        return
    order_ref, projected_ref, squares_ref, route_ref, own_ref = refs
    projected_ref[...] = projected
    squares_ref[...] = squares
    plane = lax.axis_index("req")
    mix = block_ref[:, :, columns:].astype(F32)
    mix = mix.reshape(rows, mix.shape[2])
    lane = lax.broadcasted_iota(jnp.int32, mix.shape, 1)
    route_ref[...] = jnp.sum(
        jnp.where((lane == plane) | (lane == plane + planes), mix, 0.0), axis=1, keepdims=True
    )
    line = lax.broadcasted_iota(jnp.int32, (rows, columns), 0)
    own_ref[...] = dot(order_ref[...], jnp.where(line < plane_rows, block, 0.0).astype(BF16))


def expert_kernel(projected_ref, squares_ref, route_ref, own_ref, own_down_ref, other_down_ref, order_ref, *outs):
    heads = len(outs)
    head = lax.axis_index("head")
    rows, columns = own_ref.shape
    units = own_down_ref.shape[0]
    projected = projected_ref[...] * lax.rsqrt(squares_ref[...] / (heads * columns) + 1e-06)
    gate, up = projected[:, : 2 * units], projected[:, 2 * units :]
    activated = (gate / (1.0 + jnp.exp(-gate)) * up * route_ref[...]).astype(BF16)
    activated = dot(order_ref[...], activated).astype(BF16)
    down = jnp.concatenate([own_down_ref[...], other_down_ref[...]], axis=0)
    count = rows // heads
    for h in range(heads):
        at = slice(h * columns, (h + 1) * columns)
        part = dot(activated, down[:, at]) + jnp.where(head == h, own_ref[...], 0.0)
        for step, out in enumerate(outs):
            out[:, at] = part[step * count : (step + 1) * count].astype(out.dtype)


def halve_kernel(*refs):
    parts, (own_ref, other_ref) = refs[:-2], refs[-2:]
    pool = lax.axis_index("pool")
    columns = own_ref.shape[1]
    for out, to in ((own_ref, pool), (other_ref, 1 - pool)):
        at = pl.ds(pl.multiple_of(to * columns, LANES), columns)
        out[...] = functools.reduce(
            jnp.add, [part[:, at].astype(F32) for part in parts]
        ).astype(BF16)


def spread_kernel(own_ref, other_ref, order_ref, *outs):
    pool = lax.axis_index("pool")
    own, other = own_ref[...].astype(F32), other_ref[...].astype(F32)
    both = jnp.concatenate([jnp.where(pool == 0, own, other), jnp.where(pool == 0, other, own)], axis=0)
    both = both.astype(BF16)
    columns = both.shape[1] // 2
    value = dot(order_ref[0], both[:, :columns]) + dot(order_ref[1], both[:, columns:])
    count = value.shape[0] // len(outs)
    for step, out in enumerate(outs):
        out[...] = value[step * count : (step + 1) * count].astype(BF16)


def total_kernel(*refs):
    parts, out_ref = refs[:-1], refs[-1]
    total = functools.reduce(jnp.add, [part[...].astype(F32) for part in parts])
    rows, columns = total.shape[0] // 2, total.shape[1]
    out_ref[:, :columns] = total[:rows].astype(BF16)
    out_ref[:, columns:] = total[rows:].astype(BF16)


def one_hot(rows, count):
    picked = np.asarray(rows)[..., None] == np.arange(count)
    return jnp.asarray(picked.astype(np.float32), BF16)


def shape(*dims, dtype=BF16):
    return jax.ShapeDtypeStruct(dims, dtype)


def local(
    queries,
    new_entries,
    cache_pages,
    page_table,
    cached_length,
    leave_slots,
    arrive_slots,
    residual,
    norm_gain,
    output_weight,
    expert_choice,
    route_weight,
    gate_up,
    down_weight,
):
    pools, heads, planes = lax.axis_size("pool"), lax.axis_size("head"), lax.axis_size("req")
    requests = queries.shape[0]
    slots, page, entry = cache_pages.shape[1:]
    moved = leave_slots.shape[0]
    pages = page_table.shape[2]
    rows_here, width = residual.shape
    part = rows_here // pools
    columns = width // heads
    mixes = 2 * planes + -2 * planes % LANES

    ints = jnp.concatenate(
        [page_table[:, 0, j] for j in range(pages)]
        + [cached_length.reshape(-1), leave_slots, arrive_slots]
    )
    ints = jnp.pad(ints, (0, -ints.shape[0] % LANES)).reshape(1, -1)
    own_cache = cache_pages.reshape(slots * page, entry)
    other_cache = send(own_cache, "pool", 1)
    other_ints = send(ints, "pool", 1)

    gate_up, down_weight = gate_up.reshape(-1, width), down_weight.reshape(-1, width)
    other_up, other_down = send(gate_up, "pool", 1), send(down_weight, "pool", 1)

    rows = requests // pools
    pool_order = [
        [h * rows_here + (here ^ p) * part + i for p in range(pools) for h in range(heads) for i in range(part)]
        for here in range(pools)
    ]
    head_order = [
        [(r * heads + (here ^ h)) * part + i for h in range(heads) for r in range(planes) for i in range(part)]
        for here in range(heads)
    ]
    plane_order = [
        [
            p * planes * part + r * part + i if half == at else -1
            for r in range(planes)
            for at in range(2)
            for p in range(pools)
            for i in range(part)
        ]
        for half in range(2)
    ]
    outside = (
        own_cache,
        queries,
        output_weight,
        one_hot(plane_order, pools * planes * part),
        one_hot(pool_order, requests),
        one_hot(head_order, planes * rows),
    )
    copied = [shape(*array.shape[i // 4 :], dtype=array.dtype) for i, array in enumerate(outside)]
    placed, held_cache, held_queries, held_weight, plane_order, pool_order, head_order = kernel_call(
        functools.partial(place_kernel, (heads, pools, planes, len(outside))),
        [shape(requests, heads * (columns + mixes))] + copied,
        (residual, expert_choice.T, route_weight.T),
        [pltpu.SemaphoreType.DMA((len(outside),))],
        outside,
    )
    args = held(
        held_queries,
        new_entries.reshape(-1, entry),
        held_cache,
        other_cache,
        ints,
        other_ints,
        placed,
        pool_order,
        held_weight,
    )
    sizes = (requests, pages, moved, page, heads, pools, entry // 2)
    own, other = kernel_call(
        functools.partial(attend_kernel, sizes),
        [shape(rows, heads * (columns + mixes), dtype=F32), shape(rows, heads * (columns + mixes))],
        args,
    )
    other = send(other, "pool", 1)
    other, other_up, other_down = lax.optimization_barrier((other, other_up, other_down))
    piece = shape(rows, columns + mixes)
    pieces = kernel_call(
        split_kernel,
        [shape(rows, columns + mixes, dtype=F32)] + [piece] * (heads - 1),
        held(own, other),
    )
    hidden = pieces[0]
    for step in range(1, heads):
        hidden = hidden + send(pieces[step], "head", step).astype(F32)
    hidden = hidden.astype(BF16)

    plane_blocks = jnp.stack([hidden] + [send(hidden, "req", step) for step in range(1, planes)])
    sent = plane_blocks[:, :, :columns]
    weights = held(gate_up, other_up, norm_gain.reshape(1, -1))
    total = planes * rows
    sums = [shape(total, 2 * gate_up.shape[0], dtype=F32), shape(total, 1, dtype=F32)]
    *state, route, own = kernel_call(
        functools.partial(project_kernel, 0, planes),
        sums + [shape(total, 1, dtype=F32), shape(total, columns, dtype=F32)],
        held(plane_blocks, *weights, head_order),
    )
    for step in range(1, heads):
        state = kernel_call(
            functools.partial(project_kernel, step, planes),
            sums,
            held(send(sent, "head", step), *weights, *state),
        )
    piece = shape(planes * part, width)
    pieces = kernel_call(
        expert_kernel,
        [shape(planes * part, width, dtype=F32)] + [piece] * (heads - 1),
        held(*state, route, own, down_weight, other_down, head_order),
    )
    arrived = [pieces[0]] + [send(pieces[step], "head", step) for step in range(1, heads)]
    own, other = kernel_call(
        halve_kernel, [shape(planes * part, width // pools)] * 2, held(*arrived)
    )
    other = send(other, "pool", 1)
    piece = shape(2 * rows_here, width // pools // 2)
    pieces = kernel_call(spread_kernel, [piece] * planes, held(own, other, plane_order))
    arrived = [pieces[0]] + [send(pieces[step], "req", step) for step in range(1, planes)]
    return kernel_call(total_kernel, shape(rows_here, width // pools), held(*arrived))


def solution(mesh):
    return jax.shard_map(
        local,
        mesh=mesh,
        in_specs=(
            P(("group", "req"), "head"),
            P(("group", "req"), None, "head", None),
            P("head", ("group", "req", "pool"), None, None),
            P(("group", "req"), "pool", None),
            P(("group", "req"), "pool"),
            P(("group", "req", "pool")),
            P(("group", "req", "pool")),
            P(("group", "req", "head"), None),
            P(),
            P(("head", "pool"), None),
            P(("group", "req", "head"), None),
            P(("group", "req", "head"), None),
            P(("req", "head"), None, "pool", None),
            P(("req", "head"), "pool", None),
        ),
        out_specs=P(("group", "req", "head"), "pool"),
        check_vma=False,
    )
```

```python
import functools

import jax
import jax.numpy as jnp
import numpy as np
from jax import lax
from jax.experimental import pallas as pl
from jax.experimental.pallas import tpu as pltpu
from jax.sharding import PartitionSpec as P

F32 = jnp.float32
BF16 = jnp.bfloat16
VMEM_LIMIT = 32 * 2**20
LANES = 128


def send(value, axes, step):
    size = lax.axis_size(axes)
    return lax.ppermute(value, axes, [(i, i ^ step) for i in range(size)])


def dot(a, b, contract=((1,), (0,))):
    return lax.dot_general(a, b, (contract, ((), ())), preferred_element_type=F32)


def kernel_call(body, out_shape, args, scratch=(), outside=()):
    return pl.pallas_call(
        body,
        out_shape=jax.tree.map(lambda out: pltpu.VMEM(out.shape, out.dtype), out_shape),
        in_specs=[pl.BlockSpec(memory_space=pltpu.HBM)] * len(outside)
        + [pl.BlockSpec(memory_space=pltpu.VMEM)] * len(args),
        out_specs=jax.tree.map(lambda _: pl.BlockSpec(memory_space=pltpu.VMEM), out_shape),
        scratch_shapes=list(scratch),
        compiler_params=pltpu.CompilerParams(vmem_limit_bytes=VMEM_LIMIT),
    )(*[pltpu.with_memory_space_constraint(arg, pltpu.HBM) for arg in outside], *args)


def held(*args):
    return [pltpu.with_memory_space_constraint(arg, pltpu.VMEM) for arg in args]


def column(row, start, count):
    lane = lax.broadcasted_iota(jnp.int32, (count, row.shape[1]), 1)
    line = lax.broadcasted_iota(jnp.int32, (count, row.shape[1]), 0)
    return jnp.sum(jnp.where(lane == line + start, row, 0.0), axis=1, keepdims=True)


def place_kernel(sizes, *refs):
    heads, pools, planes, count = sizes
    sources, refs = refs[:count], refs[count:]
    residual_ref, choice_ref, route_ref, placed_ref = refs[:4]
    targets, semaphores = refs[4 : 4 + count], refs[-1]
    head, pool = lax.axis_index("head"), lax.axis_index("pool")
    picked = {count - 2: pool, count - 1: head}
    copies = []
    for i in range(count):
        source = sources[i].at[picked[i]] if i in picked else sources[i]
        copies.append(pltpu.make_async_copy(source, targets[i], semaphores.at[i]))
    for copy in copies:
        copy.start()
    first = jnp.where(pool == 0, 1.0, 0.0)
    rows_here, width = residual_ref.shape
    part = rows_here // pools
    total = heads * rows_here
    line = lax.broadcasted_iota(jnp.int32, (total, rows_here), 0)
    lane = lax.broadcasted_iota(jnp.int32, (total, rows_here), 1)
    own = None
    for p in range(pools):
        inside = line - (p * heads * part + head * part)
        one = (inside >= 0) & (inside < part) & (lane == inside + (pool ^ p) * part)
        own = one if own is None else own | one
    spread = jnp.where(own, first, 0.0)
    mixes = placed_ref.shape[1] - width
    placed = dot(spread.astype(BF16), residual_ref[...])
    target = lax.broadcasted_iota(jnp.int32, (total, mixes), 1)
    mix = jnp.zeros((total, mixes), F32)
    for k in range(choice_ref.shape[0]):
        expert = jnp.sum(spread * choice_ref[k : k + 1, :].astype(F32), axis=1, keepdims=True).astype(jnp.int32)
        weight = jnp.sum(spread * route_ref[k : k + 1, :], axis=1, keepdims=True)
        high = weight.astype(BF16).astype(F32)
        lanes = (expert % heads) * (mixes // heads) + expert // heads
        mix = mix + jnp.where(target == lanes, high, 0.0)
        mix = mix + jnp.where(target == lanes + planes, weight - high, 0.0)
    columns, share = width // heads, mixes // heads
    for h in range(heads):
        start = h * (columns + share)
        placed_ref[:, start : start + columns] = placed[:, h * columns : (h + 1) * columns].astype(BF16)
        placed_ref[:, start + columns : start + columns + share] = mix[
            :, h * share : (h + 1) * share
        ].astype(BF16)
    for copy in copies:
        copy.wait()


def attend_kernel(sizes, q_ref, new_ref, own_ref, other_ref, own_ints_ref, other_ints_ref, placed_ref, order_ref, weight_ref, own_out_ref, other_out_ref):
    requests, pages, moved, page, heads, pools, head_dim = sizes
    slots = own_ref.shape[0] // page
    here = lax.axis_index("pool")
    group = q_ref.shape[1] // head_dim // pools
    rows = requests // pools
    width = weight_ref.shape[1]
    columns = width // heads
    mixes = (placed_ref.shape[1] - width) // heads

    ints = [own_ints_ref[...].astype(F32), other_ints_ref[...].astype(F32)]
    live_from, live_count = [], []
    for q in range(2):
        row, across = ints[q], ints[1 - q]
        base = pages * requests
        length = column(row, base, requests)
        for j in range(pages):
            slot = column(row, j * requests, requests)
            source = slot + float(q * slots)
            for k in range(moved):
                leave = column(across, base + requests + k, 1)
                arrive = column(row, base + requests + moved + k, 1)
                source = jnp.where(slot == arrive, leave + float((1 - q) * slots), source)
            live_from.append((source * float(page)).astype(jnp.int32))
            live_count.append(jnp.clip(length - float(j * page), 0.0, float(page)).astype(jnp.int32))

    def cache_mask(offset, count):
        entry = lax.broadcasted_iota(jnp.int32, (requests, count), 1) + offset
        mask = None
        for start, amount in zip(live_from, live_count):
            apart = entry - start
            one = (apart >= 0) & (apart < amount)
            mask = one if mask is None else mask | one
        return mask

    count = own_ref.shape[0]
    fresh = new_ref.shape[0] // requests
    entry = lax.broadcasted_iota(jnp.int32, (requests, new_ref.shape[0]), 1)
    first = lax.broadcasted_iota(jnp.int32, (requests, new_ref.shape[0]), 0) * fresh
    masks = [cache_mask(0, count), cache_mask(count, count), (entry >= first) & (entry < first + fresh)]
    queries = jnp.concatenate(
        [
            q_ref[:, pl.ds(pl.multiple_of((here * group + g) * head_dim, LANES), head_dim)]
            for g in range(group)
        ],
        axis=0,
    )
    scale = head_dim ** (-0.5)
    scores = []
    for ref, mask in zip((own_ref, other_ref, new_ref), masks):
        score = dot(queries, ref[:, :head_dim], ((1,), (1,))) * scale
        bias = jnp.where(mask, 0.0, -jnp.inf)
        scores.append(score + jnp.concatenate([bias] * group, axis=0))
    largest = functools.reduce(
        jnp.maximum, [jnp.max(score, axis=1, keepdims=True) for score in scores]
    )
    total, value = 0.0, 0.0
    for ref, score in zip((own_ref, other_ref, new_ref), scores):
        weights = jnp.exp(score - largest)
        total = total + jnp.sum(weights, axis=1, keepdims=True)
        value = value + dot(weights.astype(BF16), ref[:, head_dim:])
    value = (value / total).astype(BF16)
    attended = jnp.concatenate(
        [value[g * requests : (g + 1) * requests] for g in range(group)], axis=1
    )
    attended = dot(order_ref[...], attended).astype(BF16)
    partial = dot(attended, weight_ref[...])
    for h in range(heads):
        start = h * (columns + mixes)
        at = slice(start, start + columns)
        part = partial[:, h * columns : (h + 1) * columns] + placed_ref[:, at].astype(F32)
        own_out_ref[:, at] = part[:rows]
        other_out_ref[:, at] = part[rows:].astype(BF16)
        at = slice(start + columns, start + columns + mixes)
        part = placed_ref[:, at].astype(F32)
        own_out_ref[:, at] = part[:rows]
        other_out_ref[:, at] = part[rows:].astype(BF16)


def split_kernel(own_ref, other_ref, *outs):
    head = lax.axis_index("head")
    columns = own_ref.shape[1] // len(outs)
    for step, out in enumerate(outs):
        at = pl.ds(pl.multiple_of((head ^ step) * columns, LANES), columns)
        out[...] = (own_ref[:, at] + other_ref[:, at].astype(F32)).astype(out.dtype)


def stack_kernel(*refs):
    parts, (all_ref, first_ref) = refs[:-2], refs[-2:]
    for step, part in enumerate(reversed(parts)):
        all_ref[step] = part[...]
        first_ref[step] = part[:, : first_ref.shape[2]]


def project_kernel(step, planes, block_ref, own_up_ref, other_up_ref, gain_ref, *refs):
    head = lax.axis_index("head")
    plane_rows = block_ref.shape[1]
    rows = planes * plane_rows
    columns = gain_ref.shape[1] // lax.axis_size("head")
    units = own_up_ref.shape[0] // 2
    at = pl.ds(pl.multiple_of((head ^ step) * columns, LANES), columns)
    block = block_ref[:, :, :columns].astype(F32).reshape(rows, columns)
    scaled = (block * gain_ref[:, at]).astype(BF16)
    weights = jnp.concatenate(
        [own_up_ref[:units, at], other_up_ref[:units, at], own_up_ref[units:, at], other_up_ref[units:, at]],
        axis=0,
    )
    projected = dot(scaled, weights, ((1,), (1,)))
    squares = jnp.sum(block * block, axis=1, keepdims=True)
    if step:
        before_ref, before_squares_ref, projected_ref, squares_ref = refs
        projected_ref[...] = before_ref[...] + projected
        squares_ref[...] = before_squares_ref[...] + squares
        return
    order_ref, projected_ref, squares_ref, route_ref, own_ref = refs
    projected_ref[...] = projected
    squares_ref[...] = squares
    plane = lax.axis_index("req")
    mix = block_ref[:, :, columns:].astype(F32)
    mix = mix.reshape(rows, mix.shape[2])
    lane = lax.broadcasted_iota(jnp.int32, mix.shape, 1)
    route_ref[...] = jnp.sum(
        jnp.where((lane == plane) | (lane == plane + planes), mix, 0.0), axis=1, keepdims=True
    )
    line = lax.broadcasted_iota(jnp.int32, (rows, columns), 0)
    own_ref[...] = dot(order_ref[...], jnp.where(line < plane_rows, block, 0.0).astype(BF16))


def expert_kernel(projected_ref, squares_ref, route_ref, own_ref, own_down_ref, other_down_ref, order_ref, *outs):
    heads = len(outs)
    head = lax.axis_index("head")
    rows, columns = own_ref.shape
    units = own_down_ref.shape[0]
    projected = projected_ref[...] * lax.rsqrt(squares_ref[...] / (heads * columns) + 1e-06)
    gate, up = projected[:, : 2 * units], projected[:, 2 * units :]
    activated = (gate / (1.0 + jnp.exp(-gate)) * up * route_ref[...]).astype(BF16)
    activated = dot(order_ref[...], activated).astype(BF16)
    down = jnp.concatenate([own_down_ref[...], other_down_ref[...]], axis=0)
    count = rows // heads
    for h in range(heads):
        at = slice(h * columns, (h + 1) * columns)
        part = dot(activated, down[:, at]) + jnp.where(head == h, own_ref[...], 0.0)
        for step, out in enumerate(outs):
            out[:, at] = part[step * count : (step + 1) * count].astype(out.dtype)


def halve_kernel(*refs):
    parts, (own_ref, other_ref) = refs[:-2], refs[-2:]
    pool = lax.axis_index("pool")
    columns = own_ref.shape[1]
    for out, to in ((own_ref, pool), (other_ref, 1 - pool)):
        at = pl.ds(pl.multiple_of(to * columns, LANES), columns)
        out[...] = functools.reduce(
            jnp.add, [part[:, at].astype(F32) for part in parts]
        ).astype(BF16)


def spread_kernel(own_ref, other_ref, order_ref, *outs):
    pool = lax.axis_index("pool")
    own, other = own_ref[...].astype(F32), other_ref[...].astype(F32)
    both = jnp.concatenate([jnp.where(pool == 0, own, other), jnp.where(pool == 0, other, own)], axis=0)
    both = both.astype(BF16)
    columns = both.shape[1] // 2
    value = dot(order_ref[0], both[:, :columns]) + dot(order_ref[1], both[:, columns:])
    count = value.shape[0] // len(outs)
    for step, out in enumerate(outs):
        out[...] = value[step * count : (step + 1) * count].astype(BF16)


def total_kernel(*refs):
    parts, out_ref = refs[:-1], refs[-1]
    total = functools.reduce(jnp.add, [part[...].astype(F32) for part in parts])
    rows, columns = total.shape[0] // 2, total.shape[1]
    out_ref[:, :columns] = total[:rows].astype(BF16)
    out_ref[:, columns:] = total[rows:].astype(BF16)


def one_hot(rows, count):
    picked = np.asarray(rows)[..., None] == np.arange(count)
    return jnp.asarray(picked.astype(np.float32), BF16)


def shape(*dims, dtype=BF16):
    return jax.ShapeDtypeStruct(dims, dtype)


def local(
    queries,
    new_entries,
    cache_pages,
    page_table,
    cached_length,
    leave_slots,
    arrive_slots,
    residual,
    norm_gain,
    output_weight,
    expert_choice,
    route_weight,
    gate_up,
    down_weight,
):
    pools, heads, planes = lax.axis_size("pool"), lax.axis_size("head"), lax.axis_size("req")
    requests = queries.shape[0]
    slots, page, entry = cache_pages.shape[1:]
    moved = leave_slots.shape[0]
    pages = page_table.shape[2]
    rows_here, width = residual.shape
    part = rows_here // pools
    columns = width // heads
    mixes = 2 * planes + -2 * planes % LANES

    ints = jnp.concatenate(
        [page_table[:, 0, j] for j in range(pages)]
        + [cached_length.reshape(-1), leave_slots, arrive_slots]
    )
    ints = jnp.pad(ints, (0, -ints.shape[0] % LANES)).reshape(1, -1)
    own_cache = cache_pages.reshape(slots * page, entry)
    other_cache = send(own_cache, "pool", 1)
    other_ints = send(ints, "pool", 1)

    gate_up, down_weight = gate_up.reshape(-1, width), down_weight.reshape(-1, width)
    other_up, other_down = send(gate_up, "pool", 1), send(down_weight, "pool", 1)

    rows = requests // pools
    pool_order = [
        [h * rows_here + (here ^ p) * part + i for p in range(pools) for h in range(heads) for i in range(part)]
        for here in range(pools)
    ]
    head_order = [
        [(r * heads + (here ^ h)) * part + i for h in range(heads) for r in range(planes) for i in range(part)]
        for here in range(heads)
    ]
    plane_order = [
        [
            p * planes * part + r * part + i if half == at else -1
            for r in range(planes)
            for at in range(2)
            for p in range(pools)
            for i in range(part)
        ]
        for half in range(2)
    ]
    outside = (
        own_cache,
        queries,
        output_weight,
        one_hot(plane_order, pools * planes * part),
        one_hot(pool_order, requests),
        one_hot(head_order, planes * rows),
    )
    copied = [shape(*array.shape[i // 4 :], dtype=array.dtype) for i, array in enumerate(outside)]
    placed, held_cache, held_queries, held_weight, plane_order, pool_order, head_order = kernel_call(
        functools.partial(place_kernel, (heads, pools, planes, len(outside))),
        [shape(requests, heads * (columns + mixes))] + copied,
        [
            pltpu.with_memory_space_constraint(arg, pltpu.HBM)
            for arg in (residual, expert_choice.T, route_weight.T)
        ],
        [pltpu.SemaphoreType.DMA((len(outside),))],
        outside,
    )
    args = held(
        held_queries,
        new_entries.reshape(-1, entry),
        held_cache,
        other_cache,
        ints,
        other_ints,
        placed,
        pool_order,
        held_weight,
    )
    sizes = (requests, pages, moved, page, heads, pools, entry // 2)
    own, other = kernel_call(
        functools.partial(attend_kernel, sizes),
        [shape(rows, heads * (columns + mixes), dtype=F32), shape(rows, heads * (columns + mixes))],
        args,
    )
    other = send(other, "pool", 1)
    other, other_up, other_down = lax.optimization_barrier((other, other_up, other_down))
    piece = shape(rows, columns + mixes)
    pieces = kernel_call(
        split_kernel,
        [shape(rows, columns + mixes, dtype=F32)] + [piece] * (heads - 1),
        held(own, other),
    )
    hidden = pieces[0]
    for step in reversed(range(1, heads)):
        hidden = hidden + send(pieces[step], "head", step).astype(F32)
    hidden = hidden.astype(BF16)

    arrived = [send(hidden, "req", step) for step in reversed(range(1, planes))] + [hidden]
    plane_blocks, sent = kernel_call(
        stack_kernel,
        [shape(planes, rows, columns + mixes), shape(planes, rows, columns)],
        held(*arrived),
    )
    weights = held(gate_up, other_up, norm_gain.reshape(1, -1))
    total = planes * rows
    sums = [shape(total, 2 * gate_up.shape[0], dtype=F32), shape(total, 1, dtype=F32)]
    *state, route, own = kernel_call(
        functools.partial(project_kernel, 0, planes),
        sums + [shape(total, 1, dtype=F32), shape(total, columns, dtype=F32)],
        held(plane_blocks, *weights, head_order),
    )
    for step in reversed(range(1, heads)):
        state = kernel_call(
            functools.partial(project_kernel, step, planes),
            sums,
            held(send(sent, "head", step), *weights, *state),
        )
    piece = shape(planes * part, width)
    pieces = kernel_call(
        expert_kernel,
        [shape(planes * part, width, dtype=F32)] + [piece] * (heads - 1),
        held(*state, route, own, down_weight, other_down, head_order),
    )
    arrived = [send(pieces[step], "head", step) for step in reversed(range(1, heads))] + [pieces[0]]
    own, other = kernel_call(
        halve_kernel, [shape(planes * part, width // pools)] * 2, held(*arrived)
    )
    other = send(other, "pool", 1)
    piece = shape(2 * rows_here, width // pools // 2)
    pieces = kernel_call(spread_kernel, [piece] * planes, held(own, other, plane_order))
    arrived = [send(pieces[step], "req", step) for step in reversed(range(1, planes))] + [pieces[0]]
    return kernel_call(total_kernel, shape(rows_here, width // pools), held(*arrived))


def solution(mesh):
    return jax.shard_map(
        local,
        mesh=mesh,
        in_specs=(
            P(("group", "req"), "head"),
            P(("group", "req"), None, "head", None),
            P("head", ("group", "req", "pool"), None, None),
            P(("group", "req"), "pool", None),
            P(("group", "req"), "pool"),
            P(("group", "req", "pool")),
            P(("group", "req", "pool")),
            P(("group", "req", "head"), None),
            P(),
            P(("head", "pool"), None),
            P(("group", "req", "head"), None),
            P(("group", "req", "head"), None),
            P(("req", "head"), None, "pool", None),
            P(("req", "head"), "pool", None),
        ),
        out_specs=P(("group", "req", "head"), "pool"),
        check_vma=False,
    )
```

```python
import functools

import jax
import jax.numpy as jnp
import numpy as np
from jax import lax
from jax.experimental import pallas as pl
from jax.experimental.pallas import tpu as pltpu
from jax.sharding import PartitionSpec as P

F32 = jnp.float32
BF16 = jnp.bfloat16
VMEM_LIMIT = 32 * 2**20
LANES = 128


def send(value, axes, step):
    size = lax.axis_size(axes)
    return lax.ppermute(value, axes, [(i, i ^ step) for i in range(size)])


def cross(value, axis, step):
    size, pools = lax.axis_size(axis), lax.axis_size("pool")
    pairs = [
        (i * pools + p, (i ^ step) * pools + (p ^ (step & 1))) for i in range(size) for p in range(pools)
    ]
    return lax.ppermute(value, (axis, "pool"), pairs)


def taken():
    return lax.axis_index("pool") ^ (lax.axis_index("head") & 1) ^ (lax.axis_index("req") & 1)


def dot(a, b, contract=((1,), (0,))):
    return lax.dot_general(a, b, (contract, ((), ())), preferred_element_type=F32)


def kernel_call(body, out_shape, args, scratch=(), outside=()):
    return pl.pallas_call(
        body,
        out_shape=jax.tree.map(lambda out: pltpu.VMEM(out.shape, out.dtype), out_shape),
        in_specs=[pl.BlockSpec(memory_space=pltpu.HBM)] * len(outside)
        + [pl.BlockSpec(memory_space=pltpu.VMEM)] * len(args),
        out_specs=jax.tree.map(lambda _: pl.BlockSpec(memory_space=pltpu.VMEM), out_shape),
        scratch_shapes=list(scratch),
        compiler_params=pltpu.CompilerParams(vmem_limit_bytes=VMEM_LIMIT),
    )(*[pltpu.with_memory_space_constraint(arg, pltpu.HBM) for arg in outside], *args)


def held(*args):
    return [pltpu.with_memory_space_constraint(arg, pltpu.VMEM) for arg in args]


def column(row, start, count):
    lane = lax.broadcasted_iota(jnp.int32, (count, row.shape[1]), 1)
    line = lax.broadcasted_iota(jnp.int32, (count, row.shape[1]), 0)
    return jnp.sum(jnp.where(lane == line + start, row, 0.0), axis=1, keepdims=True)


def place_kernel(sizes, *refs):
    heads, pools, planes, count = sizes
    sources, placed_ref, targets = refs[:count], refs[count], refs[count + 1 : -1]
    residual_ref, choice_ref, route_ref = targets[-3:]
    semaphores = refs[-1]
    head, mine = lax.axis_index("head"), taken()
    first = jnp.where(lax.axis_index("pool") == 0, 1.0, 0.0)
    picked = {count - 5: mine, count - 4: head}
    copies = []
    for i in range(count):
        source = sources[i].at[picked[i]] if i in picked else sources[i]
        copies.append(pltpu.make_async_copy(source, targets[i], semaphores.at[i]))
    for copy in reversed(copies):
        copy.start()
    for copy in copies[-3:]:
        copy.wait()
    rows_here, width = residual_ref.shape
    part = rows_here // pools
    total = heads * rows_here
    line = lax.broadcasted_iota(jnp.int32, (total, rows_here), 0)
    lane = lax.broadcasted_iota(jnp.int32, (total, rows_here), 1)
    own = None
    for p in range(pools):
        inside = line - (p * heads * part + head * part)
        one = (inside >= 0) & (inside < part) & (lane == inside + (mine ^ p) * part)
        own = one if own is None else own | one
    spread = jnp.where(own, first, 0.0)
    mixes = placed_ref.shape[1] - width
    placed = dot(spread.astype(BF16), residual_ref[...])
    target = lax.broadcasted_iota(jnp.int32, (total, mixes), 1)
    mix = jnp.zeros((total, mixes), F32)
    for k in range(choice_ref.shape[0]):
        expert = jnp.sum(spread * choice_ref[k : k + 1, :].astype(F32), axis=1, keepdims=True).astype(jnp.int32)
        weight = jnp.sum(spread * route_ref[k : k + 1, :], axis=1, keepdims=True)
        high = weight.astype(BF16).astype(F32)
        lanes = (expert % heads) * (mixes // heads) + expert // heads
        mix = mix + jnp.where(target == lanes, high, 0.0)
        mix = mix + jnp.where(target == lanes + planes, weight - high, 0.0)
    columns, share = width // heads, mixes // heads
    for h in range(heads):
        start = h * (columns + share)
        placed_ref[:, start : start + columns] = placed[:, h * columns : (h + 1) * columns].astype(BF16)
        placed_ref[:, start + columns : start + columns + share] = mix[
            :, h * share : (h + 1) * share
        ].astype(BF16)
    for copy in copies[:-3]:
        copy.wait()


def attend_kernel(sizes, q_ref, new_ref, own_ref, other_ref, own_ints_ref, other_ints_ref, placed_ref, order_ref, weight_ref, own_out_ref, other_out_ref):
    requests, pages, moved, page, heads, pools, head_dim = sizes
    slots = own_ref.shape[0] // page
    here = lax.axis_index("pool")
    group = q_ref.shape[1] // head_dim // pools
    rows = requests // pools
    width = weight_ref.shape[1]
    columns = width // heads
    mixes = (placed_ref.shape[1] - width) // heads

    ints = [own_ints_ref[...].astype(F32), other_ints_ref[...].astype(F32)]
    live_from, live_count = [], []
    for q in range(2):
        row, across = ints[q], ints[1 - q]
        base = pages * requests
        length = column(row, base, requests)
        for j in range(pages):
            slot = column(row, j * requests, requests)
            source = slot + float(q * slots)
            for k in range(moved):
                leave = column(across, base + requests + k, 1)
                arrive = column(row, base + requests + moved + k, 1)
                source = jnp.where(slot == arrive, leave + float((1 - q) * slots), source)
            live_from.append((source * float(page)).astype(jnp.int32))
            live_count.append(jnp.clip(length - float(j * page), 0.0, float(page)).astype(jnp.int32))

    def cache_mask(offset, count):
        entry = lax.broadcasted_iota(jnp.int32, (requests, count), 1) + offset
        mask = None
        for start, amount in zip(live_from, live_count):
            apart = entry - start
            one = (apart >= 0) & (apart < amount)
            mask = one if mask is None else mask | one
        return mask

    count = own_ref.shape[0]
    fresh = new_ref.shape[0] // requests
    entry = lax.broadcasted_iota(jnp.int32, (requests, new_ref.shape[0]), 1)
    first = lax.broadcasted_iota(jnp.int32, (requests, new_ref.shape[0]), 0) * fresh
    masks = [cache_mask(0, count), cache_mask(count, count), (entry >= first) & (entry < first + fresh)]
    queries = jnp.concatenate(
        [
            q_ref[:, pl.ds(pl.multiple_of((here * group + g) * head_dim, LANES), head_dim)]
            for g in range(group)
        ],
        axis=0,
    )
    scale = head_dim ** (-0.5)
    scores = []
    for ref, mask in zip((own_ref, other_ref, new_ref), masks):
        score = dot(queries, ref[:, :head_dim], ((1,), (1,))) * scale
        bias = jnp.where(mask, 0.0, -jnp.inf)
        scores.append(score + jnp.concatenate([bias] * group, axis=0))
    largest = functools.reduce(
        jnp.maximum, [jnp.max(score, axis=1, keepdims=True) for score in scores]
    )
    total, value = 0.0, 0.0
    for ref, score in zip((own_ref, other_ref, new_ref), scores):
        weights = jnp.exp(score - largest)
        total = total + jnp.sum(weights, axis=1, keepdims=True)
        value = value + dot(weights.astype(BF16), ref[:, head_dim:])
    value = (value / total).astype(BF16)
    attended = jnp.concatenate(
        [value[g * requests : (g + 1) * requests] for g in range(group)], axis=1
    )
    attended = dot(order_ref[...], attended).astype(BF16)
    partial = dot(attended, weight_ref[...])
    for h in range(heads):
        start = h * (columns + mixes)
        at = slice(start, start + columns)
        part = partial[:, h * columns : (h + 1) * columns] + placed_ref[:, at].astype(F32)
        own_out_ref[:, at] = part[:rows]
        other_out_ref[:, at] = part[rows:].astype(BF16)
        at = slice(start + columns, start + columns + mixes)
        part = placed_ref[:, at].astype(F32)
        own_out_ref[:, at] = part[:rows]
        other_out_ref[:, at] = part[rows:].astype(BF16)


def split_kernel(own_ref, other_ref, *outs):
    head = lax.axis_index("head")
    columns = own_ref.shape[1] // len(outs)
    for step, out in enumerate(outs):
        at = pl.ds(pl.multiple_of((head ^ step) * columns, LANES), columns)
        out[...] = (own_ref[:, at] + other_ref[:, at].astype(F32)).astype(out.dtype)


def sum_kernel(count, *refs):
    total = functools.reduce(jnp.add, [part[...].astype(F32) for part in refs[:count]])
    for out in refs[count:]:
        out[...] = total.astype(BF16)


def stack_kernel(*refs):
    parts, (all_ref, first_ref) = refs[:-2], refs[-2:]
    for step, part in enumerate(reversed(parts)):
        all_ref[step] = part[...]
        first_ref[step] = part[:, : first_ref.shape[2]]


def project_kernel(step, planes, block_ref, own_up_ref, other_up_ref, gain_ref, *refs):
    head = lax.axis_index("head")
    plane_rows = block_ref.shape[1]
    rows = planes * plane_rows
    columns = gain_ref.shape[1] // lax.axis_size("head")
    units = own_up_ref.shape[0] // 2
    at = pl.ds(pl.multiple_of((head ^ step) * columns, LANES), columns)
    block = block_ref[:, :, :columns].astype(F32).reshape(rows, columns)
    scaled = (block * gain_ref[:, at]).astype(BF16)
    weights = jnp.concatenate(
        [own_up_ref[:units, at], other_up_ref[:units, at], own_up_ref[units:, at], other_up_ref[units:, at]],
        axis=0,
    )
    projected = dot(scaled, weights, ((1,), (1,)))
    squares = jnp.sum(block * block, axis=1, keepdims=True)
    if step:
        before_ref, before_squares_ref, projected_ref, squares_ref = refs
        projected_ref[...] = before_ref[...] + projected
        squares_ref[...] = before_squares_ref[...] + squares
        return
    order_ref, _, projected_ref, squares_ref, route_ref, own_ref = refs
    projected_ref[...] = projected
    squares_ref[...] = squares
    plane = lax.axis_index("req")
    mix = block_ref[:, :, columns:].astype(F32)
    mix = mix.reshape(rows, mix.shape[2])
    lane = lax.broadcasted_iota(jnp.int32, mix.shape, 1)
    route_ref[...] = jnp.sum(
        jnp.where((lane == plane) | (lane == plane + planes), mix, 0.0), axis=1, keepdims=True
    )
    line = lax.broadcasted_iota(jnp.int32, (rows, columns), 0)
    own_ref[...] = dot(order_ref[...], jnp.where(line < plane_rows, block, 0.0).astype(BF16))


def expert_kernel(projected_ref, squares_ref, route_ref, own_ref, own_down_ref, other_down_ref, order_ref, *outs):
    heads = len(outs)
    head = lax.axis_index("head")
    rows, columns = own_ref.shape
    units = own_down_ref.shape[0]
    projected = projected_ref[...] * lax.rsqrt(squares_ref[...] / (heads * columns) + 1e-06)
    gate, up = projected[:, : 2 * units], projected[:, 2 * units :]
    activated = (gate / (1.0 + jnp.exp(-gate)) * up * route_ref[...]).astype(BF16)
    activated = dot(order_ref[...], activated).astype(BF16)
    down = jnp.concatenate([own_down_ref[...], other_down_ref[...]], axis=0)
    count = rows // heads
    for h in range(heads):
        at = slice(h * columns, (h + 1) * columns)
        part = dot(activated, down[:, at]) + jnp.where(head == h, own_ref[...], 0.0)
        for step, out in enumerate(outs):
            out[:, at] = part[step * count : (step + 1) * count].astype(out.dtype)


def halve_kernel(*refs):
    parts, (own_ref, other_ref) = refs[:-2], refs[-2:]
    pool = lax.axis_index("pool")
    columns = own_ref.shape[1]
    for out, to in ((own_ref, pool), (other_ref, 1 - pool)):
        at = pl.ds(pl.multiple_of(to * columns, LANES), columns)
        out[...] = functools.reduce(
            jnp.add, [part[:, at].astype(F32) for part in parts]
        ).astype(BF16)


def spread_kernel(own_ref, other_ref, order_ref, *outs):
    mine = taken()
    own, other = own_ref[...].astype(F32), other_ref[...].astype(F32)
    both = jnp.concatenate([jnp.where(mine == 0, own, other), jnp.where(mine == 0, other, own)], axis=0)
    both = both.astype(BF16)
    columns = both.shape[1] // 2
    value = dot(order_ref[0], both[:, :columns]) + dot(order_ref[1], both[:, columns:])
    count = value.shape[0] // len(outs)
    for step, out in enumerate(outs):
        out[...] = value[step * count : (step + 1) * count].astype(BF16)


def total_kernel(*refs):
    parts, out_ref = refs[:-1], refs[-1]
    total = functools.reduce(jnp.add, [part[...].astype(F32) for part in parts])
    rows, columns = total.shape[0] // 2, total.shape[1]
    out_ref[:, :columns] = total[:rows].astype(BF16)
    out_ref[:, columns:] = total[rows:].astype(BF16)


def one_hot(rows, count):
    picked = np.asarray(rows)[..., None] == np.arange(count)
    return jnp.asarray(picked.astype(np.float32), BF16)


def shape(*dims, dtype=BF16):
    return jax.ShapeDtypeStruct(dims, dtype)


def local(
    queries,
    new_entries,
    cache_pages,
    page_table,
    cached_length,
    leave_slots,
    arrive_slots,
    residual,
    norm_gain,
    output_weight,
    expert_choice,
    route_weight,
    gate_up,
    down_weight,
):
    pools, heads, planes = lax.axis_size("pool"), lax.axis_size("head"), lax.axis_size("req")
    requests = queries.shape[0]
    slots, page, entry = cache_pages.shape[1:]
    moved = leave_slots.shape[0]
    pages = page_table.shape[2]
    rows_here, width = residual.shape
    part = rows_here // pools
    columns = width // heads
    mixes = 2 * planes + -2 * planes % LANES

    ints = jnp.concatenate(
        [page_table[:, 0, j] for j in range(pages)]
        + [cached_length.reshape(-1), leave_slots, arrive_slots]
    )
    ints = jnp.pad(ints, (0, -ints.shape[0] % LANES)).reshape(1, -1)
    own_cache = cache_pages.reshape(slots * page, entry)
    other_cache = send(own_cache, "pool", 1)
    other_ints = send(ints, "pool", 1)

    gate_up, down_weight = gate_up.reshape(-1, width), down_weight.reshape(-1, width)
    other_up, other_down = send(gate_up, "pool", 1), send(down_weight, "pool", 1)

    rows = requests // pools
    pool_order = [
        [h * rows_here + (here ^ p) * part + i for p in range(pools) for h in range(heads) for i in range(part)]
        for here in range(pools)
    ]
    head_order = [
        [(r * heads + (here ^ h)) * part + i for h in range(heads) for r in range(planes) for i in range(part)]
        for here in range(heads)
    ]
    plane_order = [
        [
            p * planes * part + r * part + i if half == at else -1
            for r in range(planes)
            for at in range(2)
            for p in range(pools)
            for i in range(part)
        ]
        for half in range(2)
    ]
    outside = (
        own_cache,
        queries,
        output_weight,
        one_hot(plane_order, pools * planes * part),
        one_hot(pool_order, requests),
        one_hot(head_order, planes * rows),
        residual,
        expert_choice.T,
        route_weight.T,
    )
    copied = [
        shape(*array.shape[i // 4 :], dtype=array.dtype) for i, array in enumerate(outside[:-3])
    ]
    placed, held_cache, held_queries, held_weight, plane_order, pool_order, head_order = kernel_call(
        functools.partial(place_kernel, (heads, pools, planes, len(outside))),
        [shape(requests, heads * (columns + mixes))] + copied,
        (),
        [pltpu.VMEM(array.shape, array.dtype) for array in outside[-3:]]
        + [pltpu.SemaphoreType.DMA((len(outside),))],
        outside,
    )
    args = held(
        held_queries,
        new_entries.reshape(-1, entry),
        held_cache,
        other_cache,
        ints,
        other_ints,
        placed,
        pool_order,
        held_weight,
    )
    sizes = (requests, pages, moved, page, heads, pools, entry // 2)
    own, other = kernel_call(
        functools.partial(attend_kernel, sizes),
        [shape(rows, heads * (columns + mixes), dtype=F32), shape(rows, heads * (columns + mixes))],
        args,
    )
    other = send(other, "pool", 1)
    other, other_up, other_down = lax.optimization_barrier((other, other_up, other_down))
    piece = shape(rows, columns + mixes)
    pieces = kernel_call(
        split_kernel,
        [shape(rows, columns + mixes, dtype=F32)] + [piece] * (heads - 1),
        held(own, other),
    )
    arrived = [cross(pieces[step], "head", step) for step in reversed(range(1, heads))] + [pieces[0]]
    hidden = kernel_call(
        functools.partial(sum_kernel, heads), [piece] * planes, held(*arrived)
    )

    arrived = [cross(hidden[step], "req", step) for step in reversed(range(1, planes))] + [hidden[0]]
    plane_blocks, sent = kernel_call(
        stack_kernel,
        [shape(planes, rows, columns + mixes), shape(planes, rows, columns)],
        held(*arrived),
    )
    weights = held(gate_up, other_up, norm_gain.reshape(1, -1))
    total = planes * rows
    sums = [shape(total, 2 * gate_up.shape[0], dtype=F32), shape(total, 1, dtype=F32)]
    *state, route, own = kernel_call(
        functools.partial(project_kernel, 0, planes),
        sums + [shape(total, 1, dtype=F32), shape(total, columns, dtype=F32)],
        held(plane_blocks, *weights, head_order, down_weight),
    )
    for step in reversed(range(1, heads)):
        state = kernel_call(
            functools.partial(project_kernel, step, planes),
            sums,
            held(cross(sent, "head", step), *weights, *state),
        )
    piece = shape(planes * part, width)
    pieces = kernel_call(
        expert_kernel,
        [shape(planes * part, width, dtype=F32)] + [piece] * (heads - 1),
        held(*state, route, own, down_weight, other_down, head_order),
    )
    arrived = [cross(pieces[step], "head", step) for step in reversed(range(1, heads))] + [pieces[0]]
    own, other = kernel_call(
        halve_kernel, [shape(planes * part, width // pools)] * 2, held(*arrived)
    )
    other = send(other, "pool", 1)
    piece = shape(2 * rows_here, width // pools // 2)
    pieces = kernel_call(spread_kernel, [piece] * planes, held(own, other, plane_order))
    arrived = [send(pieces[step], "req", step) for step in reversed(range(1, planes))] + [pieces[0]]
    return kernel_call(total_kernel, shape(rows_here, width // pools), held(*arrived))


def solution(mesh):
    return jax.shard_map(
        local,
        mesh=mesh,
        in_specs=(
            P(("group", "req"), "head"),
            P(("group", "req"), None, "head", None),
            P("head", ("group", "req", "pool"), None, None),
            P(("group", "req"), "pool", None),
            P(("group", "req"), "pool"),
            P(("group", "req", "pool")),
            P(("group", "req", "pool")),
            P(("group", "req", "head"), None),
            P(),
            P(("head", "pool"), None),
            P(("group", "req", "head"), None),
            P(("group", "req", "head"), None),
            P(("req", "head"), None, "pool", None),
            P(("req", "head"), "pool", None),
        ),
        out_specs=P(("group", "req", "head"), "pool"),
        check_vma=False,
    )
```

```python
import functools

import jax
import jax.numpy as jnp
import numpy as np
from jax import lax
from jax.experimental import pallas as pl
from jax.experimental.pallas import tpu as pltpu
from jax.sharding import PartitionSpec as P

F32 = jnp.float32
BF16 = jnp.bfloat16
VMEM_LIMIT = 32 * 2**20
LANES = 128


def send(value, axes, step):
    size = lax.axis_size(axes)
    return lax.ppermute(value, axes, [(i, i ^ step) for i in range(size)])


def dot(a, b, contract=((1,), (0,))):
    return lax.dot_general(a, b, (contract, ((), ())), preferred_element_type=F32)


def kernel_call(body, out_shape, args, scratch=(), outside=()):
    return pl.pallas_call(
        body,
        out_shape=jax.tree.map(lambda out: pltpu.VMEM(out.shape, out.dtype), out_shape),
        in_specs=[pl.BlockSpec(memory_space=pltpu.HBM)] * len(outside)
        + [pl.BlockSpec(memory_space=pltpu.VMEM)] * len(args),
        out_specs=jax.tree.map(lambda _: pl.BlockSpec(memory_space=pltpu.VMEM), out_shape),
        scratch_shapes=list(scratch),
        compiler_params=pltpu.CompilerParams(vmem_limit_bytes=VMEM_LIMIT),
    )(*[pltpu.with_memory_space_constraint(arg, pltpu.HBM) for arg in outside], *args)


def held(*args):
    return [pltpu.with_memory_space_constraint(arg, pltpu.VMEM) for arg in args]


def column(row, start, count):
    lane = lax.broadcasted_iota(jnp.int32, (count, row.shape[1]), 1)
    line = lax.broadcasted_iota(jnp.int32, (count, row.shape[1]), 0)
    return jnp.sum(jnp.where(lane == line + start, row, 0.0), axis=1, keepdims=True)


def place_kernel(sizes, *refs):
    heads, pools, planes, count = sizes
    sources, (placed_ref, tables_ref), targets = refs[:count], refs[count : count + 2], refs[count + 2 : -1]
    small = targets[6:]
    residual_ref, choice_ref, route_ref = small[:3]
    semaphores = refs[-1]
    head, mine = lax.axis_index("head"), lax.axis_index("pool")
    first = jnp.where(mine == 0, 1.0, 0.0)
    picked = {4: mine, 5: head}
    copies = []
    for i in range(count):
        source = sources[i].at[picked[i]] if i in picked else sources[i]
        copies.append(pltpu.make_async_copy(source, targets[i], semaphores.at[i]))
    for copy in reversed(copies):
        copy.start()
    for copy in copies[6:]:
        copy.wait()
    tables_ref[...] = jnp.zeros_like(tables_ref)
    line = 0
    for ref in small[3:]:
        tables_ref[line : line + ref.shape[0], : ref.shape[1]] = ref[...]
        line += ref.shape[0]
    rows_here, width = residual_ref.shape
    part = rows_here // pools
    total = heads * rows_here
    line = lax.broadcasted_iota(jnp.int32, (total, rows_here), 0)
    lane = lax.broadcasted_iota(jnp.int32, (total, rows_here), 1)
    own = None
    for p in range(pools):
        inside = line - (p * heads * part + head * part)
        one = (inside >= 0) & (inside < part) & (lane == inside + (mine ^ p) * part)
        own = one if own is None else own | one
    spread = jnp.where(own, first, 0.0)
    mixes = placed_ref.shape[1] - width
    placed = dot(spread.astype(BF16), residual_ref[...])
    target = lax.broadcasted_iota(jnp.int32, (total, mixes), 1)
    mix = jnp.zeros((total, mixes), F32)
    for k in range(choice_ref.shape[0]):
        expert = jnp.sum(spread * choice_ref[k : k + 1, :].astype(F32), axis=1, keepdims=True).astype(jnp.int32)
        weight = jnp.sum(spread * route_ref[k : k + 1, :], axis=1, keepdims=True)
        high = weight.astype(BF16).astype(F32)
        lanes = (expert % heads) * (mixes // heads) + expert // heads
        mix = mix + jnp.where(target == lanes, high, 0.0)
        mix = mix + jnp.where(target == lanes + planes, weight - high, 0.0)
    columns, share = width // heads, mixes // heads
    for h in range(heads):
        start = h * (columns + share)
        placed_ref[:, start : start + columns] = placed[:, h * columns : (h + 1) * columns].astype(BF16)
        placed_ref[:, start + columns : start + columns + share] = mix[
            :, h * share : (h + 1) * share
        ].astype(BF16)
    for copy in copies[:6]:
        copy.wait()


def attend_kernel(sizes, q_ref, new_ref, own_ref, other_ref, own_ints_ref, other_ints_ref, placed_ref, order_ref, weight_ref, own_out_ref, other_out_ref):
    requests, pages, moved, page, heads, pools, head_dim = sizes
    slots = own_ref.shape[0] // page
    here = lax.axis_index("pool")
    group = q_ref.shape[1] // head_dim // pools
    rows = requests // pools
    width = weight_ref.shape[1]
    columns = width // heads
    mixes = (placed_ref.shape[1] - width) // heads

    ints = [own_ints_ref[...].astype(F32), other_ints_ref[...].astype(F32)]
    live_from, live_count = [], []
    for q in range(2):
        row, across = ints[q], ints[1 - q]
        length = column(row[pages : pages + 1], 0, requests)
        for j in range(pages):
            slot = column(row[j : j + 1], 0, requests)
            source = slot + float(q * slots)
            for k in range(moved):
                leave = column(across[pages + 1 : pages + 2], k, 1)
                arrive = column(row[pages + 2 : pages + 3], k, 1)
                source = jnp.where(slot == arrive, leave + float((1 - q) * slots), source)
            live_from.append((source * float(page)).astype(jnp.int32))
            live_count.append(jnp.clip(length - float(j * page), 0.0, float(page)).astype(jnp.int32))

    def cache_mask(offset, count):
        entry = lax.broadcasted_iota(jnp.int32, (requests, count), 1) + offset
        mask = None
        for start, amount in zip(live_from, live_count):
            apart = entry - start
            one = (apart >= 0) & (apart < amount)
            mask = one if mask is None else mask | one
        return mask

    count = own_ref.shape[0]
    fresh = new_ref.shape[0] // requests
    entry = lax.broadcasted_iota(jnp.int32, (requests, new_ref.shape[0]), 1)
    first = lax.broadcasted_iota(jnp.int32, (requests, new_ref.shape[0]), 0) * fresh
    masks = [cache_mask(0, count), cache_mask(count, count), (entry >= first) & (entry < first + fresh)]
    queries = jnp.concatenate(
        [
            q_ref[:, pl.ds(pl.multiple_of((here * group + g) * head_dim, LANES), head_dim)]
            for g in range(group)
        ],
        axis=0,
    )
    scale = head_dim ** (-0.5)
    scores = []
    for ref, mask in zip((own_ref, other_ref, new_ref), masks):
        score = dot(queries, ref[:, :head_dim], ((1,), (1,))) * scale
        bias = jnp.where(mask, 0.0, -jnp.inf)
        scores.append(score + jnp.concatenate([bias] * group, axis=0))
    largest = functools.reduce(
        jnp.maximum, [jnp.max(score, axis=1, keepdims=True) for score in scores]
    )
    total, value = 0.0, 0.0
    for ref, score in zip((own_ref, other_ref, new_ref), scores):
        weights = jnp.exp(score - largest)
        total = total + jnp.sum(weights, axis=1, keepdims=True)
        value = value + dot(weights.astype(BF16), ref[:, head_dim:])
    value = (value / total).astype(BF16)
    attended = jnp.concatenate(
        [value[g * requests : (g + 1) * requests] for g in range(group)], axis=1
    )
    attended = dot(order_ref[...], attended).astype(BF16)
    partial = dot(attended, weight_ref[...])
    for h in range(heads):
        start = h * (columns + mixes)
        at = slice(start, start + columns)
        part = partial[:, h * columns : (h + 1) * columns] + placed_ref[:, at].astype(F32)
        own_out_ref[:, at] = part[:rows]
        other_out_ref[:, at] = part[rows:].astype(BF16)
        at = slice(start + columns, start + columns + mixes)
        part = placed_ref[:, at].astype(F32)
        own_out_ref[:, at] = part[:rows]
        other_out_ref[:, at] = part[rows:].astype(BF16)


def split_kernel(own_ref, other_ref, *outs):
    head = lax.axis_index("head")
    columns = own_ref.shape[1] // len(outs)
    for step, out in enumerate(outs):
        at = pl.ds(pl.multiple_of((head ^ step) * columns, LANES), columns)
        out[...] = (own_ref[:, at] + other_ref[:, at].astype(F32)).astype(out.dtype)


def add_kernel(total_ref, part_ref, out_ref):
    out_ref[...] = total_ref[...] + part_ref[...].astype(F32)


def mark_kernel(part_ref, *refs):
    out_ref = refs[-1]
    out_ref[...] = part_ref[: out_ref.shape[0], : out_ref.shape[1]]


def sum_kernel(count, *refs):
    total = functools.reduce(jnp.add, [part[...].astype(F32) for part in refs[:count]])
    for out in refs[count:]:
        out[...] = total.astype(BF16)


def stack_kernel(*refs):
    parts, (all_ref, first_ref) = refs[1:-2], refs[-2:]
    for step, part in enumerate(reversed(parts)):
        all_ref[step] = part[...]
        first_ref[step] = part[:, : first_ref.shape[2]]


def project_kernel(step, planes, block_ref, own_up_ref, other_up_ref, gain_ref, *refs):
    head = lax.axis_index("head")
    plane_rows = block_ref.shape[1]
    rows = planes * plane_rows
    columns = gain_ref.shape[1] // lax.axis_size("head")
    units = own_up_ref.shape[0] // 2
    at = pl.ds(pl.multiple_of((head ^ step) * columns, LANES), columns)
    block = block_ref[:, :, :columns].astype(F32).reshape(rows, columns)
    scaled = (block * gain_ref[:, at]).astype(BF16)
    weights = jnp.concatenate(
        [own_up_ref[:units, at], other_up_ref[:units, at], own_up_ref[units:, at], other_up_ref[units:, at]],
        axis=0,
    )
    projected = dot(scaled, weights, ((1,), (1,)))
    squares = jnp.sum(block * block, axis=1, keepdims=True)
    if step:
        before_ref, before_squares_ref, projected_ref, squares_ref = refs
        projected_ref[...] = before_ref[...] + projected
        squares_ref[...] = before_squares_ref[...] + squares
        return
    order_ref, _, projected_ref, squares_ref, route_ref, own_ref = refs
    projected_ref[...] = projected
    squares_ref[...] = squares
    plane = lax.axis_index("req")
    mix = block_ref[:, :, columns:].astype(F32)
    mix = mix.reshape(rows, mix.shape[2])
    lane = lax.broadcasted_iota(jnp.int32, mix.shape, 1)
    route_ref[...] = jnp.sum(
        jnp.where((lane == plane) | (lane == plane + planes), mix, 0.0), axis=1, keepdims=True
    )
    line = lax.broadcasted_iota(jnp.int32, (rows, columns), 0)
    own_ref[...] = dot(order_ref[...], jnp.where(line < plane_rows, block, 0.0).astype(BF16))


def expert_kernel(projected_ref, squares_ref, route_ref, own_ref, own_down_ref, other_down_ref, order_ref, *outs):
    heads = len(outs)
    head = lax.axis_index("head")
    rows, columns = own_ref.shape
    units = own_down_ref.shape[0]
    projected = projected_ref[...] * lax.rsqrt(squares_ref[...] / (heads * columns) + 1e-06)
    gate, up = projected[:, : 2 * units], projected[:, 2 * units :]
    activated = (gate / (1.0 + jnp.exp(-gate)) * up * route_ref[...]).astype(BF16)
    activated = dot(order_ref[...], activated).astype(BF16)
    down = jnp.concatenate([own_down_ref[...], other_down_ref[...]], axis=0)
    count = rows // heads
    for h in range(heads):
        at = slice(h * columns, (h + 1) * columns)
        part = dot(activated, down[:, at]) + jnp.where(head == h, own_ref[...], 0.0)
        for step, out in enumerate(outs):
            out[:, at] = part[step * count : (step + 1) * count].astype(out.dtype)


def halve_kernel(*refs):
    parts, (own_ref, other_ref) = refs[:-2], refs[-2:]
    pool = lax.axis_index("pool")
    columns = own_ref.shape[1]
    for out, to in ((own_ref, pool), (other_ref, 1 - pool)):
        at = pl.ds(pl.multiple_of(to * columns, LANES), columns)
        out[...] = functools.reduce(
            jnp.add, [part[:, at].astype(F32) for part in parts]
        ).astype(BF16)


def spread_kernel(own_ref, other_ref, order_ref, *outs):
    mine = lax.axis_index("pool")
    own, other = own_ref[...].astype(F32), other_ref[...].astype(F32)
    both = jnp.concatenate([jnp.where(mine == 0, own, other), jnp.where(mine == 0, other, own)], axis=0)
    both = both.astype(BF16)
    columns = both.shape[1] // 2
    value = dot(order_ref[0], both[:, :columns]) + dot(order_ref[1], both[:, columns:])
    count = value.shape[0] // len(outs)
    for step, out in enumerate(outs):
        out[...] = value[step * count : (step + 1) * count].astype(BF16)


def total_kernel(*refs):
    parts, out_ref = refs[:-1], refs[-1]
    total = functools.reduce(jnp.add, [part[...].astype(F32) for part in parts])
    rows, columns = total.shape[0] // 2, total.shape[1]
    out_ref[:, :columns] = total[:rows].astype(BF16)
    out_ref[:, columns:] = total[rows:].astype(BF16)


def one_hot(rows, count):
    picked = np.asarray(rows)[..., None] == np.arange(count)
    return jnp.asarray(picked.astype(np.float32), BF16)


def shape(*dims, dtype=BF16):
    return jax.ShapeDtypeStruct(dims, dtype)


def local(
    queries,
    new_entries,
    cache_pages,
    page_table,
    cached_length,
    leave_slots,
    arrive_slots,
    residual,
    norm_gain,
    output_weight,
    expert_choice,
    route_weight,
    gate_up,
    down_weight,
):
    pools, heads, planes = lax.axis_size("pool"), lax.axis_size("head"), lax.axis_size("req")
    requests = queries.shape[0]
    slots, page, entry = cache_pages.shape[1:]
    moved = leave_slots.shape[0]
    pages = page_table.shape[2]
    rows_here, width = residual.shape
    part = rows_here // pools
    columns = width // heads
    mixes = 2 * planes + -2 * planes % LANES

    own_cache = cache_pages.reshape(slots * page, entry)
    other_cache = send(own_cache, "pool", 1)

    gate_up, down_weight = gate_up.reshape(-1, width), down_weight.reshape(-1, width)

    rows = requests // pools
    pool_order = [
        [h * rows_here + (here ^ p) * part + i for p in range(pools) for h in range(heads) for i in range(part)]
        for here in range(pools)
    ]
    head_order = [
        [(r * heads + (here ^ h)) * part + i for h in range(heads) for r in range(planes) for i in range(part)]
        for here in range(heads)
    ]
    plane_order = [
        [
            p * planes * part + r * part + i if half == at else -1
            for r in range(planes)
            for at in range(2)
            for p in range(pools)
            for i in range(part)
        ]
        for half in range(2)
    ]
    outside = (
        own_cache,
        queries,
        output_weight,
        one_hot(plane_order, pools * planes * part),
        one_hot(pool_order, requests),
        one_hot(head_order, planes * rows),
        residual,
        expert_choice.T,
        route_weight.T,
        page_table.transpose(1, 2, 0).reshape(pages, requests),
        cached_length.reshape(1, requests),
        leave_slots.reshape(1, moved),
        arrive_slots.reshape(1, moved),
    )
    copied = [
        shape(*array.shape[i // 4 :], dtype=array.dtype) for i, array in enumerate(outside[:6])
    ]
    tables = shape(
        pages + 3 + -(pages + 3) % 8, requests + -requests % LANES, dtype=jnp.int32
    )
    placed, ints, held_cache, held_queries, held_weight, plane_order, pool_order, head_order = kernel_call(
        functools.partial(place_kernel, (heads, pools, planes, len(outside))),
        [shape(requests, heads * (columns + mixes)), tables] + copied,
        (),
        [pltpu.VMEM(array.shape, array.dtype) for array in outside[6:]]
        + [pltpu.SemaphoreType.DMA((len(outside),))],
        outside,
    )
    other_ints = send(ints, "pool", 1)
    args = held(
        held_queries,
        new_entries.reshape(-1, entry),
        held_cache,
        other_cache,
        ints,
        other_ints,
        placed,
        pool_order,
        held_weight,
    )
    sizes = (requests, pages, moved, page, heads, pools, entry // 2)
    own, other = kernel_call(
        functools.partial(attend_kernel, sizes),
        [shape(rows, heads * (columns + mixes), dtype=F32), shape(rows, heads * (columns + mixes))],
        args,
    )
    other = send(other, "pool", 1)
    ready = lax.optimization_barrier((gate_up, down_weight, other))
    other_up, other_down = send(ready[0], "pool", 1), send(ready[1], "pool", 1)
    piece = shape(rows, columns + mixes)
    pieces = kernel_call(
        split_kernel,
        [shape(rows, columns + mixes, dtype=F32)] + [piece] * (heads - 1),
        held(own, other),
    )
    total = pieces[0]
    for step in reversed(range(2, heads)):
        total = kernel_call(
            add_kernel,
            shape(rows, columns + mixes, dtype=F32),
            held(total, send(pieces[step], "head", step)),
        )
    hidden = kernel_call(
        functools.partial(sum_kernel, 2),
        [piece] * planes,
        held(send(pieces[1], "head", 1), total),
    )

    arrived = [send(hidden[step], "req", step) for step in reversed(range(1, planes))] + [hidden[0]]
    marks = []
    for part_arrived in arrived[:-2]:
        marks = [kernel_call(mark_kernel, shape(16, LANES), held(part_arrived, *marks))]
    plane_blocks, sent = kernel_call(
        stack_kernel,
        [shape(planes, rows, columns + mixes), shape(planes, rows, columns)],
        held(*marks, *arrived),
    )
    weights = held(gate_up, other_up, norm_gain.reshape(1, -1))
    total = planes * rows
    sums = [shape(total, 2 * gate_up.shape[0], dtype=F32), shape(total, 1, dtype=F32)]
    *state, route, own = kernel_call(
        functools.partial(project_kernel, 0, planes),
        sums + [shape(total, 1, dtype=F32), shape(total, columns, dtype=F32)],
        held(plane_blocks, *weights, head_order, down_weight),
    )
    for step in reversed(range(1, heads)):
        state = kernel_call(
            functools.partial(project_kernel, step, planes),
            sums,
            held(send(sent, "head", step), *weights, *state),
        )
    piece = shape(planes * part, width)
    pieces = kernel_call(
        expert_kernel,
        [shape(planes * part, width, dtype=F32)] + [piece] * (heads - 1),
        held(*state, route, own, down_weight, other_down, head_order),
    )
    arrived = [send(pieces[step], "head", step) for step in reversed(range(1, heads))] + [pieces[0]]
    own, other = kernel_call(
        halve_kernel, [shape(planes * part, width // pools)] * 2, held(*arrived)
    )
    other = send(other, "pool", 1)
    piece = shape(2 * rows_here, width // pools // 2)
    pieces = kernel_call(spread_kernel, [piece] * planes, held(own, other, plane_order))
    arrived = [send(pieces[step], "req", step) for step in reversed(range(1, planes))] + [pieces[0]]
    return kernel_call(total_kernel, shape(rows_here, width // pools), held(*arrived))


def solution(mesh):
    return jax.shard_map(
        local,
        mesh=mesh,
        in_specs=(
            P(("group", "req"), "head"),
            P(("group", "req"), None, "head", None),
            P("head", ("group", "req", "pool"), None, None),
            P(("group", "req"), "pool", None),
            P(("group", "req"), "pool"),
            P(("group", "req", "pool")),
            P(("group", "req", "pool")),
            P(("group", "req", "head"), None),
            P(),
            P(("head", "pool"), None),
            P(("group", "req", "head"), None),
            P(("group", "req", "head"), None),
            P(("req", "head"), None, "pool", None),
            P(("req", "head"), "pool", None),
        ),
        out_specs=P(("group", "req", "head"), "pool"),
        check_vma=False,
    )
```

```python
import functools

import jax
import jax.numpy as jnp
import numpy as np
from jax import lax
from jax.experimental import pallas as pl
from jax.experimental.pallas import tpu as pltpu
from jax.sharding import PartitionSpec as P

F32 = jnp.float32
BF16 = jnp.bfloat16
VMEM_LIMIT = 32 * 2**20
LANES = 128


def send(value, axes, step):
    size = lax.axis_size(axes)
    return lax.ppermute(value, axes, [(i, i ^ step) for i in range(size)])


def dot(a, b, contract=((1,), (0,))):
    return lax.dot_general(a, b, (contract, ((), ())), preferred_element_type=F32)


def kernel_call(body, out_shape, args, scratch=(), outside=()):
    return pl.pallas_call(
        body,
        out_shape=jax.tree.map(lambda out: pltpu.VMEM(out.shape, out.dtype), out_shape),
        in_specs=[pl.BlockSpec(memory_space=pltpu.HBM)] * len(outside)
        + [pl.BlockSpec(memory_space=pltpu.VMEM)] * len(args),
        out_specs=jax.tree.map(lambda _: pl.BlockSpec(memory_space=pltpu.VMEM), out_shape),
        scratch_shapes=list(scratch),
        compiler_params=pltpu.CompilerParams(vmem_limit_bytes=VMEM_LIMIT),
    )(*[pltpu.with_memory_space_constraint(arg, pltpu.HBM) for arg in outside], *args)


def held(*args):
    return [pltpu.with_memory_space_constraint(arg, pltpu.VMEM) for arg in args]


def column(row, start, count):
    lane = lax.broadcasted_iota(jnp.int32, (count, row.shape[1]), 1)
    line = lax.broadcasted_iota(jnp.int32, (count, row.shape[1]), 0)
    return jnp.sum(jnp.where(lane == line + start, row, 0.0), axis=1, keepdims=True)


def place_kernel(sizes, *refs):
    heads, pools, planes, count = sizes
    sources, placed_ref, targets = refs[:count], refs[count], refs[count + 1 : -1]
    residual_ref, choice_ref, route_ref = targets[6:]
    semaphores = refs[-1]
    head, mine = lax.axis_index("head"), lax.axis_index("pool")
    first = jnp.where(mine == 0, 1.0, 0.0)
    picked = {4: mine, 5: head}
    copies = []
    for i in range(count):
        source = sources[i].at[picked[i]] if i in picked else sources[i]
        copies.append(pltpu.make_async_copy(source, targets[i], semaphores.at[i]))
    for copy in reversed(copies):
        copy.start()
    for copy in copies[6:]:
        copy.wait()
    rows_here, width = residual_ref.shape
    part = rows_here // pools
    total = heads * rows_here
    line = lax.broadcasted_iota(jnp.int32, (total, rows_here), 0)
    lane = lax.broadcasted_iota(jnp.int32, (total, rows_here), 1)
    own = None
    for p in range(pools):
        inside = line - (p * heads * part + head * part)
        one = (inside >= 0) & (inside < part) & (lane == inside + (mine ^ p) * part)
        own = one if own is None else own | one
    spread = jnp.where(own, first, 0.0)
    mixes = placed_ref.shape[1] - width
    placed = dot(spread.astype(BF16), residual_ref[...])
    target = lax.broadcasted_iota(jnp.int32, (total, mixes), 1)
    mix = jnp.zeros((total, mixes), F32)
    for k in range(choice_ref.shape[0]):
        expert = jnp.sum(spread * choice_ref[k : k + 1, :].astype(F32), axis=1, keepdims=True).astype(jnp.int32)
        weight = jnp.sum(spread * route_ref[k : k + 1, :], axis=1, keepdims=True)
        high = weight.astype(BF16).astype(F32)
        lanes = (expert % heads) * (mixes // heads) + expert // heads
        mix = mix + jnp.where(target == lanes, high, 0.0)
        mix = mix + jnp.where(target == lanes + planes, weight - high, 0.0)
    columns, share = width // heads, mixes // heads
    for h in range(heads):
        start = h * (columns + share)
        placed_ref[:, start : start + columns] = placed[:, h * columns : (h + 1) * columns].astype(BF16)
        placed_ref[:, start + columns : start + columns + share] = mix[
            :, h * share : (h + 1) * share
        ].astype(BF16)
    for copy in copies[:6]:
        copy.wait()


def attend_kernel(sizes, q_ref, new_ref, own_ref, other_ref, own_ints_ref, other_ints_ref, placed_ref, order_ref, weight_ref, own_out_ref, other_out_ref):
    requests, pages, moved, page, heads, pools, head_dim = sizes
    slots = own_ref.shape[0] // page
    here = lax.axis_index("pool")
    group = q_ref.shape[1] // head_dim // pools
    rows = requests // pools
    width = weight_ref.shape[1]
    columns = width // heads
    mixes = (placed_ref.shape[1] - width) // heads

    ints = [own_ints_ref[...].astype(F32), other_ints_ref[...].astype(F32)]
    live_from, live_count = [], []
    for q in range(2):
        row, across = ints[q], ints[1 - q]
        base = pages * requests
        length = column(row, base, requests)
        for j in range(pages):
            slot = column(row, j * requests, requests)
            source = slot + float(q * slots)
            for k in range(moved):
                leave = column(across, base + requests + k, 1)
                arrive = column(row, base + requests + moved + k, 1)
                source = jnp.where(slot == arrive, leave + float((1 - q) * slots), source)
            live_from.append((source * float(page)).astype(jnp.int32))
            live_count.append(jnp.clip(length - float(j * page), 0.0, float(page)).astype(jnp.int32))

    def cache_mask(offset, count):
        entry = lax.broadcasted_iota(jnp.int32, (requests, count), 1) + offset
        mask = None
        for start, amount in zip(live_from, live_count):
            apart = entry - start
            one = (apart >= 0) & (apart < amount)
            mask = one if mask is None else mask | one
        return mask

    count = own_ref.shape[0]
    fresh = new_ref.shape[0] // requests
    entry = lax.broadcasted_iota(jnp.int32, (requests, new_ref.shape[0]), 1)
    first = lax.broadcasted_iota(jnp.int32, (requests, new_ref.shape[0]), 0) * fresh
    masks = [cache_mask(0, count), cache_mask(count, count), (entry >= first) & (entry < first + fresh)]
    queries = jnp.concatenate(
        [
            q_ref[:, pl.ds(pl.multiple_of((here * group + g) * head_dim, LANES), head_dim)]
            for g in range(group)
        ],
        axis=0,
    )
    scale = head_dim ** (-0.5)
    scores = []
    for ref, mask in zip((own_ref, other_ref, new_ref), masks):
        score = dot(queries, ref[:, :head_dim], ((1,), (1,))) * scale
        bias = jnp.where(mask, 0.0, -jnp.inf)
        scores.append(score + jnp.concatenate([bias] * group, axis=0))
    largest = functools.reduce(
        jnp.maximum, [jnp.max(score, axis=1, keepdims=True) for score in scores]
    )
    total, value = 0.0, 0.0
    for ref, score in zip((own_ref, other_ref, new_ref), scores):
        weights = jnp.exp(score - largest)
        total = total + jnp.sum(weights, axis=1, keepdims=True)
        value = value + dot(weights.astype(BF16), ref[:, head_dim:])
    value = (value / total).astype(BF16)
    attended = jnp.concatenate(
        [value[g * requests : (g + 1) * requests] for g in range(group)], axis=1
    )
    attended = dot(order_ref[...], attended).astype(BF16)
    partial = dot(attended, weight_ref[...])
    for h in range(heads):
        start = h * (columns + mixes)
        at = slice(start, start + columns)
        part = partial[:, h * columns : (h + 1) * columns] + placed_ref[:, at].astype(F32)
        own_out_ref[:, at] = part[:rows]
        other_out_ref[:, at] = part[rows:].astype(BF16)
        at = slice(start + columns, start + columns + mixes)
        part = placed_ref[:, at].astype(F32)
        own_out_ref[:, at] = part[:rows]
        other_out_ref[:, at] = part[rows:].astype(BF16)


def split_kernel(own_ref, other_ref, *outs):
    head = lax.axis_index("head")
    columns = own_ref.shape[1] // len(outs)
    for step, out in enumerate(outs):
        at = pl.ds(pl.multiple_of((head ^ step) * columns, LANES), columns)
        out[...] = (own_ref[:, at] + other_ref[:, at].astype(F32)).astype(out.dtype)


def add_kernel(total_ref, part_ref, out_ref):
    out_ref[...] = total_ref[...] + part_ref[...].astype(F32)


def mark_kernel(part_ref, *refs):
    out_ref = refs[-1]
    out_ref[...] = part_ref[: out_ref.shape[0], : out_ref.shape[1]]


def sum_kernel(count, *refs):
    total = functools.reduce(jnp.add, [part[...].astype(F32) for part in refs[:count]])
    for out in refs[count:]:
        out[...] = total.astype(BF16)


def stack_kernel(*refs):
    parts, (all_ref, first_ref) = refs[1:-2], refs[-2:]
    for step, part in enumerate(reversed(parts)):
        all_ref[step] = part[...]
        first_ref[step] = part[:, : first_ref.shape[2]]


def project_kernel(step, planes, block_ref, own_up_ref, other_up_ref, gain_ref, *refs):
    head = lax.axis_index("head")
    plane_rows = block_ref.shape[1]
    rows = planes * plane_rows
    columns = gain_ref.shape[1] // lax.axis_size("head")
    units = own_up_ref.shape[0] // 2
    at = pl.ds(pl.multiple_of((head ^ step) * columns, LANES), columns)
    block = block_ref[:, :, :columns].astype(F32).reshape(rows, columns)
    scaled = (block * gain_ref[:, at]).astype(BF16)
    weights = jnp.concatenate(
        [own_up_ref[:units, at], other_up_ref[:units, at], own_up_ref[units:, at], other_up_ref[units:, at]],
        axis=0,
    )
    projected = dot(scaled, weights, ((1,), (1,)))
    squares = jnp.sum(block * block, axis=1, keepdims=True)
    if step:
        before_ref, before_squares_ref, projected_ref, squares_ref = refs
        projected_ref[...] = before_ref[...] + projected
        squares_ref[...] = before_squares_ref[...] + squares
        return
    order_ref, _, projected_ref, squares_ref, route_ref, own_ref = refs
    projected_ref[...] = projected
    squares_ref[...] = squares
    plane = lax.axis_index("req")
    mix = block_ref[:, :, columns:].astype(F32)
    mix = mix.reshape(rows, mix.shape[2])
    lane = lax.broadcasted_iota(jnp.int32, mix.shape, 1)
    route_ref[...] = jnp.sum(
        jnp.where((lane == plane) | (lane == plane + planes), mix, 0.0), axis=1, keepdims=True
    )
    line = lax.broadcasted_iota(jnp.int32, (rows, columns), 0)
    own_ref[...] = dot(order_ref[...], jnp.where(line < plane_rows, block, 0.0).astype(BF16))


def expert_kernel(projected_ref, squares_ref, route_ref, own_ref, own_down_ref, other_down_ref, order_ref, *outs):
    heads = len(outs)
    head = lax.axis_index("head")
    rows, columns = own_ref.shape
    units = own_down_ref.shape[0]
    projected = projected_ref[...] * lax.rsqrt(squares_ref[...] / (heads * columns) + 1e-06)
    gate, up = projected[:, : 2 * units], projected[:, 2 * units :]
    activated = (gate / (1.0 + jnp.exp(-gate)) * up * route_ref[...]).astype(BF16)
    activated = dot(order_ref[...], activated).astype(BF16)
    down = jnp.concatenate([own_down_ref[...], other_down_ref[...]], axis=0)
    count = rows // heads
    for h in range(heads):
        at = slice(h * columns, (h + 1) * columns)
        part = dot(activated, down[:, at]) + jnp.where(head == h, own_ref[...], 0.0)
        for step, out in enumerate(outs):
            out[:, at] = part[step * count : (step + 1) * count].astype(out.dtype)


def halve_kernel(*refs):
    parts, (own_ref, other_ref) = refs[:-2], refs[-2:]
    pool = lax.axis_index("pool")
    columns = own_ref.shape[1]
    for out, to in ((own_ref, pool), (other_ref, 1 - pool)):
        at = pl.ds(pl.multiple_of(to * columns, LANES), columns)
        out[...] = functools.reduce(
            jnp.add, [part[:, at].astype(F32) for part in parts]
        ).astype(BF16)


def spread_kernel(own_ref, other_ref, order_ref, *outs):
    mine = lax.axis_index("pool")
    own, other = own_ref[...].astype(F32), other_ref[...].astype(F32)
    both = jnp.concatenate([jnp.where(mine == 0, own, other), jnp.where(mine == 0, other, own)], axis=0)
    both = both.astype(BF16)
    columns = both.shape[1] // 2
    value = dot(order_ref[0], both[:, :columns]) + dot(order_ref[1], both[:, columns:])
    count = value.shape[0] // len(outs)
    for step, out in enumerate(outs):
        out[...] = value[step * count : (step + 1) * count].astype(BF16)


def total_kernel(*refs):
    parts, out_ref = refs[:-1], refs[-1]
    total = functools.reduce(jnp.add, [part[...].astype(F32) for part in parts])
    rows, columns = total.shape[0] // 2, total.shape[1]
    out_ref[:, :columns] = total[:rows].astype(BF16)
    out_ref[:, columns:] = total[rows:].astype(BF16)


def one_hot(rows, count):
    picked = np.asarray(rows)[..., None] == np.arange(count)
    return jnp.asarray(picked.astype(np.float32), BF16)


def shape(*dims, dtype=BF16):
    return jax.ShapeDtypeStruct(dims, dtype)


def local(
    queries,
    new_entries,
    cache_pages,
    page_table,
    cached_length,
    leave_slots,
    arrive_slots,
    residual,
    norm_gain,
    output_weight,
    expert_choice,
    route_weight,
    gate_up,
    down_weight,
):
    pools, heads, planes = lax.axis_size("pool"), lax.axis_size("head"), lax.axis_size("req")
    requests = queries.shape[0]
    slots, page, entry = cache_pages.shape[1:]
    moved = leave_slots.shape[0]
    pages = page_table.shape[2]
    rows_here, width = residual.shape
    part = rows_here // pools
    columns = width // heads
    mixes = 2 * planes + -2 * planes % LANES

    own_cache = cache_pages.reshape(slots * page, entry)
    other_cache = send(own_cache, "pool", 1)
    ints = jnp.concatenate(
        [page_table[:, 0, j] for j in range(pages)]
        + [cached_length.reshape(-1), leave_slots, arrive_slots]
    )
    ints = jnp.pad(ints, (0, -ints.shape[0] % LANES)).reshape(1, -1)
    other_ints = send(ints, "pool", 1)

    gate_up, down_weight = gate_up.reshape(-1, width), down_weight.reshape(-1, width)

    rows = requests // pools
    pool_order = [
        [h * rows_here + (here ^ p) * part + i for p in range(pools) for h in range(heads) for i in range(part)]
        for here in range(pools)
    ]
    head_order = [
        [(r * heads + (here ^ h)) * part + i for h in range(heads) for r in range(planes) for i in range(part)]
        for here in range(heads)
    ]
    plane_order = [
        [
            p * planes * part + r * part + i if half == at else -1
            for r in range(planes)
            for at in range(2)
            for p in range(pools)
            for i in range(part)
        ]
        for half in range(2)
    ]
    outside = (
        own_cache,
        queries,
        output_weight,
        one_hot(plane_order, pools * planes * part),
        one_hot(pool_order, requests),
        one_hot(head_order, planes * rows),
        residual,
        expert_choice.T,
        route_weight.T,
    )
    copied = [
        shape(*array.shape[i // 4 :], dtype=array.dtype) for i, array in enumerate(outside[:6])
    ]
    placed, held_cache, held_queries, held_weight, plane_order, pool_order, head_order = kernel_call(
        functools.partial(place_kernel, (heads, pools, planes, len(outside))),
        [shape(requests, heads * (columns + mixes))] + copied,
        (),
        [pltpu.VMEM(array.shape, array.dtype) for array in outside[6:]]
        + [pltpu.SemaphoreType.DMA((len(outside),))],
        outside,
    )
    args = held(
        held_queries,
        new_entries.reshape(-1, entry),
        held_cache,
        other_cache,
        ints,
        other_ints,
        placed,
        pool_order,
        held_weight,
    )
    sizes = (requests, pages, moved, page, heads, pools, entry // 2)
    own, other = kernel_call(
        functools.partial(attend_kernel, sizes),
        [shape(rows, heads * (columns + mixes), dtype=F32), shape(rows, heads * (columns + mixes))],
        args,
    )
    other = send(other, "pool", 1)
    ready = lax.optimization_barrier((gate_up, down_weight, other))
    other_up, other_down = send(ready[0], "pool", 1), send(ready[1], "pool", 1)
    piece = shape(rows, columns + mixes)
    pieces = kernel_call(
        split_kernel,
        [shape(rows, columns + mixes, dtype=F32)] + [piece] * (heads - 1),
        held(own, other),
    )
    total = pieces[0]
    for step in reversed(range(2, heads)):
        total = kernel_call(
            add_kernel,
            shape(rows, columns + mixes, dtype=F32),
            held(total, send(pieces[step], "head", step)),
        )
    hidden = kernel_call(
        functools.partial(sum_kernel, 2),
        [piece] * planes,
        held(send(pieces[1], "head", 1), total),
    )

    arrived = [send(hidden[step], "req", step) for step in reversed(range(1, planes))] + [hidden[0]]
    marks = []
    for part_arrived in arrived[:-2]:
        marks = [kernel_call(mark_kernel, shape(16, LANES), held(part_arrived, *marks))]
    plane_blocks, sent = kernel_call(
        stack_kernel,
        [shape(planes, rows, columns + mixes), shape(planes, rows, columns)],
        held(*marks, *arrived),
    )
    weights = held(gate_up, other_up, norm_gain.reshape(1, -1))
    total = planes * rows
    sums = [shape(total, 2 * gate_up.shape[0], dtype=F32), shape(total, 1, dtype=F32)]
    *state, route, own = kernel_call(
        functools.partial(project_kernel, 0, planes),
        sums + [shape(total, 1, dtype=F32), shape(total, columns, dtype=F32)],
        held(plane_blocks, *weights, head_order, down_weight),
    )
    for step in reversed(range(1, heads)):
        state = kernel_call(
            functools.partial(project_kernel, step, planes),
            sums,
            held(send(sent, "head", step), *weights, *state),
        )
    piece = shape(planes * part, width)
    pieces = kernel_call(
        expert_kernel,
        [shape(planes * part, width, dtype=F32)] + [piece] * (heads - 1),
        held(*state, route, own, down_weight, other_down, head_order),
    )
    arrived = [send(pieces[step], "head", step) for step in reversed(range(1, heads))] + [pieces[0]]
    own, other = kernel_call(
        halve_kernel, [shape(planes * part, width // pools)] * 2, held(*arrived)
    )
    other = send(other, "pool", 1)
    piece = shape(2 * rows_here, width // pools // 2)
    pieces = kernel_call(spread_kernel, [piece] * planes, held(own, other, plane_order))
    arrived = [send(pieces[step], "req", step) for step in reversed(range(1, planes))] + [pieces[0]]
    return kernel_call(total_kernel, shape(rows_here, width // pools), held(*arrived))


def solution(mesh):
    return jax.shard_map(
        local,
        mesh=mesh,
        in_specs=(
            P(("group", "req"), "head"),
            P(("group", "req"), None, "head", None),
            P("head", ("group", "req", "pool"), None, None),
            P(("group", "req"), "pool", None),
            P(("group", "req"), "pool"),
            P(("group", "req", "pool")),
            P(("group", "req", "pool")),
            P(("group", "req", "head"), None),
            P(),
            P(("head", "pool"), None),
            P(("group", "req", "head"), None),
            P(("group", "req", "head"), None),
            P(("req", "head"), None, "pool", None),
            P(("req", "head"), "pool", None),
        ),
        out_specs=P(("group", "req", "head"), "pool"),
        check_vma=False,
    )
```

```python
import functools

import jax
import jax.numpy as jnp
import numpy as np
from jax import lax
from jax.experimental import pallas as pl
from jax.experimental.pallas import tpu as pltpu
from jax.sharding import PartitionSpec as P

F32 = jnp.float32
BF16 = jnp.bfloat16
VMEM_LIMIT = 32 * 2**20
LANES = 128


def send(value, axes, step):
    size = lax.axis_size(axes)
    return lax.ppermute(value, axes, [(i, i ^ step) for i in range(size)])


def dot(a, b, contract=((1,), (0,))):
    return lax.dot_general(a, b, (contract, ((), ())), preferred_element_type=F32)


def kernel_call(body, out_shape, args, scratch=(), outside=()):
    return pl.pallas_call(
        body,
        out_shape=jax.tree.map(lambda out: pltpu.VMEM(out.shape, out.dtype), out_shape),
        in_specs=[pl.BlockSpec(memory_space=pltpu.HBM)] * len(outside)
        + [pl.BlockSpec(memory_space=pltpu.VMEM)] * len(args),
        out_specs=jax.tree.map(lambda _: pl.BlockSpec(memory_space=pltpu.VMEM), out_shape),
        scratch_shapes=list(scratch),
        compiler_params=pltpu.CompilerParams(vmem_limit_bytes=VMEM_LIMIT),
    )(*[pltpu.with_memory_space_constraint(arg, pltpu.HBM) for arg in outside], *args)


def held(*args):
    return [pltpu.with_memory_space_constraint(arg, pltpu.VMEM) for arg in args]


def column(row, start, count):
    lane = lax.broadcasted_iota(jnp.int32, (count, row.shape[1]), 1)
    line = lax.broadcasted_iota(jnp.int32, (count, row.shape[1]), 0)
    return jnp.sum(jnp.where(lane == line + start, row, 0.0), axis=1, keepdims=True)


def place_kernel(sizes, *refs):
    heads, pools, planes, count = sizes
    sources, placed_ref, targets = refs[:count], refs[count], refs[count + 1 : -1]
    residual_ref, choice_ref, route_ref = targets[7:]
    semaphores = refs[-1]
    head, mine = lax.axis_index("head"), lax.axis_index("pool")
    first = jnp.where(mine == 0, 1.0, 0.0)
    picked = {5: mine, 6: head}
    copies = []
    for i in range(count):
        source = sources[i].at[picked[i]] if i in picked else sources[i]
        copies.append(pltpu.make_async_copy(source, targets[i], semaphores.at[i]))
    for copy in reversed(copies):
        copy.start()
    for copy in copies[7:]:
        copy.wait()
    rows_here, width = residual_ref.shape
    part = rows_here // pools
    total = heads * rows_here
    line = lax.broadcasted_iota(jnp.int32, (total, rows_here), 0)
    lane = lax.broadcasted_iota(jnp.int32, (total, rows_here), 1)
    own = None
    for p in range(pools):
        inside = line - (p * heads * part + head * part)
        one = (inside >= 0) & (inside < part) & (lane == inside + (mine ^ p) * part)
        own = one if own is None else own | one
    spread = jnp.where(own, first, 0.0)
    mixes = placed_ref.shape[1] - width
    placed = dot(spread.astype(BF16), residual_ref[...])
    target = lax.broadcasted_iota(jnp.int32, (total, mixes), 1)
    mix = jnp.zeros((total, mixes), F32)
    for k in range(choice_ref.shape[0]):
        expert = jnp.sum(spread * choice_ref[k : k + 1, :].astype(F32), axis=1, keepdims=True).astype(jnp.int32)
        weight = jnp.sum(spread * route_ref[k : k + 1, :], axis=1, keepdims=True)
        high = weight.astype(BF16).astype(F32)
        lanes = (expert % heads) * (mixes // heads) + expert // heads
        mix = mix + jnp.where(target == lanes, high, 0.0)
        mix = mix + jnp.where(target == lanes + planes, weight - high, 0.0)
    columns, share = width // heads, mixes // heads
    for h in range(heads):
        start = h * (columns + share)
        placed_ref[:, start : start + columns] = placed[:, h * columns : (h + 1) * columns].astype(BF16)
        placed_ref[:, start + columns : start + columns + share] = mix[
            :, h * share : (h + 1) * share
        ].astype(BF16)
    for copy in copies[:7]:
        copy.wait()


def attend_kernel(sizes, q_ref, new_ref, own_ref, other_ref, own_ints_ref, other_ints_ref, placed_ref, order_ref, weight_ref, own_out_ref, other_out_ref):
    requests, pages, moved, page, heads, pools, head_dim = sizes
    slots = own_ref.shape[0] // page
    here = lax.axis_index("pool")
    group = q_ref.shape[1] // head_dim // pools
    rows = requests // pools
    width = weight_ref.shape[1]
    columns = width // heads
    mixes = (placed_ref.shape[1] - width) // heads

    ints = [own_ints_ref[...].astype(F32), other_ints_ref[...].astype(F32)]
    live_from, live_count = [], []
    for q in range(2):
        row, across = ints[q], ints[1 - q]
        base = pages * requests
        length = column(row, base, requests)
        for j in range(pages):
            slot = column(row, j * requests, requests)
            source = slot + float(q * slots)
            for k in range(moved):
                leave = column(across, base + requests + k, 1)
                arrive = column(row, base + requests + moved + k, 1)
                source = jnp.where(slot == arrive, leave + float((1 - q) * slots), source)
            live_from.append((source * float(page)).astype(jnp.int32))
            live_count.append(jnp.clip(length - float(j * page), 0.0, float(page)).astype(jnp.int32))

    def cache_mask(offset, count):
        entry = lax.broadcasted_iota(jnp.int32, (requests, count), 1) + offset
        mask = None
        for start, amount in zip(live_from, live_count):
            apart = entry - start
            one = (apart >= 0) & (apart < amount)
            mask = one if mask is None else mask | one
        return mask

    count = own_ref.shape[0]
    fresh = new_ref.shape[1]
    entry = lax.broadcasted_iota(jnp.int32, (requests, requests * fresh), 1)
    first = lax.broadcasted_iota(jnp.int32, (requests, requests * fresh), 0) * fresh
    newest = new_ref[...].astype(F32).reshape(requests * fresh, new_ref.shape[2]).astype(BF16)
    masks = [cache_mask(0, count), cache_mask(count, count), (entry >= first) & (entry < first + fresh)]
    queries = jnp.concatenate(
        [
            q_ref[:, pl.ds(pl.multiple_of((here * group + g) * head_dim, LANES), head_dim)]
            for g in range(group)
        ],
        axis=0,
    )
    scale = head_dim ** (-0.5)
    scores = []
    for ref, mask in zip((own_ref, other_ref, newest), masks):
        score = dot(queries, ref[:, :head_dim], ((1,), (1,))) * scale
        bias = jnp.where(mask, 0.0, -jnp.inf)
        scores.append(score + jnp.concatenate([bias] * group, axis=0))
    largest = functools.reduce(
        jnp.maximum, [jnp.max(score, axis=1, keepdims=True) for score in scores]
    )
    total, value = 0.0, 0.0
    for ref, score in zip((own_ref, other_ref, newest), scores):
        weights = jnp.exp(score - largest)
        total = total + jnp.sum(weights, axis=1, keepdims=True)
        value = value + dot(weights.astype(BF16), ref[:, head_dim:])
    value = (value / total).astype(BF16)
    attended = jnp.concatenate(
        [value[g * requests : (g + 1) * requests] for g in range(group)], axis=1
    )
    attended = dot(order_ref[...], attended).astype(BF16)
    partial = dot(attended, weight_ref[...])
    for h in range(heads):
        start = h * (columns + mixes)
        at = slice(start, start + columns)
        part = partial[:, h * columns : (h + 1) * columns] + placed_ref[:, at].astype(F32)
        own_out_ref[:, at] = part[:rows]
        other_out_ref[:, at] = part[rows:].astype(BF16)
        at = slice(start + columns, start + columns + mixes)
        part = placed_ref[:, at].astype(F32)
        own_out_ref[:, at] = part[:rows]
        other_out_ref[:, at] = part[rows:].astype(BF16)


def split_kernel(own_ref, other_ref, *outs):
    head = lax.axis_index("head")
    columns = own_ref.shape[1] // len(outs)
    for step, out in enumerate(outs):
        at = pl.ds(pl.multiple_of((head ^ step) * columns, LANES), columns)
        out[...] = (own_ref[:, at] + other_ref[:, at].astype(F32)).astype(out.dtype)


def add_kernel(total_ref, part_ref, out_ref):
    out_ref[...] = total_ref[...] + part_ref[...].astype(F32)


def mark_kernel(part_ref, *refs):
    out_ref = refs[-1]
    out_ref[...] = part_ref[: out_ref.shape[0], : out_ref.shape[1]]


def sum_kernel(count, *refs):
    total = functools.reduce(jnp.add, [part[...].astype(F32) for part in refs[:count]])
    for out in refs[count:]:
        out[...] = total.astype(BF16)


def stack_kernel(*refs):
    parts, (all_ref, first_ref) = refs[1:-2], refs[-2:]
    for step, part in enumerate(reversed(parts)):
        all_ref[step] = part[...]
        first_ref[step] = part[:, : first_ref.shape[2]]


def project_kernel(step, planes, block_ref, own_up_ref, other_up_ref, gain_ref, *refs):
    head = lax.axis_index("head")
    plane_rows = block_ref.shape[1]
    rows = planes * plane_rows
    columns = gain_ref.shape[1] // lax.axis_size("head")
    units = own_up_ref.shape[0] // 2
    at = pl.ds(pl.multiple_of((head ^ step) * columns, LANES), columns)
    block = block_ref[:, :, :columns].astype(F32).reshape(rows, columns)
    scaled = (block * gain_ref[:, at]).astype(BF16)
    weights = jnp.concatenate(
        [own_up_ref[:units, at], other_up_ref[:units, at], own_up_ref[units:, at], other_up_ref[units:, at]],
        axis=0,
    )
    projected = dot(scaled, weights, ((1,), (1,)))
    squares = jnp.sum(block * block, axis=1, keepdims=True)
    if step:
        before_ref, before_squares_ref, projected_ref, squares_ref = refs
        projected_ref[...] = before_ref[...] + projected
        squares_ref[...] = before_squares_ref[...] + squares
        return
    order_ref, _, projected_ref, squares_ref, route_ref, own_ref = refs
    projected_ref[...] = projected
    squares_ref[...] = squares
    plane = lax.axis_index("req")
    mix = block_ref[:, :, columns:].astype(F32)
    mix = mix.reshape(rows, mix.shape[2])
    lane = lax.broadcasted_iota(jnp.int32, mix.shape, 1)
    route_ref[...] = jnp.sum(
        jnp.where((lane == plane) | (lane == plane + planes), mix, 0.0), axis=1, keepdims=True
    )
    line = lax.broadcasted_iota(jnp.int32, (rows, columns), 0)
    own_ref[...] = dot(order_ref[...], jnp.where(line < plane_rows, block, 0.0).astype(BF16))


def expert_kernel(projected_ref, squares_ref, route_ref, own_ref, own_down_ref, other_down_ref, order_ref, *outs):
    heads = len(outs)
    head = lax.axis_index("head")
    rows, columns = own_ref.shape
    units = own_down_ref.shape[0]
    projected = projected_ref[...] * lax.rsqrt(squares_ref[...] / (heads * columns) + 1e-06)
    gate, up = projected[:, : 2 * units], projected[:, 2 * units :]
    activated = (gate / (1.0 + jnp.exp(-gate)) * up * route_ref[...]).astype(BF16)
    activated = dot(order_ref[...], activated).astype(BF16)
    down = jnp.concatenate([own_down_ref[...], other_down_ref[...]], axis=0)
    count = rows // heads
    for h in range(heads):
        at = slice(h * columns, (h + 1) * columns)
        part = dot(activated, down[:, at]) + jnp.where(head == h, own_ref[...], 0.0)
        for step, out in enumerate(outs):
            out[:, at] = part[step * count : (step + 1) * count].astype(out.dtype)


def halve_kernel(*refs):
    parts, (own_ref, other_ref) = refs[:-2], refs[-2:]
    pool = lax.axis_index("pool")
    columns = own_ref.shape[1]
    for out, to in ((own_ref, pool), (other_ref, 1 - pool)):
        at = pl.ds(pl.multiple_of(to * columns, LANES), columns)
        out[...] = functools.reduce(
            jnp.add, [part[:, at].astype(F32) for part in parts]
        ).astype(BF16)


def spread_kernel(own_ref, other_ref, order_ref, *outs):
    mine = lax.axis_index("pool")
    own, other = own_ref[...].astype(F32), other_ref[...].astype(F32)
    both = jnp.concatenate([jnp.where(mine == 0, own, other), jnp.where(mine == 0, other, own)], axis=0)
    both = both.astype(BF16)
    columns = both.shape[1] // 2
    value = dot(order_ref[0], both[:, :columns]) + dot(order_ref[1], both[:, columns:])
    count = value.shape[0] // len(outs)
    for step, out in enumerate(outs):
        out[...] = value[step * count : (step + 1) * count].astype(BF16)


def total_kernel(*refs):
    parts, out_ref = refs[:-1], refs[-1]
    total = functools.reduce(jnp.add, [part[...].astype(F32) for part in parts])
    rows, columns = total.shape[0] // 2, total.shape[1]
    out_ref[:, :columns] = total[:rows].astype(BF16)
    out_ref[:, columns:] = total[rows:].astype(BF16)


def one_hot(rows, count):
    picked = np.asarray(rows)[..., None] == np.arange(count)
    return jnp.asarray(picked.astype(np.float32), BF16)


def shape(*dims, dtype=BF16):
    return jax.ShapeDtypeStruct(dims, dtype)


def local(
    queries,
    new_entries,
    cache_pages,
    page_table,
    cached_length,
    leave_slots,
    arrive_slots,
    residual,
    norm_gain,
    output_weight,
    expert_choice,
    route_weight,
    gate_up,
    down_weight,
):
    pools, heads, planes = lax.axis_size("pool"), lax.axis_size("head"), lax.axis_size("req")
    requests = queries.shape[0]
    slots, page, entry = cache_pages.shape[1:]
    moved = leave_slots.shape[0]
    pages = page_table.shape[2]
    rows_here, width = residual.shape
    part = rows_here // pools
    columns = width // heads
    mixes = 2 * planes + -2 * planes % LANES

    own_cache = cache_pages.reshape(slots * page, entry)
    other_cache = send(own_cache, "pool", 1)
    ints = jnp.concatenate(
        [page_table[:, 0, j] for j in range(pages)]
        + [cached_length.reshape(-1), leave_slots, arrive_slots]
    )
    ints = jnp.pad(ints, (0, -ints.shape[0] % LANES)).reshape(1, -1)
    other_ints = send(ints, "pool", 1)

    gate_up, down_weight = gate_up.reshape(-1, width), down_weight.reshape(-1, width)

    rows = requests // pools
    pool_order = [
        [h * rows_here + (here ^ p) * part + i for p in range(pools) for h in range(heads) for i in range(part)]
        for here in range(pools)
    ]
    head_order = [
        [(r * heads + (here ^ h)) * part + i for h in range(heads) for r in range(planes) for i in range(part)]
        for here in range(heads)
    ]
    plane_order = [
        [
            p * planes * part + r * part + i if half == at else -1
            for r in range(planes)
            for at in range(2)
            for p in range(pools)
            for i in range(part)
        ]
        for half in range(2)
    ]
    outside = (
        own_cache,
        queries,
        output_weight,
        new_entries.reshape(requests, -1, entry),
        one_hot(plane_order, pools * planes * part),
        one_hot(pool_order, requests),
        one_hot(head_order, planes * rows),
        residual,
        expert_choice.T,
        route_weight.T,
    )
    copied = [
        shape(*array.shape[i // 5 :], dtype=array.dtype) for i, array in enumerate(outside[:7])
    ]
    placed, held_cache, held_queries, held_weight, held_entries, plane_order, pool_order, head_order = kernel_call(
        functools.partial(place_kernel, (heads, pools, planes, len(outside))),
        [shape(requests, heads * (columns + mixes))] + copied,
        (),
        [pltpu.VMEM(array.shape, array.dtype) for array in outside[7:]]
        + [pltpu.SemaphoreType.DMA((len(outside),))],
        outside,
    )
    args = held(
        held_queries,
        held_entries,
        held_cache,
        other_cache,
        ints,
        other_ints,
        placed,
        pool_order,
        held_weight,
    )
    sizes = (requests, pages, moved, page, heads, pools, entry // 2)
    own, other = kernel_call(
        functools.partial(attend_kernel, sizes),
        [shape(rows, heads * (columns + mixes), dtype=F32), shape(rows, heads * (columns + mixes))],
        args,
    )
    other = send(other, "pool", 1)
    ready = lax.optimization_barrier((gate_up, down_weight, other))
    other_up, other_down = send(ready[0], "pool", 1), send(ready[1], "pool", 1)
    piece = shape(rows, columns + mixes)
    pieces = kernel_call(
        split_kernel,
        [shape(rows, columns + mixes, dtype=F32)] + [piece] * (heads - 1),
        held(own, other),
    )
    total = pieces[0]
    for step in reversed(range(2, heads)):
        total = kernel_call(
            add_kernel,
            shape(rows, columns + mixes, dtype=F32),
            held(total, send(pieces[step], "head", step)),
        )
    hidden = kernel_call(
        functools.partial(sum_kernel, 2),
        [piece] * planes,
        held(send(pieces[1], "head", 1), total),
    )

    arrived = [send(hidden[step], "req", step) for step in reversed(range(1, planes))] + [hidden[0]]
    marks = []
    for part_arrived in arrived[:-2]:
        marks = [kernel_call(mark_kernel, shape(16, LANES), held(part_arrived, *marks))]
    plane_blocks, sent = kernel_call(
        stack_kernel,
        [shape(planes, rows, columns + mixes), shape(planes, rows, columns)],
        held(*marks, *arrived),
    )
    weights = held(gate_up, other_up, norm_gain.reshape(1, -1))
    total = planes * rows
    sums = [shape(total, 2 * gate_up.shape[0], dtype=F32), shape(total, 1, dtype=F32)]
    *state, route, own = kernel_call(
        functools.partial(project_kernel, 0, planes),
        sums + [shape(total, 1, dtype=F32), shape(total, columns, dtype=F32)],
        held(plane_blocks, *weights, head_order, down_weight),
    )
    for step in reversed(range(1, heads)):
        state = kernel_call(
            functools.partial(project_kernel, step, planes),
            sums,
            held(send(sent, "head", step), *weights, *state),
        )
    piece = shape(planes * part, width)
    pieces = kernel_call(
        expert_kernel,
        [shape(planes * part, width, dtype=F32)] + [piece] * (heads - 1),
        held(*state, route, own, down_weight, other_down, head_order),
    )
    arrived = [send(pieces[step], "head", step) for step in reversed(range(1, heads))] + [pieces[0]]
    own, other = kernel_call(
        halve_kernel, [shape(planes * part, width // pools)] * 2, held(*arrived)
    )
    other = send(other, "pool", 1)
    piece = shape(2 * rows_here, width // pools // 2)
    pieces = kernel_call(spread_kernel, [piece] * planes, held(own, other, plane_order))
    arrived = [send(pieces[step], "req", step) for step in reversed(range(1, planes))] + [pieces[0]]
    return kernel_call(total_kernel, shape(rows_here, width // pools), held(*arrived))


def solution(mesh):
    return jax.shard_map(
        local,
        mesh=mesh,
        in_specs=(
            P(("group", "req"), "head"),
            P(("group", "req"), None, "head", None),
            P("head", ("group", "req", "pool"), None, None),
            P(("group", "req"), "pool", None),
            P(("group", "req"), "pool"),
            P(("group", "req", "pool")),
            P(("group", "req", "pool")),
            P(("group", "req", "head"), None),
            P(),
            P(("head", "pool"), None),
            P(("group", "req", "head"), None),
            P(("group", "req", "head"), None),
            P(("req", "head"), None, "pool", None),
            P(("req", "head"), "pool", None),
        ),
        out_specs=P(("group", "req", "head"), "pool"),
        check_vma=False,
    )
```

```python
import functools

import jax
import jax.numpy as jnp
import numpy as np
from jax import lax
from jax.experimental import pallas as pl
from jax.experimental.pallas import tpu as pltpu
from jax.sharding import PartitionSpec as P

F32 = jnp.float32
BF16 = jnp.bfloat16
VMEM_LIMIT = 32 * 2**20
LANES = 128


def send(value, axes, step):
    size = lax.axis_size(axes)
    return lax.ppermute(value, axes, [(i, i ^ step) for i in range(size)])


def give(value, source):
    return lax.ppermute(value, "pool", [(source, 1 - source)])


def send_last(value, axis, step):
    size, pools = lax.axis_size(axis), lax.axis_size("pool")
    pairs = [(i * pools + pools - 1, (i ^ step) * pools + pools - 1) for i in range(size)]
    return lax.ppermute(value, (axis, "pool"), pairs)


def dot(a, b, contract=((1,), (0,))):
    return lax.dot_general(a, b, (contract, ((), ())), preferred_element_type=F32)


def kernel_call(body, out_shape, args, scratch=(), outside=()):
    return pl.pallas_call(
        body,
        out_shape=jax.tree.map(lambda out: pltpu.VMEM(out.shape, out.dtype), out_shape),
        in_specs=[pl.BlockSpec(memory_space=pltpu.HBM)] * len(outside)
        + [pl.BlockSpec(memory_space=pltpu.VMEM)] * len(args),
        out_specs=jax.tree.map(lambda _: pl.BlockSpec(memory_space=pltpu.VMEM), out_shape),
        scratch_shapes=list(scratch),
        compiler_params=pltpu.CompilerParams(vmem_limit_bytes=VMEM_LIMIT),
    )(*[pltpu.with_memory_space_constraint(arg, pltpu.HBM) for arg in outside], *args)


def held(*args):
    return [pltpu.with_memory_space_constraint(arg, pltpu.VMEM) for arg in args]


def column(row, start, count):
    lane = lax.broadcasted_iota(jnp.int32, (count, row.shape[1]), 1)
    line = lax.broadcasted_iota(jnp.int32, (count, row.shape[1]), 0)
    return jnp.sum(jnp.where(lane == line + start, row, 0.0), axis=1, keepdims=True)


def place_kernel(sizes, *refs):
    heads, pools, planes, count = sizes
    sources, placed_ref, targets = refs[:count], refs[count], refs[count + 1 : -1]
    residual_ref, choice_ref, route_ref = targets[7:]
    semaphores = refs[-1]
    head, mine = lax.axis_index("head"), lax.axis_index("pool")
    first = jnp.where(mine == 0, 1.0, 0.0)
    picked = {5: mine, 6: head}
    copies = []
    for i in range(count):
        source = sources[i].at[picked[i]] if i in picked else sources[i]
        copies.append(pltpu.make_async_copy(source, targets[i], semaphores.at[i]))
    for copy in reversed(copies):
        copy.start()
    for copy in copies[7:]:
        copy.wait()
    rows_here, width = residual_ref.shape
    part = rows_here // pools
    total = heads * rows_here
    line = lax.broadcasted_iota(jnp.int32, (total, rows_here), 0)
    lane = lax.broadcasted_iota(jnp.int32, (total, rows_here), 1)
    own = None
    for p in range(pools):
        inside = line - (p * heads * part + head * part)
        one = (inside >= 0) & (inside < part) & (lane == inside + p * part)
        own = one if own is None else own | one
    spread = jnp.where(own, first, 0.0)
    mixes = placed_ref.shape[1] - width
    placed = dot(spread.astype(BF16), residual_ref[...])
    target = lax.broadcasted_iota(jnp.int32, (total, mixes), 1)
    mix = jnp.zeros((total, mixes), F32)
    for k in range(choice_ref.shape[0]):
        expert = jnp.sum(spread * choice_ref[k : k + 1, :].astype(F32), axis=1, keepdims=True).astype(jnp.int32)
        weight = jnp.sum(spread * route_ref[k : k + 1, :], axis=1, keepdims=True)
        high = weight.astype(BF16).astype(F32)
        lanes = (expert % heads) * (mixes // heads) + expert // heads
        mix = mix + jnp.where(target == lanes, high, 0.0)
        mix = mix + jnp.where(target == lanes + planes, weight - high, 0.0)
    columns, share = width // heads, mixes // heads
    for h in range(heads):
        start = h * (columns + share)
        placed_ref[:, start : start + columns] = placed[:, h * columns : (h + 1) * columns].astype(BF16)
        placed_ref[:, start + columns : start + columns + share] = mix[
            :, h * share : (h + 1) * share
        ].astype(BF16)
    for copy in copies[:7]:
        copy.wait()


def attend_kernel(sizes, q_ref, new_ref, own_ref, other_ref, own_ints_ref, other_ints_ref, placed_ref, order_ref, weight_ref, own_out_ref, other_out_ref):
    requests, pages, moved, page, heads, pools, head_dim = sizes
    slots = own_ref.shape[0] // page
    here = lax.axis_index("pool")
    group = q_ref.shape[1] // head_dim // pools
    width = weight_ref.shape[1]
    columns = width // heads
    mixes = (placed_ref.shape[1] - width) // heads

    ints = [own_ints_ref[...].astype(F32), other_ints_ref[...].astype(F32)]
    live_from, live_count = [], []
    for q in range(2):
        row, across = ints[q], ints[1 - q]
        base = pages * requests
        length = column(row, base, requests)
        for j in range(pages):
            slot = column(row, j * requests, requests)
            source = slot + float(q * slots)
            for k in range(moved):
                leave = column(across, base + requests + k, 1)
                arrive = column(row, base + requests + moved + k, 1)
                source = jnp.where(slot == arrive, leave + float((1 - q) * slots), source)
            live_from.append((source * float(page)).astype(jnp.int32))
            live_count.append(jnp.clip(length - float(j * page), 0.0, float(page)).astype(jnp.int32))

    def cache_mask(offset, count):
        entry = lax.broadcasted_iota(jnp.int32, (requests, count), 1) + offset
        mask = None
        for start, amount in zip(live_from, live_count):
            apart = entry - start
            one = (apart >= 0) & (apart < amount)
            mask = one if mask is None else mask | one
        return mask

    count = own_ref.shape[0]
    fresh = new_ref.shape[1]
    entry = lax.broadcasted_iota(jnp.int32, (requests, requests * fresh), 1)
    first = lax.broadcasted_iota(jnp.int32, (requests, requests * fresh), 0) * fresh
    newest = new_ref[...].astype(F32).reshape(requests * fresh, new_ref.shape[2]).astype(BF16)
    masks = [cache_mask(0, count), cache_mask(count, count), (entry >= first) & (entry < first + fresh)]
    queries = jnp.concatenate(
        [
            q_ref[:, pl.ds(pl.multiple_of((here * group + g) * head_dim, LANES), head_dim)]
            for g in range(group)
        ],
        axis=0,
    )
    scale = head_dim ** (-0.5)
    scores = []
    for ref, mask in zip((own_ref, other_ref, newest), masks):
        score = dot(queries, ref[:, :head_dim], ((1,), (1,))) * scale
        bias = jnp.where(mask, 0.0, -jnp.inf)
        scores.append(score + jnp.concatenate([bias] * group, axis=0))
    largest = functools.reduce(
        jnp.maximum, [jnp.max(score, axis=1, keepdims=True) for score in scores]
    )
    total, value = 0.0, 0.0
    for ref, score in zip((own_ref, other_ref, newest), scores):
        weights = jnp.exp(score - largest)
        total = total + jnp.sum(weights, axis=1, keepdims=True)
        value = value + dot(weights.astype(BF16), ref[:, head_dim:])
    value = (value / total).astype(BF16)
    attended = jnp.concatenate(
        [value[g * requests : (g + 1) * requests] for g in range(group)], axis=1
    )
    attended = dot(order_ref[...], attended).astype(BF16)
    partial = dot(attended, weight_ref[...])
    for h in range(heads):
        start = h * (columns + mixes)
        at = slice(start, start + columns)
        part = partial[:, h * columns : (h + 1) * columns] + placed_ref[:, at].astype(F32)
        own_out_ref[:, at] = part
        other_out_ref[:, at] = part.astype(BF16)
        at = slice(start + columns, start + columns + mixes)
        part = placed_ref[:, at].astype(F32)
        own_out_ref[:, at] = part
        other_out_ref[:, at] = part.astype(BF16)


def split_kernel(own_ref, other_ref, *outs):
    head = lax.axis_index("head")
    columns = own_ref.shape[1] // len(outs)
    for step, out in enumerate(outs):
        at = pl.ds(pl.multiple_of((head ^ step) * columns, LANES), columns)
        out[...] = (own_ref[:, at] + other_ref[:, at].astype(F32)).astype(out.dtype)


def add_kernel(total_ref, part_ref, out_ref):
    out_ref[...] = total_ref[...] + part_ref[...].astype(F32)


def mark_kernel(part_ref, *refs):
    out_ref = refs[-1]
    out_ref[...] = part_ref[: out_ref.shape[0], : out_ref.shape[1]]


def sum_kernel(count, *refs):
    total = functools.reduce(jnp.add, [part[...].astype(F32) for part in refs[:count]])
    for out in refs[count:]:
        out[...] = total.astype(BF16)


def stack_kernel(*refs):
    parts, (mine_ref, other_ref) = refs[1:-2], refs[-2:]
    rows = mine_ref.shape[1]
    for step, part in enumerate(reversed(parts)):
        block = part[...].astype(F32)
        other_ref[step] = block[:rows].astype(BF16)
        mine_ref[step] = block[rows:].astype(BF16)


def choose_kernel(mine_ref, given_ref, all_ref, first_ref):
    last = lax.axis_index("pool") == 1
    block = jnp.where(last, mine_ref[...].astype(F32), given_ref[...].astype(F32)).astype(BF16)
    all_ref[...] = block
    first_ref[...] = block[:, :, : first_ref.shape[2]]


def project_kernel(step, planes, block_ref, own_up_ref, other_up_ref, gain_ref, *refs):
    head = lax.axis_index("head")
    plane_rows = block_ref.shape[1]
    rows = planes * plane_rows
    columns = gain_ref.shape[1] // lax.axis_size("head")
    units = own_up_ref.shape[0] // 2
    at = pl.ds(pl.multiple_of((head ^ step) * columns, LANES), columns)
    block = block_ref[:, :, :columns].astype(F32).reshape(rows, columns)
    scaled = (block * gain_ref[:, at]).astype(BF16)
    weights = jnp.concatenate(
        [own_up_ref[:units, at], other_up_ref[:units, at], own_up_ref[units:, at], other_up_ref[units:, at]],
        axis=0,
    )
    projected = dot(scaled, weights, ((1,), (1,)))
    squares = jnp.sum(block * block, axis=1, keepdims=True)
    if step:
        before_ref, before_squares_ref, projected_ref, squares_ref = refs
        projected_ref[...] = before_ref[...] + projected
        squares_ref[...] = before_squares_ref[...] + squares
        return
    order_ref, _, projected_ref, squares_ref, route_ref, own_ref = refs
    projected_ref[...] = projected
    squares_ref[...] = squares
    plane = lax.axis_index("req")
    mix = block_ref[:, :, columns:].astype(F32)
    mix = mix.reshape(rows, mix.shape[2])
    lane = lax.broadcasted_iota(jnp.int32, mix.shape, 1)
    route_ref[...] = jnp.sum(
        jnp.where((lane == plane) | (lane == plane + planes), mix, 0.0), axis=1, keepdims=True
    )
    line = lax.broadcasted_iota(jnp.int32, (rows, columns), 0)
    own_ref[...] = dot(order_ref[...], jnp.where(line < plane_rows, block, 0.0).astype(BF16))


def expert_kernel(projected_ref, squares_ref, route_ref, own_ref, own_down_ref, other_down_ref, order_ref, *outs):
    heads = len(outs)
    head = lax.axis_index("head")
    rows, columns = own_ref.shape
    units = own_down_ref.shape[0]
    projected = projected_ref[...] * lax.rsqrt(squares_ref[...] / (heads * columns) + 1e-06)
    gate, up = projected[:, : 2 * units], projected[:, 2 * units :]
    activated = (gate / (1.0 + jnp.exp(-gate)) * up * route_ref[...]).astype(BF16)
    activated = dot(order_ref[...], activated).astype(BF16)
    down = jnp.concatenate([own_down_ref[...], other_down_ref[...]], axis=0)
    count = rows // heads
    for h in range(heads):
        at = slice(h * columns, (h + 1) * columns)
        part = dot(activated, down[:, at]) + jnp.where(head == h, own_ref[...], 0.0)
        for step, out in enumerate(outs):
            out[:, at] = part[step * count : (step + 1) * count].astype(out.dtype)


def halve_kernel(*refs):
    parts, (own_ref, other_ref) = refs[:-2], refs[-2:]
    pool = lax.axis_index("pool")
    columns = own_ref.shape[1]
    for out, to in ((own_ref, pool), (other_ref, 1 - pool)):
        at = pl.ds(pl.multiple_of(to * columns, LANES), columns)
        out[...] = functools.reduce(
            jnp.add, [part[:, at].astype(F32) for part in parts]
        ).astype(BF16)


def spread_kernel(own_ref, other_ref, order_ref, *outs):
    mine = lax.axis_index("pool")
    own, other = own_ref[...].astype(F32), other_ref[...].astype(F32)
    both = jnp.concatenate([jnp.where(mine == 0, own, other), jnp.where(mine == 0, other, own)], axis=0)
    both = both.astype(BF16)
    columns = both.shape[1] // 2
    value = dot(order_ref[0], both[:, :columns]) + dot(order_ref[1], both[:, columns:])
    count = value.shape[0] // len(outs)
    for step, out in enumerate(outs):
        out[...] = value[step * count : (step + 1) * count].astype(BF16)


def total_kernel(*refs):
    parts, out_ref = refs[:-1], refs[-1]
    total = functools.reduce(jnp.add, [part[...].astype(F32) for part in parts])
    rows, columns = total.shape[0] // 2, total.shape[1]
    out_ref[:, :columns] = total[:rows].astype(BF16)
    out_ref[:, columns:] = total[rows:].astype(BF16)


def one_hot(rows, count):
    picked = np.asarray(rows)[..., None] == np.arange(count)
    return jnp.asarray(picked.astype(np.float32), BF16)


def shape(*dims, dtype=BF16):
    return jax.ShapeDtypeStruct(dims, dtype)


def local(
    queries,
    new_entries,
    cache_pages,
    page_table,
    cached_length,
    leave_slots,
    arrive_slots,
    residual,
    norm_gain,
    output_weight,
    expert_choice,
    route_weight,
    gate_up,
    down_weight,
):
    pools, heads, planes = lax.axis_size("pool"), lax.axis_size("head"), lax.axis_size("req")
    requests = queries.shape[0]
    slots, page, entry = cache_pages.shape[1:]
    moved = leave_slots.shape[0]
    pages = page_table.shape[2]
    rows_here, width = residual.shape
    part = rows_here // pools
    columns = width // heads
    mixes = 2 * planes + -2 * planes % LANES

    own_cache = cache_pages.reshape(slots * page, entry)
    other_cache = send(own_cache, "pool", 1)
    ints = jnp.concatenate(
        [page_table[:, 0, j] for j in range(pages)]
        + [cached_length.reshape(-1), leave_slots, arrive_slots]
    )
    ints = jnp.pad(ints, (0, -ints.shape[0] % LANES)).reshape(1, -1)
    other_ints = send(ints, "pool", 1)

    gate_up, down_weight = gate_up.reshape(-1, width), down_weight.reshape(-1, width)

    rows = requests // pools
    pool_order = [
        [h * rows_here + p * part + i for p in range(pools) for h in range(heads) for i in range(part)]
    ] * pools
    head_order = [
        [(r * heads + (here ^ h)) * part + i for h in range(heads) for r in range(planes) for i in range(part)]
        for here in range(heads)
    ]
    plane_order = [
        [
            p * planes * part + r * part + i if half == at else -1
            for r in range(planes)
            for at in range(2)
            for p in range(pools)
            for i in range(part)
        ]
        for half in range(2)
    ]
    outside = (
        own_cache,
        queries,
        output_weight,
        new_entries.reshape(requests, -1, entry),
        one_hot(plane_order, pools * planes * part),
        one_hot(pool_order, requests),
        one_hot(head_order, planes * rows),
        residual,
        expert_choice.T,
        route_weight.T,
    )
    copied = [
        shape(*array.shape[i // 5 :], dtype=array.dtype) for i, array in enumerate(outside[:7])
    ]
    placed, held_cache, held_queries, held_weight, held_entries, plane_order, pool_order, head_order = kernel_call(
        functools.partial(place_kernel, (heads, pools, planes, len(outside))),
        [shape(requests, heads * (columns + mixes))] + copied,
        (),
        [pltpu.VMEM(array.shape, array.dtype) for array in outside[7:]]
        + [pltpu.SemaphoreType.DMA((len(outside),))],
        outside,
    )
    args = held(
        held_queries,
        held_entries,
        held_cache,
        other_cache,
        ints,
        other_ints,
        placed,
        pool_order,
        held_weight,
    )
    sizes = (requests, pages, moved, page, heads, pools, entry // 2)
    own, other = kernel_call(
        functools.partial(attend_kernel, sizes),
        [
            shape(requests, heads * (columns + mixes), dtype=F32),
            shape(requests, heads * (columns + mixes)),
        ],
        args,
    )
    other = give(other, 0)
    ready = lax.optimization_barrier((gate_up, down_weight, other))
    other_up, other_down = send(ready[0], "pool", 1), send(ready[1], "pool", 1)
    piece = shape(requests, columns + mixes)
    pieces = kernel_call(
        split_kernel,
        [shape(requests, columns + mixes, dtype=F32)] + [piece] * (heads - 1),
        held(own, other),
    )
    total = pieces[0]
    for step in reversed(range(2, heads)):
        total = kernel_call(
            add_kernel,
            shape(requests, columns + mixes, dtype=F32),
            held(total, send_last(pieces[step], "head", step)),
        )
    hidden = kernel_call(
        functools.partial(sum_kernel, 2),
        [piece] * planes,
        held(send_last(pieces[1], "head", 1), total),
    )

    arrived = [send_last(hidden[step], "req", step) for step in reversed(range(1, planes))] + [hidden[0]]
    marks = []
    for part_arrived in arrived[:-2]:
        marks = [kernel_call(mark_kernel, shape(16, LANES), held(part_arrived, *marks))]
    piece = shape(planes, rows, columns + mixes)
    mine, given = kernel_call(stack_kernel, [piece] * 2, held(*marks, *arrived))
    plane_blocks, sent = kernel_call(
        choose_kernel, [piece, shape(planes, rows, columns)], held(mine, give(given, 1))
    )
    weights = held(gate_up, other_up, norm_gain.reshape(1, -1))
    total = planes * rows
    sums = [shape(total, 2 * gate_up.shape[0], dtype=F32), shape(total, 1, dtype=F32)]
    *state, route, own = kernel_call(
        functools.partial(project_kernel, 0, planes),
        sums + [shape(total, 1, dtype=F32), shape(total, columns, dtype=F32)],
        held(plane_blocks, *weights, head_order, down_weight),
    )
    for step in reversed(range(1, heads)):
        state = kernel_call(
            functools.partial(project_kernel, step, planes),
            sums,
            held(send(sent, "head", step), *weights, *state),
        )
    piece = shape(planes * part, width)
    pieces = kernel_call(
        expert_kernel,
        [shape(planes * part, width, dtype=F32)] + [piece] * (heads - 1),
        held(*state, route, own, down_weight, other_down, head_order),
    )
    arrived = [send(pieces[step], "head", step) for step in reversed(range(1, heads))] + [pieces[0]]
    own, other = kernel_call(
        halve_kernel, [shape(planes * part, width // pools)] * 2, held(*arrived)
    )
    other = send(other, "pool", 1)
    piece = shape(2 * rows_here, width // pools // 2)
    pieces = kernel_call(spread_kernel, [piece] * planes, held(own, other, plane_order))
    arrived = [send(pieces[step], "req", step) for step in reversed(range(1, planes))] + [pieces[0]]
    return kernel_call(total_kernel, shape(rows_here, width // pools), held(*arrived))


def solution(mesh):
    return jax.shard_map(
        local,
        mesh=mesh,
        in_specs=(
            P(("group", "req"), "head"),
            P(("group", "req"), None, "head", None),
            P("head", ("group", "req", "pool"), None, None),
            P(("group", "req"), "pool", None),
            P(("group", "req"), "pool"),
            P(("group", "req", "pool")),
            P(("group", "req", "pool")),
            P(("group", "req", "head"), None),
            P(),
            P(("head", "pool"), None),
            P(("group", "req", "head"), None),
            P(("group", "req", "head"), None),
            P(("req", "head"), None, "pool", None),
            P(("req", "head"), "pool", None),
        ),
        out_specs=P(("group", "req", "head"), "pool"),
        check_vma=False,
    )
```

```python
import functools

import jax
import jax.numpy as jnp
import numpy as np
from jax import lax
from jax.experimental import pallas as pl
from jax.experimental.pallas import tpu as pltpu
from jax.sharding import PartitionSpec as P

F32 = jnp.float32
BF16 = jnp.bfloat16
VMEM_LIMIT = 32 * 2**20
LANES = 128


def send(value, axes, step):
    size = lax.axis_size(axes)
    return lax.ppermute(value, axes, [(i, i ^ step) for i in range(size)])


def cross(value, axis, step):
    size, pools = lax.axis_size(axis), lax.axis_size("pool")
    pairs = [
        (i * pools + p, (i ^ step) * pools + (p ^ (step & 1))) for i in range(size) for p in range(pools)
    ]
    return lax.ppermute(value, (axis, "pool"), pairs)


def part_taken():
    return lax.axis_index("pool") ^ (lax.axis_index("req") & 1)


def dot(a, b, contract=((1,), (0,))):
    return lax.dot_general(a, b, (contract, ((), ())), preferred_element_type=F32)


def kernel_call(body, out_shape, args, scratch=(), outside=()):
    return pl.pallas_call(
        body,
        out_shape=jax.tree.map(lambda out: pltpu.VMEM(out.shape, out.dtype), out_shape),
        in_specs=[pl.BlockSpec(memory_space=pltpu.HBM)] * len(outside)
        + [pl.BlockSpec(memory_space=pltpu.VMEM)] * len(args),
        out_specs=jax.tree.map(lambda _: pl.BlockSpec(memory_space=pltpu.VMEM), out_shape),
        scratch_shapes=list(scratch),
        compiler_params=pltpu.CompilerParams(vmem_limit_bytes=VMEM_LIMIT),
    )(*[pltpu.with_memory_space_constraint(arg, pltpu.HBM) for arg in outside], *args)


def held(*args):
    return [pltpu.with_memory_space_constraint(arg, pltpu.VMEM) for arg in args]


def column(row, start, count):
    lane = lax.broadcasted_iota(jnp.int32, (count, row.shape[1]), 1)
    line = lax.broadcasted_iota(jnp.int32, (count, row.shape[1]), 0)
    return jnp.sum(jnp.where(lane == line + start, row, 0.0), axis=1, keepdims=True)


def place_kernel(sizes, *refs):
    heads, pools, planes, count = sizes
    sources, placed_ref, targets = refs[:count], refs[count], refs[count + 1 : -1]
    residual_ref, choice_ref, route_ref = targets[7:]
    semaphores = refs[-1]
    head, mine = lax.axis_index("head"), part_taken()
    first = jnp.where(lax.axis_index("pool") == 0, 1.0, 0.0)
    picked = {5: mine, 6: head}
    copies = []
    for i in range(count):
        source = sources[i].at[picked[i]] if i in picked else sources[i]
        copies.append(pltpu.make_async_copy(source, targets[i], semaphores.at[i]))
    for copy in reversed(copies):
        copy.start()
    for copy in copies[7:]:
        copy.wait()
    rows_here, width = residual_ref.shape
    part = rows_here // pools
    total = heads * rows_here
    line = lax.broadcasted_iota(jnp.int32, (total, rows_here), 0)
    lane = lax.broadcasted_iota(jnp.int32, (total, rows_here), 1)
    own = None
    for p in range(pools):
        inside = line - (p * heads * part + head * part)
        one = (inside >= 0) & (inside < part) & (lane == inside + (mine ^ p) * part)
        own = one if own is None else own | one
    spread = jnp.where(own, first, 0.0)
    mixes = placed_ref.shape[1] - width
    placed = dot(spread.astype(BF16), residual_ref[...])
    target = lax.broadcasted_iota(jnp.int32, (total, mixes), 1)
    mix = jnp.zeros((total, mixes), F32)
    for k in range(choice_ref.shape[0]):
        expert = jnp.sum(spread * choice_ref[k : k + 1, :].astype(F32), axis=1, keepdims=True).astype(jnp.int32)
        weight = jnp.sum(spread * route_ref[k : k + 1, :], axis=1, keepdims=True)
        high = weight.astype(BF16).astype(F32)
        lanes = (expert % heads) * (mixes // heads) + expert // heads
        mix = mix + jnp.where(target == lanes, high, 0.0)
        mix = mix + jnp.where(target == lanes + planes, weight - high, 0.0)
    columns, share = width // heads, mixes // heads
    for h in range(heads):
        start = h * (columns + share)
        placed_ref[:, start : start + columns] = placed[:, h * columns : (h + 1) * columns].astype(BF16)
        placed_ref[:, start + columns : start + columns + share] = mix[
            :, h * share : (h + 1) * share
        ].astype(BF16)
    for copy in copies[:7]:
        copy.wait()


def attend_kernel(sizes, q_ref, new_ref, own_ref, other_ref, own_ints_ref, other_ints_ref, placed_ref, order_ref, weight_ref, own_out_ref, other_out_ref):
    requests, pages, moved, page, heads, pools, head_dim = sizes
    slots = own_ref.shape[0] // page
    here = lax.axis_index("pool")
    group = q_ref.shape[1] // head_dim // pools
    rows = requests // pools
    width = weight_ref.shape[1]
    columns = width // heads
    mixes = (placed_ref.shape[1] - width) // heads

    ints = [own_ints_ref[...].astype(F32), other_ints_ref[...].astype(F32)]
    live_from, live_count = [], []
    for q in range(2):
        row, across = ints[q], ints[1 - q]
        base = pages * requests
        length = column(row, base, requests)
        for j in range(pages):
            slot = column(row, j * requests, requests)
            source = slot + float(q * slots)
            for k in range(moved):
                leave = column(across, base + requests + k, 1)
                arrive = column(row, base + requests + moved + k, 1)
                source = jnp.where(slot == arrive, leave + float((1 - q) * slots), source)
            live_from.append((source * float(page)).astype(jnp.int32))
            live_count.append(jnp.clip(length - float(j * page), 0.0, float(page)).astype(jnp.int32))

    def cache_mask(offset, count):
        entry = lax.broadcasted_iota(jnp.int32, (requests, count), 1) + offset
        mask = None
        for start, amount in zip(live_from, live_count):
            apart = entry - start
            one = (apart >= 0) & (apart < amount)
            mask = one if mask is None else mask | one
        return mask

    count = own_ref.shape[0]
    fresh = new_ref.shape[1]
    entry = lax.broadcasted_iota(jnp.int32, (requests, requests * fresh), 1)
    first = lax.broadcasted_iota(jnp.int32, (requests, requests * fresh), 0) * fresh
    newest = new_ref[...].astype(F32).reshape(requests * fresh, new_ref.shape[2]).astype(BF16)
    masks = [cache_mask(0, count), cache_mask(count, count), (entry >= first) & (entry < first + fresh)]
    queries = jnp.concatenate(
        [
            q_ref[:, pl.ds(pl.multiple_of((here * group + g) * head_dim, LANES), head_dim)]
            for g in range(group)
        ],
        axis=0,
    )
    scale = head_dim ** (-0.5)
    scores = []
    for ref, mask in zip((own_ref, other_ref, newest), masks):
        score = dot(queries, ref[:, :head_dim], ((1,), (1,))) * scale
        bias = jnp.where(mask, 0.0, -jnp.inf)
        scores.append(score + jnp.concatenate([bias] * group, axis=0))
    largest = functools.reduce(
        jnp.maximum, [jnp.max(score, axis=1, keepdims=True) for score in scores]
    )
    total, value = 0.0, 0.0
    for ref, score in zip((own_ref, other_ref, newest), scores):
        weights = jnp.exp(score - largest)
        total = total + jnp.sum(weights, axis=1, keepdims=True)
        value = value + dot(weights.astype(BF16), ref[:, head_dim:])
    value = (value / total).astype(BF16)
    attended = jnp.concatenate(
        [value[g * requests : (g + 1) * requests] for g in range(group)], axis=1
    )
    attended = dot(order_ref[...], attended).astype(BF16)
    partial = dot(attended, weight_ref[...])
    for h in range(heads):
        start = h * (columns + mixes)
        at = slice(start, start + columns)
        part = partial[:, h * columns : (h + 1) * columns] + placed_ref[:, at].astype(F32)
        own_out_ref[:, at] = part[:rows]
        other_out_ref[:, at] = part[rows:].astype(BF16)
        at = slice(start + columns, start + columns + mixes)
        part = placed_ref[:, at].astype(F32)
        own_out_ref[:, at] = part[:rows]
        other_out_ref[:, at] = part[rows:].astype(BF16)


def split_kernel(own_ref, other_ref, *outs):
    head = lax.axis_index("head")
    columns = own_ref.shape[1] // len(outs)
    for step, out in enumerate(outs):
        at = pl.ds(pl.multiple_of((head ^ step) * columns, LANES), columns)
        out[...] = (own_ref[:, at] + other_ref[:, at].astype(F32)).astype(out.dtype)


def add_kernel(total_ref, part_ref, out_ref):
    out_ref[...] = total_ref[...] + part_ref[...].astype(F32)


def mark_kernel(part_ref, *refs):
    out_ref = refs[-1]
    out_ref[...] = part_ref[: out_ref.shape[0], : out_ref.shape[1]]


def sum_kernel(count, *refs):
    total = functools.reduce(jnp.add, [part[...].astype(F32) for part in refs[:count]])
    for out in refs[count:]:
        out[...] = total.astype(BF16)


def stack_kernel(*refs):
    parts, (all_ref, first_ref) = refs[1:-2], refs[-2:]
    for step, part in enumerate(reversed(parts)):
        all_ref[step] = part[...]
        first_ref[step] = part[:, : first_ref.shape[2]]


def projection(step, block_ref, own_up_ref, other_up_ref, gain_ref):
    head = lax.axis_index("head")
    rows = block_ref.shape[0] * block_ref.shape[1]
    columns = gain_ref.shape[1] // lax.axis_size("head")
    units = own_up_ref.shape[0] // 2
    at = pl.ds(pl.multiple_of((head ^ step) * columns, LANES), columns)
    block = block_ref[:, :, :columns].astype(F32).reshape(rows, columns)
    scaled = (block * gain_ref[:, at]).astype(BF16)
    weights = jnp.concatenate(
        [own_up_ref[:units, at], other_up_ref[:units, at], own_up_ref[units:, at], other_up_ref[units:, at]],
        axis=0,
    )
    projected = dot(scaled, weights, ((1,), (1,)))
    return block, projected, jnp.sum(block * block, axis=1, keepdims=True)


def project_kernel(step, planes, block_ref, own_up_ref, other_up_ref, gain_ref, *refs):
    block, projected, squares = projection(step, block_ref, own_up_ref, other_up_ref, gain_ref)
    plane_rows = block_ref.shape[1]
    rows, columns = block.shape
    if step:
        before_ref, before_squares_ref, projected_ref, squares_ref = refs
        projected_ref[...] = before_ref[...] + projected
        squares_ref[...] = before_squares_ref[...] + squares
        return
    order_ref, _, projected_ref, squares_ref, route_ref, own_ref = refs
    projected_ref[...] = projected
    squares_ref[...] = squares
    plane = lax.axis_index("req")
    mix = block_ref[:, :, columns:].astype(F32)
    mix = mix.reshape(rows, mix.shape[2])
    lane = lax.broadcasted_iota(jnp.int32, mix.shape, 1)
    route_ref[...] = jnp.sum(
        jnp.where((lane == plane) | (lane == plane + planes), mix, 0.0), axis=1, keepdims=True
    )
    line = lax.broadcasted_iota(jnp.int32, (rows, columns), 0)
    own_ref[...] = dot(order_ref[...], jnp.where(line < plane_rows, block, 0.0).astype(BF16))


def expert_kernel(block_ref, own_up_ref, other_up_ref, gain_ref, projected_ref, squares_ref, route_ref, own_ref, own_down_ref, other_down_ref, order_ref, *outs):
    heads = len(outs)
    _, projected, squares = projection(1, block_ref, own_up_ref, other_up_ref, gain_ref)
    projected = projected + projected_ref[...]
    squares = squares + squares_ref[...]
    head = lax.axis_index("head")
    rows, columns = own_ref.shape
    units = own_down_ref.shape[0]
    projected = projected * lax.rsqrt(squares / (heads * columns) + 1e-06)
    gate, up = projected[:, : 2 * units], projected[:, 2 * units :]
    activated = (gate / (1.0 + jnp.exp(-gate)) * up * route_ref[...]).astype(BF16)
    activated = dot(order_ref[...], activated).astype(BF16)
    down = jnp.concatenate([own_down_ref[...], other_down_ref[...]], axis=0)
    count = rows // heads
    for h in range(heads):
        at = slice(h * columns, (h + 1) * columns)
        part = dot(activated, down[:, at]) + jnp.where(head == h, own_ref[...], 0.0)
        for step, out in enumerate(outs):
            out[:, at] = part[step * count : (step + 1) * count].astype(out.dtype)


def halve_kernel(*refs):
    parts, (own_ref, other_ref) = refs[:-2], refs[-2:]
    pool = lax.axis_index("pool")
    columns = own_ref.shape[1]
    for out, to in ((own_ref, pool), (other_ref, 1 - pool)):
        at = pl.ds(pl.multiple_of(to * columns, LANES), columns)
        out[...] = functools.reduce(
            jnp.add, [part[:, at].astype(F32) for part in parts]
        ).astype(BF16)


def spread_kernel(own_ref, other_ref, order_ref, *outs):
    mine = part_taken()
    own, other = own_ref[...].astype(F32), other_ref[...].astype(F32)
    both = jnp.concatenate([jnp.where(mine == 0, own, other), jnp.where(mine == 0, other, own)], axis=0)
    both = both.astype(BF16)
    columns = both.shape[1] // 2
    value = dot(order_ref[0], both[:, :columns]) + dot(order_ref[1], both[:, columns:])
    count = value.shape[0] // len(outs)
    for step, out in enumerate(outs):
        out[...] = value[step * count : (step + 1) * count].astype(BF16)


def total_kernel(*refs):
    parts, out_ref = refs[:-1], refs[-1]
    total = functools.reduce(jnp.add, [part[...].astype(F32) for part in parts])
    rows, columns = total.shape[0] // 2, total.shape[1]
    out_ref[:, :columns] = total[:rows].astype(BF16)
    out_ref[:, columns:] = total[rows:].astype(BF16)


def one_hot(rows, count):
    picked = np.asarray(rows)[..., None] == np.arange(count)
    return jnp.asarray(picked.astype(np.float32), BF16)


def shape(*dims, dtype=BF16):
    return jax.ShapeDtypeStruct(dims, dtype)


def local(
    queries,
    new_entries,
    cache_pages,
    page_table,
    cached_length,
    leave_slots,
    arrive_slots,
    residual,
    norm_gain,
    output_weight,
    expert_choice,
    route_weight,
    gate_up,
    down_weight,
):
    pools, heads, planes = lax.axis_size("pool"), lax.axis_size("head"), lax.axis_size("req")
    requests = queries.shape[0]
    slots, page, entry = cache_pages.shape[1:]
    moved = leave_slots.shape[0]
    pages = page_table.shape[2]
    rows_here, width = residual.shape
    part = rows_here // pools
    columns = width // heads
    mixes = 2 * planes + -2 * planes % LANES

    own_cache = cache_pages.reshape(slots * page, entry)
    other_cache = send(own_cache, "pool", 1)
    ints = jnp.concatenate(
        [page_table[:, 0, j] for j in range(pages)]
        + [cached_length.reshape(-1), leave_slots, arrive_slots]
    )
    ints = jnp.pad(ints, (0, -ints.shape[0] % LANES)).reshape(1, -1)
    other_ints = send(ints, "pool", 1)

    gate_up, down_weight = gate_up.reshape(-1, width), down_weight.reshape(-1, width)

    rows = requests // pools
    pool_order = [
        [h * rows_here + (here ^ p) * part + i for p in range(pools) for h in range(heads) for i in range(part)]
        for here in range(pools)
    ]
    head_order = [
        [(r * heads + (here ^ h)) * part + i for h in range(heads) for r in range(planes) for i in range(part)]
        for here in range(heads)
    ]
    plane_order = [
        [
            p * planes * part + r * part + i if half == at else -1
            for r in range(planes)
            for at in range(2)
            for p in range(pools)
            for i in range(part)
        ]
        for half in range(2)
    ]
    outside = (
        own_cache,
        queries,
        output_weight,
        new_entries.reshape(requests, -1, entry),
        one_hot(plane_order, pools * planes * part),
        one_hot(pool_order, requests),
        one_hot(head_order, planes * rows),
        residual,
        expert_choice.T,
        route_weight.T,
    )
    copied = [
        shape(*array.shape[i // 5 :], dtype=array.dtype) for i, array in enumerate(outside[:7])
    ]
    placed, held_cache, held_queries, held_weight, held_entries, plane_order, pool_order, head_order = kernel_call(
        functools.partial(place_kernel, (heads, pools, planes, len(outside))),
        [shape(requests, heads * (columns + mixes))] + copied,
        (),
        [pltpu.VMEM(array.shape, array.dtype) for array in outside[7:]]
        + [pltpu.SemaphoreType.DMA((len(outside),))],
        outside,
    )
    args = held(
        held_queries,
        held_entries,
        held_cache,
        other_cache,
        ints,
        other_ints,
        placed,
        pool_order,
        held_weight,
    )
    sizes = (requests, pages, moved, page, heads, pools, entry // 2)
    own, other = kernel_call(
        functools.partial(attend_kernel, sizes),
        [shape(rows, heads * (columns + mixes), dtype=F32), shape(rows, heads * (columns + mixes))],
        args,
    )
    other = send(other, "pool", 1)
    ready = lax.optimization_barrier((gate_up, down_weight, other))
    other_up, other_down = send(ready[0], "pool", 1), send(ready[1], "pool", 1)
    piece = shape(rows, columns + mixes)
    pieces = kernel_call(
        split_kernel,
        [shape(rows, columns + mixes, dtype=F32)] + [piece] * (heads - 1),
        held(own, other),
    )
    total = pieces[0]
    for step in reversed(range(2, heads)):
        total = kernel_call(
            add_kernel,
            shape(rows, columns + mixes, dtype=F32),
            held(total, send(pieces[step], "head", step)),
        )
    hidden = kernel_call(
        functools.partial(sum_kernel, 2),
        [piece] * planes,
        held(send(pieces[1], "head", 1), total),
    )

    arrived = [cross(hidden[step], "req", step) for step in reversed(range(1, planes))] + [hidden[0]]
    marks = []
    for part_arrived in arrived[:-2]:
        marks = [kernel_call(mark_kernel, shape(16, LANES), held(part_arrived, *marks))]
    plane_blocks, sent = kernel_call(
        stack_kernel,
        [shape(planes, rows, columns + mixes), shape(planes, rows, columns)],
        held(*marks, *arrived),
    )
    weights = held(gate_up, other_up, norm_gain.reshape(1, -1))
    total = planes * rows
    sums = [shape(total, 2 * gate_up.shape[0], dtype=F32), shape(total, 1, dtype=F32)]
    *state, route, own = kernel_call(
        functools.partial(project_kernel, 0, planes),
        sums + [shape(total, 1, dtype=F32), shape(total, columns, dtype=F32)],
        held(plane_blocks, *weights, head_order, down_weight),
    )
    for step in reversed(range(2, heads)):
        state = kernel_call(
            functools.partial(project_kernel, step, planes),
            sums,
            held(send(sent, "head", step), *weights, *state),
        )
    piece = shape(planes * part, width)
    pieces = kernel_call(
        expert_kernel,
        [shape(planes * part, width, dtype=F32)] + [piece] * (heads - 1),
        held(send(sent, "head", 1), *weights, *state, route, own, down_weight, other_down, head_order),
    )
    arrived = [send(pieces[step], "head", step) for step in reversed(range(1, heads))] + [pieces[0]]
    own, other = kernel_call(
        halve_kernel, [shape(planes * part, width // pools)] * 2, held(*arrived)
    )
    other = send(other, "pool", 1)
    piece = shape(2 * rows_here, width // pools // 2)
    pieces = kernel_call(spread_kernel, [piece] * planes, held(own, other, plane_order))
    arrived = [send(pieces[step], "req", step) for step in reversed(range(1, planes))] + [pieces[0]]
    return pl.pallas_call(
        total_kernel,
        out_shape=shape(rows_here, width // pools),
        in_specs=[pl.BlockSpec(memory_space=pltpu.VMEM)] * planes,
        out_specs=pl.BlockSpec(memory_space=pltpu.VMEM),
    )(*held(*arrived))


def solution(mesh):
    return jax.shard_map(
        local,
        mesh=mesh,
        in_specs=(
            P(("group", "req"), "head"),
            P(("group", "req"), None, "head", None),
            P("head", ("group", "req", "pool"), None, None),
            P(("group", "req"), "pool", None),
            P(("group", "req"), "pool"),
            P(("group", "req", "pool")),
            P(("group", "req", "pool")),
            P(("group", "req", "head"), None),
            P(),
            P(("head", "pool"), None),
            P(("group", "req", "head"), None),
            P(("group", "req", "head"), None),
            P(("req", "head"), None, "pool", None),
            P(("req", "head"), "pool", None),
        ),
        out_specs=P(("group", "req", "head"), "pool"),
        check_vma=False,
    )
```

```python
import functools

import jax
import jax.numpy as jnp
import numpy as np
from jax import lax
from jax.experimental import pallas as pl
from jax.experimental.pallas import tpu as pltpu
from jax.sharding import PartitionSpec as P

F32 = jnp.float32
BF16 = jnp.bfloat16
VMEM_LIMIT = 32 * 2**20
LANES = 128


def send(value, axes, step):
    size = lax.axis_size(axes)
    return lax.ppermute(value, axes, [(i, i ^ step) for i in range(size)])


def cross(value, axis, step):
    size, pools = lax.axis_size(axis), lax.axis_size("pool")
    pairs = [
        (i * pools + p, (i ^ step) * pools + (p ^ (step & 1))) for i in range(size) for p in range(pools)
    ]
    return lax.ppermute(value, (axis, "pool"), pairs)


def turn_step(turn, pool, size):
    return size - 1 - (turn - pool) % (size - 1)


def own_step(turn, size):
    step = turn_step(turn, 0, size)
    for pool in range(1, lax.axis_size("pool")):
        step = jnp.where(lax.axis_index("pool") == pool, turn_step(turn, pool, size), step)
    return step


def send_turn(value, axis, turn):
    size, pools = lax.axis_size(axis), lax.axis_size("pool")
    pairs = [
        (i * pools + p, (i ^ turn_step(turn, p, size)) * pools + p) for i in range(size) for p in range(pools)
    ]
    return lax.ppermute(value, (axis, "pool"), pairs)


def part_taken():
    return lax.axis_index("pool") ^ (lax.axis_index("req") & 1)


def dot(a, b, contract=((1,), (0,))):
    return lax.dot_general(a, b, (contract, ((), ())), preferred_element_type=F32)


def kernel_call(body, out_shape, args, scratch=(), outside=()):
    return pl.pallas_call(
        body,
        out_shape=jax.tree.map(lambda out: pltpu.VMEM(out.shape, out.dtype), out_shape),
        in_specs=[pl.BlockSpec(memory_space=pltpu.HBM)] * len(outside)
        + [pl.BlockSpec(memory_space=pltpu.VMEM)] * len(args),
        out_specs=jax.tree.map(lambda _: pl.BlockSpec(memory_space=pltpu.VMEM), out_shape),
        scratch_shapes=list(scratch),
        compiler_params=pltpu.CompilerParams(vmem_limit_bytes=VMEM_LIMIT),
    )(*[pltpu.with_memory_space_constraint(arg, pltpu.HBM) for arg in outside], *args)


def held(*args):
    return [pltpu.with_memory_space_constraint(arg, pltpu.VMEM) for arg in args]


def column(row, start, count):
    lane = lax.broadcasted_iota(jnp.int32, (count, row.shape[1]), 1)
    line = lax.broadcasted_iota(jnp.int32, (count, row.shape[1]), 0)
    return jnp.sum(jnp.where(lane == line + start, row, 0.0), axis=1, keepdims=True)


def place_kernel(sizes, *refs):
    heads, pools, planes, count = sizes
    sources, placed_ref, targets = refs[:count], refs[count], refs[count + 1 : -1]
    residual_ref, choice_ref, route_ref = targets[7:]
    semaphores = refs[-1]
    head, mine = lax.axis_index("head"), part_taken()
    first = jnp.where(lax.axis_index("pool") == 0, 1.0, 0.0)
    picked = {5: mine, 6: head * pools + lax.axis_index("pool")}
    copies = []
    for i in range(count):
        source = sources[i].at[picked[i]] if i in picked else sources[i]
        copies.append(pltpu.make_async_copy(source, targets[i], semaphores.at[i]))
    for copy in reversed(copies):
        copy.start()
    for copy in copies[7:]:
        copy.wait()
    rows_here, width = residual_ref.shape
    part = rows_here // pools
    total = heads * rows_here
    line = lax.broadcasted_iota(jnp.int32, (total, rows_here), 0)
    lane = lax.broadcasted_iota(jnp.int32, (total, rows_here), 1)
    own = None
    for p in range(pools):
        inside = line - (p * heads * part + head * part)
        one = (inside >= 0) & (inside < part) & (lane == inside + (mine ^ p) * part)
        own = one if own is None else own | one
    spread = jnp.where(own, first, 0.0)
    mixes = placed_ref.shape[1] - width
    placed = dot(spread.astype(BF16), residual_ref[...])
    target = lax.broadcasted_iota(jnp.int32, (total, mixes), 1)
    mix = jnp.zeros((total, mixes), F32)
    for k in range(choice_ref.shape[0]):
        expert = jnp.sum(spread * choice_ref[k : k + 1, :].astype(F32), axis=1, keepdims=True).astype(jnp.int32)
        weight = jnp.sum(spread * route_ref[k : k + 1, :], axis=1, keepdims=True)
        high = weight.astype(BF16).astype(F32)
        lanes = (expert % heads) * (mixes // heads) + expert // heads
        mix = mix + jnp.where(target == lanes, high, 0.0)
        mix = mix + jnp.where(target == lanes + planes, weight - high, 0.0)
    columns, share = width // heads, mixes // heads
    for h in range(heads):
        start = h * (columns + share)
        placed_ref[:, start : start + columns] = placed[:, h * columns : (h + 1) * columns].astype(BF16)
        placed_ref[:, start + columns : start + columns + share] = mix[
            :, h * share : (h + 1) * share
        ].astype(BF16)
    for copy in copies[:7]:
        copy.wait()


def attend_kernel(sizes, q_ref, new_ref, own_ref, other_ref, own_ints_ref, other_ints_ref, placed_ref, order_ref, weight_ref, own_out_ref, other_out_ref):
    requests, pages, moved, page, heads, pools, head_dim = sizes
    slots = own_ref.shape[0] // page
    here = lax.axis_index("pool")
    group = q_ref.shape[1] // head_dim // pools
    rows = requests // pools
    width = weight_ref.shape[1]
    columns = width // heads
    mixes = (placed_ref.shape[1] - width) // heads

    ints = [own_ints_ref[...].astype(F32), other_ints_ref[...].astype(F32)]
    live_from, live_count = [], []
    for q in range(2):
        row, across = ints[q], ints[1 - q]
        base = pages * requests
        length = column(row, base, requests)
        for j in range(pages):
            slot = column(row, j * requests, requests)
            source = slot + float(q * slots)
            for k in range(moved):
                leave = column(across, base + requests + k, 1)
                arrive = column(row, base + requests + moved + k, 1)
                source = jnp.where(slot == arrive, leave + float((1 - q) * slots), source)
            live_from.append((source * float(page)).astype(jnp.int32))
            live_count.append(jnp.clip(length - float(j * page), 0.0, float(page)).astype(jnp.int32))

    def cache_mask(offset, count):
        entry = lax.broadcasted_iota(jnp.int32, (requests, count), 1) + offset
        mask = None
        for start, amount in zip(live_from, live_count):
            apart = entry - start
            one = (apart >= 0) & (apart < amount)
            mask = one if mask is None else mask | one
        return mask

    count = own_ref.shape[0]
    fresh = new_ref.shape[1]
    entry = lax.broadcasted_iota(jnp.int32, (requests, requests * fresh), 1)
    first = lax.broadcasted_iota(jnp.int32, (requests, requests * fresh), 0) * fresh
    newest = new_ref[...].astype(F32).reshape(requests * fresh, new_ref.shape[2]).astype(BF16)
    masks = [cache_mask(0, count), cache_mask(count, count), (entry >= first) & (entry < first + fresh)]
    queries = jnp.concatenate(
        [
            q_ref[:, pl.ds(pl.multiple_of((here * group + g) * head_dim, LANES), head_dim)]
            for g in range(group)
        ],
        axis=0,
    )
    scale = head_dim ** (-0.5)
    scores = []
    for ref, mask in zip((own_ref, other_ref, newest), masks):
        score = dot(queries, ref[:, :head_dim], ((1,), (1,))) * scale
        bias = jnp.where(mask, 0.0, -jnp.inf)
        scores.append(score + jnp.concatenate([bias] * group, axis=0))
    largest = functools.reduce(
        jnp.maximum, [jnp.max(score, axis=1, keepdims=True) for score in scores]
    )
    total, value = 0.0, 0.0
    for ref, score in zip((own_ref, other_ref, newest), scores):
        weights = jnp.exp(score - largest)
        total = total + jnp.sum(weights, axis=1, keepdims=True)
        value = value + dot(weights.astype(BF16), ref[:, head_dim:])
    value = (value / total).astype(BF16)
    attended = jnp.concatenate(
        [value[g * requests : (g + 1) * requests] for g in range(group)], axis=1
    )
    attended = dot(order_ref[...], attended).astype(BF16)
    partial = dot(attended, weight_ref[...])
    for h in range(heads):
        start = h * (columns + mixes)
        at = slice(start, start + columns)
        part = partial[:, h * columns : (h + 1) * columns] + placed_ref[:, at].astype(F32)
        own_out_ref[:, at] = part[:rows]
        other_out_ref[:, at] = part[rows:].astype(BF16)
        at = slice(start + columns, start + columns + mixes)
        part = placed_ref[:, at].astype(F32)
        own_out_ref[:, at] = part[:rows]
        other_out_ref[:, at] = part[rows:].astype(BF16)


def split_kernel(own_ref, other_ref, *outs):
    head = lax.axis_index("head")
    columns = own_ref.shape[1] // len(outs)
    for step, out in enumerate(outs):
        at = pl.ds(pl.multiple_of((head ^ step) * columns, LANES), columns)
        out[...] = (own_ref[:, at] + other_ref[:, at].astype(F32)).astype(out.dtype)


def add_kernel(total_ref, part_ref, out_ref):
    out_ref[...] = total_ref[...] + part_ref[...].astype(F32)


def mark_kernel(part_ref, *refs):
    out_ref = refs[-1]
    out_ref[...] = part_ref[: out_ref.shape[0], : out_ref.shape[1]]


def sum_kernel(count, *refs):
    total = functools.reduce(jnp.add, [part[...].astype(F32) for part in refs[:count]])
    for out in refs[count:]:
        out[...] = total.astype(BF16)


def stack_kernel(*refs):
    parts, (all_ref, first_ref) = refs[1:-2], refs[-2:]
    for step, part in enumerate(reversed(parts)):
        all_ref[step] = part[...]
        first_ref[step] = part[:, : first_ref.shape[2]]


def projection(step, block_ref, own_up_ref, other_up_ref, gain_ref):
    head = lax.axis_index("head")
    rows = block_ref.shape[0] * block_ref.shape[1]
    columns = gain_ref.shape[1] // lax.axis_size("head")
    units = own_up_ref.shape[0] // 2
    at = pl.ds(pl.multiple_of((head ^ step) * columns, LANES), columns)
    block = block_ref[:, :, :columns].astype(F32).reshape(rows, columns)
    scaled = (block * gain_ref[:, at]).astype(BF16)
    weights = jnp.concatenate(
        [own_up_ref[:units, at], other_up_ref[:units, at], own_up_ref[units:, at], other_up_ref[units:, at]],
        axis=0,
    )
    projected = dot(scaled, weights, ((1,), (1,)))
    return block, projected, jnp.sum(block * block, axis=1, keepdims=True)


def project_kernel(turn, planes, block_ref, own_up_ref, other_up_ref, gain_ref, *refs):
    step = 0 if turn is None else own_step(turn, lax.axis_size("head"))
    block, projected, squares = projection(step, block_ref, own_up_ref, other_up_ref, gain_ref)
    plane_rows = block_ref.shape[1]
    rows, columns = block.shape
    if turn is not None:
        before_ref, before_squares_ref, projected_ref, squares_ref = refs
        projected_ref[...] = before_ref[...] + projected
        squares_ref[...] = before_squares_ref[...] + squares
        return
    order_ref, _, projected_ref, squares_ref, route_ref, own_ref = refs
    projected_ref[...] = projected
    squares_ref[...] = squares
    plane = lax.axis_index("req")
    mix = block_ref[:, :, columns:].astype(F32)
    mix = mix.reshape(rows, mix.shape[2])
    lane = lax.broadcasted_iota(jnp.int32, mix.shape, 1)
    route_ref[...] = jnp.sum(
        jnp.where((lane == plane) | (lane == plane + planes), mix, 0.0), axis=1, keepdims=True
    )
    line = lax.broadcasted_iota(jnp.int32, (rows, columns), 0)
    own_ref[...] = dot(order_ref[...], jnp.where(line < plane_rows, block, 0.0).astype(BF16))


def expert_kernel(block_ref, own_up_ref, other_up_ref, gain_ref, projected_ref, squares_ref, route_ref, own_ref, own_down_ref, other_down_ref, order_ref, *outs):
    heads = len(outs)
    _, projected, squares = projection(own_step(heads - 2, heads), block_ref, own_up_ref, other_up_ref, gain_ref)
    projected = projected + projected_ref[...]
    squares = squares + squares_ref[...]
    head = lax.axis_index("head")
    rows, columns = own_ref.shape
    units = own_down_ref.shape[0]
    projected = projected * lax.rsqrt(squares / (heads * columns) + 1e-06)
    gate, up = projected[:, : 2 * units], projected[:, 2 * units :]
    activated = (gate / (1.0 + jnp.exp(-gate)) * up * route_ref[...]).astype(BF16)
    activated = dot(order_ref[...], activated).astype(BF16)
    down = jnp.concatenate([own_down_ref[...], other_down_ref[...]], axis=0)
    count = rows // heads
    for h in range(heads):
        at = slice(h * columns, (h + 1) * columns)
        part = dot(activated, down[:, at]) + jnp.where(head == h, own_ref[...], 0.0)
        for step, out in enumerate(outs):
            out[:, at] = part[step * count : (step + 1) * count].astype(out.dtype)


def halve_kernel(*refs):
    parts, (own_ref, other_ref) = refs[:-2], refs[-2:]
    pool = lax.axis_index("pool")
    columns = own_ref.shape[1]
    for out, to in ((own_ref, pool), (other_ref, 1 - pool)):
        at = pl.ds(pl.multiple_of(to * columns, LANES), columns)
        out[...] = functools.reduce(
            jnp.add, [part[:, at].astype(F32) for part in parts]
        ).astype(BF16)


def spread_kernel(own_ref, other_ref, order_ref, *outs):
    mine = part_taken()
    own, other = own_ref[...].astype(F32), other_ref[...].astype(F32)
    both = jnp.concatenate([jnp.where(mine == 0, own, other), jnp.where(mine == 0, other, own)], axis=0)
    both = both.astype(BF16)
    columns = both.shape[1] // 2
    value = dot(order_ref[0], both[:, :columns]) + dot(order_ref[1], both[:, columns:])
    count = value.shape[0] // len(outs)
    for step, out in enumerate(outs):
        out[...] = value[step * count : (step + 1) * count].astype(BF16)


def total_kernel(*refs):
    parts, out_ref = refs[:-1], refs[-1]
    total = functools.reduce(jnp.add, [part[...].astype(F32) for part in parts])
    rows, columns = total.shape[0] // 2, total.shape[1]
    out_ref[:, :columns] = total[:rows].astype(BF16)
    out_ref[:, columns:] = total[rows:].astype(BF16)


def one_hot(rows, count):
    picked = np.asarray(rows)[..., None] == np.arange(count)
    return jnp.asarray(picked.astype(np.float32), BF16)


def shape(*dims, dtype=BF16):
    return jax.ShapeDtypeStruct(dims, dtype)


def local(
    queries,
    new_entries,
    cache_pages,
    page_table,
    cached_length,
    leave_slots,
    arrive_slots,
    residual,
    norm_gain,
    output_weight,
    expert_choice,
    route_weight,
    gate_up,
    down_weight,
):
    pools, heads, planes = lax.axis_size("pool"), lax.axis_size("head"), lax.axis_size("req")
    requests = queries.shape[0]
    slots, page, entry = cache_pages.shape[1:]
    moved = leave_slots.shape[0]
    pages = page_table.shape[2]
    rows_here, width = residual.shape
    part = rows_here // pools
    columns = width // heads
    mixes = 2 * planes + -2 * planes % LANES

    own_cache = cache_pages.reshape(slots * page, entry)
    other_cache = send(own_cache, "pool", 1)
    ints = jnp.concatenate(
        [page_table[:, 0, j] for j in range(pages)]
        + [cached_length.reshape(-1), leave_slots, arrive_slots]
    )
    ints = jnp.pad(ints, (0, -ints.shape[0] % LANES)).reshape(1, -1)
    other_ints = send(ints, "pool", 1)

    gate_up, down_weight = gate_up.reshape(-1, width), down_weight.reshape(-1, width)

    rows = requests // pools
    pool_order = [
        [h * rows_here + (here ^ p) * part + i for p in range(pools) for h in range(heads) for i in range(part)]
        for here in range(pools)
    ]
    head_order = [
        [
            (r * heads + (here ^ h)) * part + i
            for h in [0] + [turn_step(turn, p, heads) for turn in range(heads - 1)]
            for r in range(planes)
            for i in range(part)
        ]
        for here in range(heads)
        for p in range(pools)
    ]
    plane_order = [
        [
            p * planes * part + r * part + i if half == at else -1
            for r in range(planes)
            for at in range(2)
            for p in range(pools)
            for i in range(part)
        ]
        for half in range(2)
    ]
    outside = (
        own_cache,
        queries,
        output_weight,
        new_entries.reshape(requests, -1, entry),
        one_hot(plane_order, pools * planes * part),
        one_hot(pool_order, requests),
        one_hot(head_order, planes * rows),
        residual,
        expert_choice.T,
        route_weight.T,
    )
    copied = [
        shape(*array.shape[i // 5 :], dtype=array.dtype) for i, array in enumerate(outside[:7])
    ]
    placed, held_cache, held_queries, held_weight, held_entries, plane_order, pool_order, head_order = kernel_call(
        functools.partial(place_kernel, (heads, pools, planes, len(outside))),
        [shape(requests, heads * (columns + mixes))] + copied,
        (),
        [pltpu.VMEM(array.shape, array.dtype) for array in outside[7:]]
        + [pltpu.SemaphoreType.DMA((len(outside),))],
        outside,
    )
    args = held(
        held_queries,
        held_entries,
        held_cache,
        other_cache,
        ints,
        other_ints,
        placed,
        pool_order,
        held_weight,
    )
    sizes = (requests, pages, moved, page, heads, pools, entry // 2)
    own, other = kernel_call(
        functools.partial(attend_kernel, sizes),
        [shape(rows, heads * (columns + mixes), dtype=F32), shape(rows, heads * (columns + mixes))],
        args,
    )
    other = send(other, "pool", 1)
    ready = lax.optimization_barrier((gate_up, down_weight, other))
    other_up, other_down = send(ready[0], "pool", 1), send(ready[1], "pool", 1)
    piece = shape(rows, columns + mixes)
    pieces = kernel_call(
        split_kernel,
        [shape(rows, columns + mixes, dtype=F32)] + [piece] * (heads - 1),
        held(own, other),
    )
    total = pieces[0]
    for step in reversed(range(2, heads)):
        total = kernel_call(
            add_kernel,
            shape(rows, columns + mixes, dtype=F32),
            held(total, send(pieces[step], "head", step)),
        )
    hidden = kernel_call(
        functools.partial(sum_kernel, 2),
        [piece] * planes,
        held(send(pieces[1], "head", 1), total),
    )

    arrived = [cross(hidden[step], "req", step) for step in reversed(range(1, planes))] + [hidden[0]]
    marks = []
    for part_arrived in arrived[:-2]:
        marks = [kernel_call(mark_kernel, shape(16, LANES), held(part_arrived, *marks))]
    plane_blocks, sent = kernel_call(
        stack_kernel,
        [shape(planes, rows, columns + mixes), shape(planes, rows, columns)],
        held(*marks, *arrived),
    )
    weights = held(gate_up, other_up, norm_gain.reshape(1, -1))
    total = planes * rows
    sums = [shape(total, 2 * gate_up.shape[0], dtype=F32), shape(total, 1, dtype=F32)]
    *state, route, own = kernel_call(
        functools.partial(project_kernel, None, planes),
        sums + [shape(total, 1, dtype=F32), shape(total, columns, dtype=F32)],
        held(plane_blocks, *weights, head_order, down_weight),
    )
    for turn in range(heads - 2):
        state = kernel_call(
            functools.partial(project_kernel, turn, planes),
            sums,
            held(send_turn(sent, "head", turn), *weights, *state),
        )
    piece = shape(planes * part, width)
    pieces = kernel_call(
        expert_kernel,
        [shape(planes * part, width, dtype=F32)] + [piece] * (heads - 1),
        held(send_turn(sent, "head", heads - 2), *weights, *state, route, own, down_weight, other_down, head_order),
    )
    arrived = [send_turn(pieces[turn + 1], "head", turn) for turn in range(heads - 1)] + [pieces[0]]
    own, other = kernel_call(
        halve_kernel, [shape(planes * part, width // pools)] * 2, held(*arrived)
    )
    other = send(other, "pool", 1)
    piece = shape(2 * rows_here, width // pools // 2)
    pieces = kernel_call(spread_kernel, [piece] * planes, held(own, other, plane_order))
    arrived = [send(pieces[step], "req", step) for step in reversed(range(1, planes))] + [pieces[0]]
    return pl.pallas_call(
        total_kernel,
        out_shape=shape(rows_here, width // pools),
        in_specs=[pl.BlockSpec(memory_space=pltpu.VMEM)] * planes,
        out_specs=pl.BlockSpec(memory_space=pltpu.VMEM),
    )(*held(*arrived))


def solution(mesh):
    return jax.shard_map(
        local,
        mesh=mesh,
        in_specs=(
            P(("group", "req"), "head"),
            P(("group", "req"), None, "head", None),
            P("head", ("group", "req", "pool"), None, None),
            P(("group", "req"), "pool", None),
            P(("group", "req"), "pool"),
            P(("group", "req", "pool")),
            P(("group", "req", "pool")),
            P(("group", "req", "head"), None),
            P(),
            P(("head", "pool"), None),
            P(("group", "req", "head"), None),
            P(("group", "req", "head"), None),
            P(("req", "head"), None, "pool", None),
            P(("req", "head"), "pool", None),
        ),
        out_specs=P(("group", "req", "head"), "pool"),
        check_vma=False,
    )
```

```python
import functools

import jax
import jax.numpy as jnp
import numpy as np
from jax import lax
from jax.experimental import pallas as pl
from jax.experimental.pallas import tpu as pltpu
from jax.sharding import PartitionSpec as P

F32 = jnp.float32
BF16 = jnp.bfloat16
VMEM_LIMIT = 32 * 2**20
LANES = 128


def send(value, axes, step):
    size = lax.axis_size(axes)
    return lax.ppermute(value, axes, [(i, i ^ step) for i in range(size)])


def part_taken():
    return lax.axis_index("pool")


def dot(a, b, contract=((1,), (0,))):
    return lax.dot_general(a, b, (contract, ((), ())), preferred_element_type=F32)


def kernel_call(body, out_shape, args, scratch=(), outside=()):
    return pl.pallas_call(
        body,
        out_shape=jax.tree.map(lambda out: pltpu.VMEM(out.shape, out.dtype), out_shape),
        in_specs=[pl.BlockSpec(memory_space=pltpu.HBM)] * len(outside)
        + [pl.BlockSpec(memory_space=pltpu.VMEM)] * len(args),
        out_specs=jax.tree.map(lambda _: pl.BlockSpec(memory_space=pltpu.VMEM), out_shape),
        scratch_shapes=list(scratch),
        compiler_params=pltpu.CompilerParams(vmem_limit_bytes=VMEM_LIMIT),
    )(*[pltpu.with_memory_space_constraint(arg, pltpu.HBM) for arg in outside], *args)


def held(*args):
    return [pltpu.with_memory_space_constraint(arg, pltpu.VMEM) for arg in args]


def column(row, start, count):
    lane = lax.broadcasted_iota(jnp.int32, (count, row.shape[1]), 1)
    line = lax.broadcasted_iota(jnp.int32, (count, row.shape[1]), 0)
    return jnp.sum(jnp.where(lane == line + start, row, 0.0), axis=1, keepdims=True)


def place_kernel(sizes, *refs):
    heads, pools, planes, count = sizes
    sources, placed_ref, targets = refs[:count], refs[count], refs[count + 1 : -1]
    residual_ref, choice_ref, route_ref = targets[7:]
    semaphores = refs[-1]
    head, mine = lax.axis_index("head"), part_taken()
    first = jnp.where(lax.axis_index("pool") == 0, 1.0, 0.0)
    picked = {5: mine, 6: head}
    copies = []
    for i in range(count):
        source = sources[i].at[picked[i]] if i in picked else sources[i]
        copies.append(pltpu.make_async_copy(source, targets[i], semaphores.at[i]))
    for copy in reversed(copies):
        copy.start()
    for copy in copies[7:]:
        copy.wait()
    rows_here, width = residual_ref.shape
    part = rows_here // pools
    total = heads * rows_here
    line = lax.broadcasted_iota(jnp.int32, (total, rows_here), 0)
    lane = lax.broadcasted_iota(jnp.int32, (total, rows_here), 1)
    own = None
    for p in range(pools):
        inside = line - (p * heads * part + head * part)
        one = (inside >= 0) & (inside < part) & (lane == inside + (mine ^ p) * part)
        own = one if own is None else own | one
    spread = jnp.where(own, first, 0.0)
    mixes = placed_ref.shape[1] - width
    placed = dot(spread.astype(BF16), residual_ref[...])
    target = lax.broadcasted_iota(jnp.int32, (total, mixes), 1)
    mix = jnp.zeros((total, mixes), F32)
    for k in range(choice_ref.shape[0]):
        expert = jnp.sum(spread * choice_ref[k : k + 1, :].astype(F32), axis=1, keepdims=True).astype(jnp.int32)
        weight = jnp.sum(spread * route_ref[k : k + 1, :], axis=1, keepdims=True)
        high = weight.astype(BF16).astype(F32)
        lanes = (expert % heads) * (mixes // heads) + expert // heads
        mix = mix + jnp.where(target == lanes, high, 0.0)
        mix = mix + jnp.where(target == lanes + planes, weight - high, 0.0)
    columns, share = width // heads, mixes // heads
    for h in range(heads):
        start = h * (columns + share)
        placed_ref[:, start : start + columns] = placed[:, h * columns : (h + 1) * columns].astype(BF16)
        placed_ref[:, start + columns : start + columns + share] = mix[
            :, h * share : (h + 1) * share
        ].astype(BF16)
    for copy in copies[:7]:
        copy.wait()


def attend_kernel(sizes, q_ref, new_ref, own_ref, other_ref, own_ints_ref, other_ints_ref, placed_ref, order_ref, weight_ref, own_out_ref, other_out_ref):
    requests, pages, moved, page, heads, pools, head_dim = sizes
    slots = own_ref.shape[0] // page
    here = lax.axis_index("pool")
    group = q_ref.shape[1] // head_dim // pools
    rows = requests // pools
    width = weight_ref.shape[1]
    columns = width // heads
    mixes = (placed_ref.shape[1] - width) // heads

    ints = [own_ints_ref[...].astype(F32), other_ints_ref[...].astype(F32)]
    live_from, live_count = [], []
    for q in range(2):
        row, across = ints[q], ints[1 - q]
        base = pages * requests
        length = column(row, base, requests)
        for j in range(pages):
            slot = column(row, j * requests, requests)
            source = slot + float(q * slots)
            for k in range(moved):
                leave = column(across, base + requests + k, 1)
                arrive = column(row, base + requests + moved + k, 1)
                source = jnp.where(slot == arrive, leave + float((1 - q) * slots), source)
            live_from.append((source * float(page)).astype(jnp.int32))
            live_count.append(jnp.clip(length - float(j * page), 0.0, float(page)).astype(jnp.int32))

    def cache_mask(offset, count):
        entry = lax.broadcasted_iota(jnp.int32, (requests, count), 1) + offset
        mask = None
        for start, amount in zip(live_from, live_count):
            apart = entry - start
            one = (apart >= 0) & (apart < amount)
            mask = one if mask is None else mask | one
        return mask

    count = own_ref.shape[0]
    fresh = new_ref.shape[1]
    entry = lax.broadcasted_iota(jnp.int32, (requests, requests * fresh), 1)
    first = lax.broadcasted_iota(jnp.int32, (requests, requests * fresh), 0) * fresh
    newest = new_ref[...].astype(F32).reshape(requests * fresh, new_ref.shape[2]).astype(BF16)
    masks = [cache_mask(0, count), cache_mask(count, count), (entry >= first) & (entry < first + fresh)]
    queries = jnp.concatenate(
        [
            q_ref[:, pl.ds(pl.multiple_of((here * group + g) * head_dim, LANES), head_dim)]
            for g in range(group)
        ],
        axis=0,
    )
    scale = head_dim ** (-0.5)
    scores = []
    for ref, mask in zip((own_ref, other_ref, newest), masks):
        score = dot(queries, ref[:, :head_dim], ((1,), (1,))) * scale
        bias = jnp.where(mask, 0.0, -jnp.inf)
        scores.append(score + jnp.concatenate([bias] * group, axis=0))
    largest = functools.reduce(
        jnp.maximum, [jnp.max(score, axis=1, keepdims=True) for score in scores]
    )
    total, value = 0.0, 0.0
    for ref, score in zip((own_ref, other_ref, newest), scores):
        weights = jnp.exp(score - largest)
        total = total + jnp.sum(weights, axis=1, keepdims=True)
        value = value + dot(weights.astype(BF16), ref[:, head_dim:])
    value = (value / total).astype(BF16)
    attended = jnp.concatenate(
        [value[g * requests : (g + 1) * requests] for g in range(group)], axis=1
    )
    attended = dot(order_ref[...], attended).astype(BF16)
    partial = dot(attended, weight_ref[...])
    for h in range(heads):
        start = h * (columns + mixes)
        at = slice(start, start + columns)
        part = partial[:, h * columns : (h + 1) * columns] + placed_ref[:, at].astype(F32)
        own_out_ref[:, at] = part[:rows]
        other_out_ref[:, at] = part[rows:].astype(BF16)
        at = slice(start + columns, start + columns + mixes)
        part = placed_ref[:, at].astype(F32)
        own_out_ref[:, at] = part[:rows]
        other_out_ref[:, at] = part[rows:].astype(BF16)


def split_kernel(own_ref, other_ref, *outs):
    head = lax.axis_index("head")
    columns = own_ref.shape[1] // len(outs)
    for step, out in enumerate(outs):
        at = pl.ds(pl.multiple_of((head ^ step) * columns, LANES), columns)
        out[...] = (own_ref[:, at] + other_ref[:, at].astype(F32)).astype(out.dtype)


def add_kernel(total_ref, part_ref, out_ref):
    out_ref[...] = total_ref[...] + part_ref[...].astype(F32)


def mark_kernel(part_ref, *refs):
    out_ref = refs[-1]
    out_ref[...] = part_ref[: out_ref.shape[0], : out_ref.shape[1]]


def sum_kernel(count, *refs):
    total = functools.reduce(jnp.add, [part[...].astype(F32) for part in refs[:count]])
    for out in refs[count:]:
        out[...] = total.astype(BF16)


def stack_kernel(*refs):
    parts, (all_ref, first_ref) = refs[1:-2], refs[-2:]
    for step, part in enumerate(reversed(parts)):
        all_ref[step] = part[...]
        first_ref[step] = part[:, : first_ref.shape[2]]


def projection(step, block_ref, own_up_ref, other_up_ref, gain_ref):
    head = lax.axis_index("head")
    rows = block_ref.shape[0] * block_ref.shape[1]
    columns = gain_ref.shape[1] // lax.axis_size("head")
    units = own_up_ref.shape[0] // 2
    at = pl.ds(pl.multiple_of((head ^ step) * columns, LANES), columns)
    block = block_ref[:, :, :columns].astype(F32).reshape(rows, columns)
    scaled = (block * gain_ref[:, at]).astype(BF16)
    weights = jnp.concatenate(
        [own_up_ref[:units, at], other_up_ref[:units, at], own_up_ref[units:, at], other_up_ref[units:, at]],
        axis=0,
    )
    projected = dot(scaled, weights, ((1,), (1,)))
    return block, projected, jnp.sum(block * block, axis=1, keepdims=True)


def project_kernel(step, planes, block_ref, own_up_ref, other_up_ref, gain_ref, *refs):
    block, projected, squares = projection(step, block_ref, own_up_ref, other_up_ref, gain_ref)
    plane_rows = block_ref.shape[1]
    rows, columns = block.shape
    if step:
        before_ref, before_squares_ref, projected_ref, squares_ref = refs
        projected_ref[...] = before_ref[...] + projected
        squares_ref[...] = before_squares_ref[...] + squares
        return
    order_ref, _, projected_ref, squares_ref, route_ref, own_ref = refs
    projected_ref[...] = projected
    squares_ref[...] = squares
    plane = lax.axis_index("req")
    mix = block_ref[:, :, columns:].astype(F32)
    mix = mix.reshape(rows, mix.shape[2])
    lane = lax.broadcasted_iota(jnp.int32, mix.shape, 1)
    route_ref[...] = jnp.sum(
        jnp.where((lane == plane) | (lane == plane + planes), mix, 0.0), axis=1, keepdims=True
    )
    line = lax.broadcasted_iota(jnp.int32, (rows, columns), 0)
    own_ref[...] = dot(order_ref[...], jnp.where(line < plane_rows, block, 0.0).astype(BF16))


def expert_kernel(block_ref, own_up_ref, other_up_ref, gain_ref, projected_ref, squares_ref, route_ref, own_ref, own_down_ref, other_down_ref, order_ref, *outs):
    heads = len(outs)
    _, projected, squares = projection(1, block_ref, own_up_ref, other_up_ref, gain_ref)
    projected = projected + projected_ref[...]
    squares = squares + squares_ref[...]
    head = lax.axis_index("head")
    rows, columns = own_ref.shape
    units = own_down_ref.shape[0]
    projected = projected * lax.rsqrt(squares / (heads * columns) + 1e-06)
    gate, up = projected[:, : 2 * units], projected[:, 2 * units :]
    activated = (gate / (1.0 + jnp.exp(-gate)) * up * route_ref[...]).astype(BF16)
    activated = dot(order_ref[...], activated).astype(BF16)
    down = jnp.concatenate([own_down_ref[...], other_down_ref[...]], axis=0)
    count = rows // heads
    for h in range(heads):
        at = slice(h * columns, (h + 1) * columns)
        part = dot(activated, down[:, at]) + jnp.where(head == h, own_ref[...], 0.0)
        for step, out in enumerate(outs):
            out[:, at] = part[step * count : (step + 1) * count].astype(out.dtype)


def halve_kernel(*refs):
    parts, (own_ref, other_ref) = refs[:-2], refs[-2:]
    pool = lax.axis_index("pool")
    columns = own_ref.shape[1]
    for out, to in ((own_ref, pool), (other_ref, 1 - pool)):
        at = pl.ds(pl.multiple_of(to * columns, LANES), columns)
        out[...] = functools.reduce(
            jnp.add, [part[:, at].astype(F32) for part in parts]
        ).astype(BF16)


def spread_kernel(own_ref, other_ref, order_ref, *outs):
    mine = part_taken()
    own, other = own_ref[...].astype(F32), other_ref[...].astype(F32)
    both = jnp.concatenate([jnp.where(mine == 0, own, other), jnp.where(mine == 0, other, own)], axis=0)
    both = both.astype(BF16)
    columns = both.shape[1] // 2
    value = dot(order_ref[0], both[:, :columns]) + dot(order_ref[1], both[:, columns:])
    count = value.shape[0] // len(outs)
    for step, out in enumerate(outs):
        out[...] = value[step * count : (step + 1) * count].astype(BF16)


def total_kernel(*refs):
    parts, out_ref = refs[:-1], refs[-1]
    total = functools.reduce(jnp.add, [part[...].astype(F32) for part in parts])
    rows, columns = total.shape[0] // 2, total.shape[1]
    out_ref[:, :columns] = total[:rows].astype(BF16)
    out_ref[:, columns:] = total[rows:].astype(BF16)


def one_hot(rows, count):
    picked = np.asarray(rows)[..., None] == np.arange(count)
    return jnp.asarray(picked.astype(np.float32), BF16)


def shape(*dims, dtype=BF16):
    return jax.ShapeDtypeStruct(dims, dtype)


def local(
    queries,
    new_entries,
    cache_pages,
    page_table,
    cached_length,
    leave_slots,
    arrive_slots,
    residual,
    norm_gain,
    output_weight,
    expert_choice,
    route_weight,
    gate_up,
    down_weight,
):
    pools, heads, planes = lax.axis_size("pool"), lax.axis_size("head"), lax.axis_size("req")
    requests = queries.shape[0]
    slots, page, entry = cache_pages.shape[1:]
    moved = leave_slots.shape[0]
    pages = page_table.shape[2]
    rows_here, width = residual.shape
    part = rows_here // pools
    columns = width // heads
    mixes = 2 * planes + -2 * planes % LANES

    own_cache = cache_pages.reshape(slots * page, entry)
    other_cache = send(own_cache, "pool", 1)
    ints = jnp.concatenate(
        [page_table[:, 0, j] for j in range(pages)]
        + [cached_length.reshape(-1), leave_slots, arrive_slots]
    )
    ints = jnp.pad(ints, (0, -ints.shape[0] % LANES)).reshape(1, -1)
    other_ints = send(ints, "pool", 1)

    gate_up, down_weight = gate_up.reshape(-1, width), down_weight.reshape(-1, width)

    rows = requests // pools
    pool_order = [
        [h * rows_here + (here ^ p) * part + i for p in range(pools) for h in range(heads) for i in range(part)]
        for here in range(pools)
    ]
    head_order = [
        [(r * heads + (here ^ h)) * part + i for h in range(heads) for r in range(planes) for i in range(part)]
        for here in range(heads)
    ]
    plane_order = [
        [
            p * planes * part + r * part + i if half == at else -1
            for r in range(planes)
            for at in range(2)
            for p in range(pools)
            for i in range(part)
        ]
        for half in range(2)
    ]
    outside = (
        own_cache,
        queries,
        output_weight,
        new_entries.reshape(requests, -1, entry),
        one_hot(plane_order, pools * planes * part),
        one_hot(pool_order, requests),
        one_hot(head_order, planes * rows),
        residual,
        expert_choice.T,
        route_weight.T,
    )
    copied = [
        shape(*array.shape[i // 5 :], dtype=array.dtype) for i, array in enumerate(outside[:7])
    ]
    placed, held_cache, held_queries, held_weight, held_entries, plane_order, pool_order, head_order = kernel_call(
        functools.partial(place_kernel, (heads, pools, planes, len(outside))),
        [shape(requests, heads * (columns + mixes))] + copied,
        (),
        [pltpu.VMEM(array.shape, array.dtype) for array in outside[7:]]
        + [pltpu.SemaphoreType.DMA((len(outside),))],
        outside,
    )
    args = held(
        held_queries,
        held_entries,
        held_cache,
        other_cache,
        ints,
        other_ints,
        placed,
        pool_order,
        held_weight,
    )
    sizes = (requests, pages, moved, page, heads, pools, entry // 2)
    own, other = kernel_call(
        functools.partial(attend_kernel, sizes),
        [shape(rows, heads * (columns + mixes), dtype=F32), shape(rows, heads * (columns + mixes))],
        args,
    )
    other = send(other, "pool", 1)
    ready = lax.optimization_barrier((gate_up, down_weight, other))
    other_up, other_down = send(ready[0], "pool", 1), send(ready[1], "pool", 1)
    piece = shape(rows, columns + mixes)
    pieces = kernel_call(
        split_kernel,
        [shape(rows, columns + mixes, dtype=F32)] + [piece] * (heads - 1),
        held(own, other),
    )
    total = pieces[0]
    for step in reversed(range(2, heads)):
        total = kernel_call(
            add_kernel,
            shape(rows, columns + mixes, dtype=F32),
            held(total, send(pieces[step], "head", step)),
        )
    hidden = kernel_call(
        functools.partial(sum_kernel, 2),
        [piece] * planes,
        held(send(pieces[1], "head", 1), total),
    )

    arrived = [send(hidden[step], "req", step) for step in reversed(range(1, planes))] + [hidden[0]]
    marks = []
    for part_arrived in arrived[:-2]:
        marks = [kernel_call(mark_kernel, shape(16, LANES), held(part_arrived, *marks))]
    plane_blocks, sent = kernel_call(
        stack_kernel,
        [shape(planes, rows, columns + mixes), shape(planes, rows, columns)],
        held(*marks, *arrived),
    )
    weights = held(gate_up, other_up, norm_gain.reshape(1, -1))
    total = planes * rows
    sums = [shape(total, 2 * gate_up.shape[0], dtype=F32), shape(total, 1, dtype=F32)]
    *state, route, own = kernel_call(
        functools.partial(project_kernel, 0, planes),
        sums + [shape(total, 1, dtype=F32), shape(total, columns, dtype=F32)],
        held(plane_blocks, *weights, head_order, down_weight),
    )
    for step in reversed(range(2, heads)):
        state = kernel_call(
            functools.partial(project_kernel, step, planes),
            sums,
            held(send(sent, "head", step), *weights, *state),
        )
    piece = shape(planes * part, width)
    pieces = kernel_call(
        expert_kernel,
        [shape(planes * part, width, dtype=F32)] + [piece] * (heads - 1),
        held(send(sent, "head", 1), *weights, *state, route, own, down_weight, other_down, head_order),
    )
    arrived = [send(pieces[step], "head", step) for step in reversed(range(1, heads))] + [pieces[0]]
    own, other = kernel_call(
        halve_kernel, [shape(planes * part, width // pools)] * 2, held(*arrived)
    )
    other = send(other, "pool", 1)
    piece = shape(2 * rows_here, width // pools // 2)
    pieces = kernel_call(spread_kernel, [piece] * planes, held(own, other, plane_order))
    arrived = [send(pieces[step], "req", step) for step in reversed(range(1, planes))] + [pieces[0]]
    return pl.pallas_call(
        total_kernel,
        out_shape=shape(rows_here, width // pools),
        in_specs=[pl.BlockSpec(memory_space=pltpu.VMEM)] * planes,
        out_specs=pl.BlockSpec(memory_space=pltpu.VMEM),
    )(*held(*arrived))


def solution(mesh):
    return jax.shard_map(
        local,
        mesh=mesh,
        in_specs=(
            P(("group", "req"), "head"),
            P(("group", "req"), None, "head", None),
            P("head", ("group", "req", "pool"), None, None),
            P(("group", "req"), "pool", None),
            P(("group", "req"), "pool"),
            P(("group", "req", "pool")),
            P(("group", "req", "pool")),
            P(("group", "req", "head"), None),
            P(),
            P(("head", "pool"), None),
            P(("group", "req", "head"), None),
            P(("group", "req", "head"), None),
            P(("req", "head"), None, "pool", None),
            P(("req", "head"), "pool", None),
        ),
        out_specs=P(("group", "req", "head"), "pool"),
        check_vma=False,
    )
```

```python
import functools

import jax
import jax.numpy as jnp
import numpy as np
from jax import lax
from jax.experimental import pallas as pl
from jax.experimental.pallas import tpu as pltpu
from jax.sharding import PartitionSpec as P

F32 = jnp.float32
BF16 = jnp.bfloat16
VMEM_LIMIT = 32 * 2**20
LANES = 128


def send(value, axes, step):
    size = lax.axis_size(axes)
    return lax.ppermute(value, axes, [(i, i ^ step) for i in range(size)])


def dot(a, b, contract=((1,), (0,))):
    return lax.dot_general(a, b, (contract, ((), ())), preferred_element_type=F32)


def kernel_call(body, out_shape, args, scratch=(), outside=()):
    return pl.pallas_call(
        body,
        out_shape=jax.tree.map(lambda out: pltpu.VMEM(out.shape, out.dtype), out_shape),
        in_specs=[pl.BlockSpec(memory_space=pltpu.HBM)] * len(outside)
        + [pl.BlockSpec(memory_space=pltpu.VMEM)] * len(args),
        out_specs=jax.tree.map(lambda _: pl.BlockSpec(memory_space=pltpu.VMEM), out_shape),
        scratch_shapes=list(scratch),
        compiler_params=pltpu.CompilerParams(vmem_limit_bytes=VMEM_LIMIT),
    )(*[pltpu.with_memory_space_constraint(arg, pltpu.HBM) for arg in outside], *args)


def held(*args):
    return [pltpu.with_memory_space_constraint(arg, pltpu.VMEM) for arg in args]


def column(row, start, count):
    lane = lax.broadcasted_iota(jnp.int32, (count, row.shape[1]), 1)
    line = lax.broadcasted_iota(jnp.int32, (count, row.shape[1]), 0)
    return jnp.sum(jnp.where(lane == line + start, row, 0.0), axis=1, keepdims=True)


def place_kernel(sizes, *refs):
    heads, pools, planes, count = sizes
    sources, placed_ref, targets = refs[:count], refs[count], refs[count + 1 : -1]
    residual_ref, choice_ref, route_ref = targets[7:]
    semaphores = refs[-1]
    head, mine = lax.axis_index("head"), lax.axis_index("pool")
    first = jnp.where(mine == 0, 1.0, 0.0)
    picked = {5: mine, 6: head}
    copies = []
    for i in range(count):
        source = sources[i].at[picked[i]] if i in picked else sources[i]
        copies.append(pltpu.make_async_copy(source, targets[i], semaphores.at[i]))
    for copy in reversed(copies):
        copy.start()
    for copy in copies[7:]:
        copy.wait()
    rows_here, width = residual_ref.shape
    part = rows_here // pools
    total = heads * rows_here
    line = lax.broadcasted_iota(jnp.int32, (total, rows_here), 0)
    lane = lax.broadcasted_iota(jnp.int32, (total, rows_here), 1)
    own = None
    for p in range(pools):
        inside = line - (p * heads * part + head * part)
        one = (inside >= 0) & (inside < part) & (lane == inside + (mine ^ p) * part)
        own = one if own is None else own | one
    spread = jnp.where(own, first, 0.0)
    mixes = placed_ref.shape[1] - width
    placed = dot(spread.astype(BF16), residual_ref[...])
    target = lax.broadcasted_iota(jnp.int32, (total, mixes), 1)
    mix = jnp.zeros((total, mixes), F32)
    for k in range(choice_ref.shape[0]):
        expert = jnp.sum(spread * choice_ref[k : k + 1, :].astype(F32), axis=1, keepdims=True).astype(jnp.int32)
        weight = jnp.sum(spread * route_ref[k : k + 1, :], axis=1, keepdims=True)
        high = weight.astype(BF16).astype(F32)
        lanes = (expert % heads) * (mixes // heads) + expert // heads
        mix = mix + jnp.where(target == lanes, high, 0.0)
        mix = mix + jnp.where(target == lanes + planes, weight - high, 0.0)
    columns, share = width // heads, mixes // heads
    for h in range(heads):
        start = h * (columns + share)
        placed_ref[:, start : start + columns] = placed[:, h * columns : (h + 1) * columns].astype(BF16)
        placed_ref[:, start + columns : start + columns + share] = mix[
            :, h * share : (h + 1) * share
        ].astype(BF16)
    for copy in copies[:7]:
        copy.wait()


def attend_kernel(sizes, q_ref, new_ref, own_ref, other_ref, own_ints_ref, other_ints_ref, placed_ref, order_ref, weight_ref, own_out_ref, other_out_ref):
    requests, pages, moved, page, heads, pools, head_dim = sizes
    slots = own_ref.shape[0] // page
    here = lax.axis_index("pool")
    group = q_ref.shape[1] // head_dim // pools
    rows = requests // pools
    width = weight_ref.shape[1]
    columns = width // heads
    mixes = (placed_ref.shape[1] - width) // heads

    ints = [own_ints_ref[...].astype(F32), other_ints_ref[...].astype(F32)]
    live_from, live_count = [], []
    for q in range(2):
        row, across = ints[q], ints[1 - q]
        base = pages * requests
        length = column(row, base, requests)
        for j in range(pages):
            slot = column(row, j * requests, requests)
            source = slot + float(q * slots)
            for k in range(moved):
                leave = column(across, base + requests + k, 1)
                arrive = column(row, base + requests + moved + k, 1)
                source = jnp.where(slot == arrive, leave + float((1 - q) * slots), source)
            live_from.append((source * float(page)).astype(jnp.int32))
            live_count.append(jnp.clip(length - float(j * page), 0.0, float(page)).astype(jnp.int32))

    def cache_mask(offset, count):
        entry = lax.broadcasted_iota(jnp.int32, (requests, count), 1) + offset
        mask = None
        for start, amount in zip(live_from, live_count):
            apart = entry - start
            one = (apart >= 0) & (apart < amount)
            mask = one if mask is None else mask | one
        return mask

    count = own_ref.shape[0]
    fresh = new_ref.shape[1]
    entry = lax.broadcasted_iota(jnp.int32, (requests, requests * fresh), 1)
    first = lax.broadcasted_iota(jnp.int32, (requests, requests * fresh), 0) * fresh
    newest = new_ref[...].astype(F32).reshape(requests * fresh, new_ref.shape[2]).astype(BF16)
    masks = [cache_mask(0, count), cache_mask(count, count), (entry >= first) & (entry < first + fresh)]
    queries = jnp.concatenate(
        [
            q_ref[:, pl.ds(pl.multiple_of((here * group + g) * head_dim, LANES), head_dim)]
            for g in range(group)
        ],
        axis=0,
    )
    scale = head_dim ** (-0.5)
    scores = []
    for ref, mask in zip((own_ref, other_ref, newest), masks):
        score = dot(queries, ref[:, :head_dim], ((1,), (1,))) * scale
        bias = jnp.where(mask, 0.0, -jnp.inf)
        scores.append(score + jnp.concatenate([bias] * group, axis=0))
    largest = functools.reduce(
        jnp.maximum, [jnp.max(score, axis=1, keepdims=True) for score in scores]
    )
    total, value = 0.0, 0.0
    for ref, score in zip((own_ref, other_ref, newest), scores):
        weights = jnp.exp(score - largest)
        total = total + jnp.sum(weights, axis=1, keepdims=True)
        value = value + dot(weights.astype(BF16), ref[:, head_dim:])
    value = (value / total).astype(BF16)
    attended = jnp.concatenate(
        [value[g * requests : (g + 1) * requests] for g in range(group)], axis=1
    )
    attended = dot(order_ref[...], attended).astype(BF16)
    partial = dot(attended, weight_ref[...])
    for h in range(heads):
        start = h * (columns + mixes)
        at = slice(start, start + columns)
        part = partial[:, h * columns : (h + 1) * columns] + placed_ref[:, at].astype(F32)
        own_out_ref[:, at] = part[:rows]
        other_out_ref[:, at] = part[rows:].astype(BF16)
        at = slice(start + columns, start + columns + mixes)
        part = placed_ref[:, at].astype(F32)
        own_out_ref[:, at] = part[:rows]
        other_out_ref[:, at] = part[rows:].astype(BF16)


def split_kernel(own_ref, other_ref, *outs):
    head = lax.axis_index("head")
    columns = own_ref.shape[1] // len(outs)
    for step, out in enumerate(outs):
        at = pl.ds(pl.multiple_of((head ^ step) * columns, LANES), columns)
        out[...] = (own_ref[:, at] + other_ref[:, at].astype(F32)).astype(out.dtype)


def add_kernel(total_ref, part_ref, out_ref):
    out_ref[...] = total_ref[...] + part_ref[...].astype(F32)


def mark_kernel(part_ref, *refs):
    out_ref = refs[-1]
    out_ref[...] = part_ref[: out_ref.shape[0], : out_ref.shape[1]]


def sum_kernel(count, *refs):
    total = functools.reduce(jnp.add, [part[...].astype(F32) for part in refs[:count]])
    for out in refs[count:]:
        out[...] = total.astype(BF16)


def stack_kernel(*refs):
    parts, (all_ref, first_ref) = refs[1:-2], refs[-2:]
    for step, part in enumerate(reversed(parts)):
        all_ref[step] = part[...]
        first_ref[step] = part[:, : first_ref.shape[2]]


def project_kernel(step, planes, block_ref, own_up_ref, other_up_ref, gain_ref, *refs):
    head = lax.axis_index("head")
    plane_rows = block_ref.shape[1]
    rows = planes * plane_rows
    columns = gain_ref.shape[1] // lax.axis_size("head")
    units = own_up_ref.shape[0] // 2
    at = pl.ds(pl.multiple_of((head ^ step) * columns, LANES), columns)
    block = block_ref[:, :, :columns].astype(F32).reshape(rows, columns)
    scaled = (block * gain_ref[:, at]).astype(BF16)
    weights = jnp.concatenate(
        [own_up_ref[:units, at], other_up_ref[:units, at], own_up_ref[units:, at], other_up_ref[units:, at]],
        axis=0,
    )
    projected = dot(scaled, weights, ((1,), (1,)))
    squares = jnp.sum(block * block, axis=1, keepdims=True)
    if step:
        before_ref, before_squares_ref, projected_ref, squares_ref = refs
        projected_ref[...] = before_ref[...] + projected
        squares_ref[...] = before_squares_ref[...] + squares
        return
    order_ref, _, projected_ref, squares_ref, route_ref, own_ref = refs
    projected_ref[...] = projected
    squares_ref[...] = squares
    plane = lax.axis_index("req")
    mix = block_ref[:, :, columns:].astype(F32)
    mix = mix.reshape(rows, mix.shape[2])
    lane = lax.broadcasted_iota(jnp.int32, mix.shape, 1)
    route_ref[...] = jnp.sum(
        jnp.where((lane == plane) | (lane == plane + planes), mix, 0.0), axis=1, keepdims=True
    )
    line = lax.broadcasted_iota(jnp.int32, (rows, columns), 0)
    own_ref[...] = dot(order_ref[...], jnp.where(line < plane_rows, block, 0.0).astype(BF16))


def expert_kernel(projected_ref, squares_ref, route_ref, own_ref, own_down_ref, other_down_ref, order_ref, *outs):
    heads = len(outs)
    head = lax.axis_index("head")
    rows, columns = own_ref.shape
    units = own_down_ref.shape[0]
    projected = projected_ref[...] * lax.rsqrt(squares_ref[...] / (heads * columns) + 1e-06)
    gate, up = projected[:, : 2 * units], projected[:, 2 * units :]
    activated = (gate / (1.0 + jnp.exp(-gate)) * up * route_ref[...]).astype(BF16)
    activated = dot(order_ref[...], activated).astype(BF16)
    down = jnp.concatenate([own_down_ref[...], other_down_ref[...]], axis=0)
    count = rows // heads
    for h in range(heads):
        at = slice(h * columns, (h + 1) * columns)
        part = dot(activated, down[:, at]) + jnp.where(head == h, own_ref[...], 0.0)
        for step, out in enumerate(outs):
            out[:, at] = part[step * count : (step + 1) * count].astype(out.dtype)


def halve_kernel(*refs):
    parts, (own_ref, other_ref) = refs[:-2], refs[-2:]
    pool = lax.axis_index("pool")
    columns = own_ref.shape[1]
    for out, to in ((own_ref, pool), (other_ref, 1 - pool)):
        at = pl.ds(pl.multiple_of(to * columns, LANES), columns)
        out[...] = functools.reduce(
            jnp.add, [part[:, at].astype(F32) for part in parts]
        ).astype(BF16)


def spread_kernel(own_ref, other_ref, order_ref, *outs):
    mine = lax.axis_index("pool")
    own, other = own_ref[...].astype(F32), other_ref[...].astype(F32)
    both = jnp.concatenate([jnp.where(mine == 0, own, other), jnp.where(mine == 0, other, own)], axis=0)
    both = both.astype(BF16)
    columns = both.shape[1] // 2
    value = dot(order_ref[0], both[:, :columns]) + dot(order_ref[1], both[:, columns:])
    count = value.shape[0] // len(outs)
    for step, out in enumerate(outs):
        out[...] = value[step * count : (step + 1) * count].astype(BF16)


def total_kernel(*refs):
    parts, out_ref = refs[:-1], refs[-1]
    total = functools.reduce(jnp.add, [part[...].astype(F32) for part in parts])
    rows, columns = total.shape[0] // 2, total.shape[1]
    out_ref[:, :columns] = total[:rows].astype(BF16)
    out_ref[:, columns:] = total[rows:].astype(BF16)


def one_hot(rows, count):
    picked = np.asarray(rows)[..., None] == np.arange(count)
    return jnp.asarray(picked.astype(np.float32), BF16)


def shape(*dims, dtype=BF16):
    return jax.ShapeDtypeStruct(dims, dtype)


def local(
    queries,
    new_entries,
    cache_pages,
    page_table,
    cached_length,
    leave_slots,
    arrive_slots,
    residual,
    norm_gain,
    output_weight,
    expert_choice,
    route_weight,
    gate_up,
    down_weight,
):
    pools, heads, planes = lax.axis_size("pool"), lax.axis_size("head"), lax.axis_size("req")
    requests = queries.shape[0]
    slots, page, entry = cache_pages.shape[1:]
    moved = leave_slots.shape[0]
    pages = page_table.shape[2]
    rows_here, width = residual.shape
    part = rows_here // pools
    columns = width // heads
    mixes = 2 * planes + -2 * planes % LANES

    own_cache = cache_pages.reshape(slots * page, entry)
    other_cache = send(own_cache, "pool", 1)
    ints = jnp.concatenate(
        [page_table[:, 0, j] for j in range(pages)]
        + [cached_length.reshape(-1), leave_slots, arrive_slots]
    )
    ints = jnp.pad(ints, (0, -ints.shape[0] % LANES)).reshape(1, -1)
    other_ints = send(ints, "pool", 1)

    gate_up, down_weight = gate_up.reshape(-1, width), down_weight.reshape(-1, width)

    rows = requests // pools
    pool_order = [
        [h * rows_here + (here ^ p) * part + i for p in range(pools) for h in range(heads) for i in range(part)]
        for here in range(pools)
    ]
    head_order = [
        [(r * heads + (here ^ h)) * part + i for h in range(heads) for r in range(planes) for i in range(part)]
        for here in range(heads)
    ]
    plane_order = [
        [
            p * planes * part + r * part + i if half == at else -1
            for r in range(planes)
            for at in range(2)
            for p in range(pools)
            for i in range(part)
        ]
        for half in range(2)
    ]
    outside = (
        own_cache,
        queries,
        output_weight,
        new_entries.reshape(requests, -1, entry),
        one_hot(plane_order, pools * planes * part),
        one_hot(pool_order, requests),
        one_hot(head_order, planes * rows),
        residual,
        expert_choice.T,
        route_weight.T,
    )
    copied = [
        shape(*array.shape[i // 5 :], dtype=array.dtype) for i, array in enumerate(outside[:7])
    ]
    placed, held_cache, held_queries, held_weight, held_entries, plane_order, pool_order, head_order = kernel_call(
        functools.partial(place_kernel, (heads, pools, planes, len(outside))),
        [shape(requests, heads * (columns + mixes))] + copied,
        (),
        [pltpu.VMEM(array.shape, array.dtype) for array in outside[7:]]
        + [pltpu.SemaphoreType.DMA((len(outside),))],
        outside,
    )
    args = held(
        held_queries,
        held_entries,
        held_cache,
        other_cache,
        ints,
        other_ints,
        placed,
        pool_order,
        held_weight,
    )
    sizes = (requests, pages, moved, page, heads, pools, entry // 2)
    own, other = kernel_call(
        functools.partial(attend_kernel, sizes),
        [shape(rows, heads * (columns + mixes), dtype=F32), shape(rows, heads * (columns + mixes))],
        args,
    )
    other = send(other, "pool", 1)
    piece = shape(rows, columns + mixes)
    pieces = kernel_call(
        split_kernel,
        [shape(rows, columns + mixes, dtype=F32)] + [piece] * (heads - 1),
        held(own, other),
    )
    ready = lax.optimization_barrier((gate_up, down_weight, pieces[1]))
    other_up, other_down = send(ready[0], "pool", 1), send(ready[1], "pool", 1)
    total = pieces[0]
    for step in reversed(range(2, heads)):
        total = kernel_call(
            add_kernel,
            shape(rows, columns + mixes, dtype=F32),
            held(total, send(pieces[step], "head", step)),
        )
    hidden = kernel_call(
        functools.partial(sum_kernel, 2),
        [piece] * planes,
        held(send(pieces[1], "head", 1), total),
    )

    arrived = [send(hidden[step], "req", step) for step in reversed(range(1, planes))] + [hidden[0]]
    marks = []
    for part_arrived in arrived[:-2]:
        marks = [kernel_call(mark_kernel, shape(16, LANES), held(part_arrived, *marks))]
    plane_blocks, sent = kernel_call(
        stack_kernel,
        [shape(planes, rows, columns + mixes), shape(planes, rows, columns)],
        held(*marks, *arrived),
    )
    weights = held(gate_up, other_up, norm_gain.reshape(1, -1))
    total = planes * rows
    sums = [shape(total, 2 * gate_up.shape[0], dtype=F32), shape(total, 1, dtype=F32)]
    *state, route, own = kernel_call(
        functools.partial(project_kernel, 0, planes),
        sums + [shape(total, 1, dtype=F32), shape(total, columns, dtype=F32)],
        held(plane_blocks, *weights, head_order, down_weight),
    )
    for step in reversed(range(1, heads)):
        state = kernel_call(
            functools.partial(project_kernel, step, planes),
            sums,
            held(send(sent, "head", step), *weights, *state),
        )
    piece = shape(planes * part, width)
    pieces = kernel_call(
        expert_kernel,
        [shape(planes * part, width, dtype=F32)] + [piece] * (heads - 1),
        held(*state, route, own, down_weight, other_down, head_order),
    )
    arrived = [send(pieces[step], "head", step) for step in reversed(range(1, heads))] + [pieces[0]]
    own, other = kernel_call(
        halve_kernel, [shape(planes * part, width // pools)] * 2, held(*arrived)
    )
    other = send(other, "pool", 1)
    piece = shape(2 * rows_here, width // pools // 2)
    pieces = kernel_call(spread_kernel, [piece] * planes, held(own, other, plane_order))
    arrived = [send(pieces[step], "req", step) for step in reversed(range(1, planes))] + [pieces[0]]
    return kernel_call(total_kernel, shape(rows_here, width // pools), held(*arrived))


def solution(mesh):
    return jax.shard_map(
        local,
        mesh=mesh,
        in_specs=(
            P(("group", "req"), "head"),
            P(("group", "req"), None, "head", None),
            P("head", ("group", "req", "pool"), None, None),
            P(("group", "req"), "pool", None),
            P(("group", "req"), "pool"),
            P(("group", "req", "pool")),
            P(("group", "req", "pool")),
            P(("group", "req", "head"), None),
            P(),
            P(("head", "pool"), None),
            P(("group", "req", "head"), None),
            P(("group", "req", "head"), None),
            P(("req", "head"), None, "pool", None),
            P(("req", "head"), "pool", None),
        ),
        out_specs=P(("group", "req", "head"), "pool"),
        check_vma=False,
    )
```
